32 devices in a mesh: blk: 16 (over z, x, core), win: 2 (over y).
Axes of the slice: x: 2, y: 2, z: 4, core: 2. Of those that a mesh axis runs over, the one named last changes fastest.
Arguments:
- tokens: bfloat16 [2, 16384, 1024], P('win', 'blk'), may hold values from -6 to 6
- cotangent: bfloat16 [2, 16384, 1024], P('win', 'blk'), may hold values from -6 to 6
- carry_in: float32 [2, 32, 16, 1024], P('win', 'blk'), may hold values from -6 to 6
- block_flags: int32 [2, 32], P('win', 'blk'), may hold values from 0 to 1, as said below
- qkv_w: float32 [3, 1024, 1024], P(None, 'blk'), may hold values from -0.1875 to 0.1875
- qkv_m: float32 [3, 1024, 1024], P(None, 'blk'), may hold values from -24 to 24
- qkv_v: float32 [3, 1024, 1024], P(None, 'blk'), may hold values from 68.8128 to 275.2512
- out_w: float32 [1024, 1024], P('blk'), may hold values from -3 to 3
- out_m: float32 [1024, 1024], P('blk'), may hold values from -6 to 6
- out_v: float32 [1024, 1024], P('blk'), may hold values from 8.51968 to 32.768
- up_w: float32 [1024, 4096], P('blk'), may hold values from -0.1875 to 0.1875
- up_m: float32 [1024, 4096], P('blk'), may hold values from -32 to 32
- up_v: float32 [1024, 4096], P('blk'), may hold values from 154.0096 to 622.592
- down_w: float32 [4096, 1024], P('blk'), may hold values from -0.09375 to 0.09375
- down_m: float32 [4096, 1024], P('blk'), may hold values from -48 to 48
- down_v: float32 [4096, 1024], P('blk'), may hold values from 275.2512 to 1114.112
- gain_w: float32 [2, 1024], P(None, 'blk'), may hold values from 0.5 to 1.5
- gain_m: float32 [2, 1024], P(None, 'blk'), may hold values from -32 to 32
- gain_v: float32 [2, 1024], P(None, 'blk'), may hold values from 154.0096 to 622.592
- ssm_w: float32 [3, 16, 1024], P(None, None, 'blk'), may hold values from -30 to 4, as said below
- ssm_m: float32 [3, 16, 1024], P(None, None, 'blk'), may hold values from -6 to 6
- ssm_v: float32 [3, 16, 1024], P(None, None, 'blk'), may hold values from 1.5532032 to 6.22592
Outputs:
- layer_out: bfloat16 [2, 16384, 1024], P('win', 'blk')
- input_grad: float32 [2, 16384, 1024], P('win', 'blk')
- carry_grad: float32 [2, 32, 16, 1024], P('win', 'blk')
- qkv_first: float32 [3, 1024, 1024], P(None, 'blk')
- qkv_second: float32 [3, 1024, 1024], P(None, 'blk')
- qkv_new: float32 [3, 1024, 1024], P(None, 'blk')
- out_first: float32 [1024, 1024], P('blk')
- out_second: float32 [1024, 1024], P('blk')
- out_new: float32 [1024, 1024], P('blk')
- up_first: float32 [1024, 4096], P('blk')
- up_second: float32 [1024, 4096], P('blk')
- up_new: float32 [1024, 4096], P('blk')
- down_first: float32 [4096, 1024], P('blk')
- down_second: float32 [4096, 1024], P('blk')
- down_new: float32 [4096, 1024], P('blk')
- gain_first: float32 [2, 1024], P(None, 'blk')
- gain_second: float32 [2, 1024], P(None, 'blk')
- gain_new: float32 [2, 1024], P(None, 'blk')
- ssm_first: float32 [3, 16, 1024], P(None, None, 'blk')
- ssm_second: float32 [2, 16, 1024], P(None, None, 'blk')
- rate_second: float32 [16, 1024], P(None, 'blk')
- ssm_new: float32 [3, 16, 1024], P(None, None, 'blk')
The draws below stay inside these ranges and needn't reach their ends.
Inputs may be any that keep to these rules, and one draw needn't show every extreme that they name: block_flags of block 0 of every row is 1; a 1 marks a block that begins a window. ssm_w[0] holds logarithms of decay rates.
All inputs are finite; a program needn't handle non-finite values.
Results may differ from the reference program's by a relative error of at most 0.0128.
The reference program's roundings to bfloat16 on the way count: a program that leaves them out, or rounds other values in their place, can miss the bound.
Values may be sent and summed in bfloat16 or wider, within the bound.
No kernel may reach another device: no remote copies, remote signals or barrier semaphores. Data moves between devices by JAX's collectives and lax.ppermute only.
A program may use at most 320 MiB of HBM per device.

```python
import math
import jax
import jax.numpy as jnp
from jax import lax

D = 1024
FF = 4096
HEADS = 8
HEAD_DIM = 128
NS = 16
CTX = 128
BLOCK = 512
STEP = 10
N_BLOCKS = 32
SEQ = 16384
ROWS = 2
TOKENS = 32768


def draw_block_flags(key, part):
    key = jax.random.fold_in(key, 11)
    first_key, second_key = jax.random.split(key)
    starts = (jax.random.randint(first_key, (ROWS, N_BLOCKS), 0, 8) == 0).astype(jnp.int32)
    whole_row = jax.random.randint(second_key, (), 0, ROWS)
    row_ids = lax.broadcasted_iota(jnp.int32, (ROWS, N_BLOCKS), 0)
    col_ids = lax.broadcasted_iota(jnp.int32, (ROWS, N_BLOCKS), 1)
    starts = jnp.where(row_ids == whole_row, 0, starts)
    return jnp.where(col_ids == 0, 1, starts).astype(jnp.int32)


def draw_ssm_w(key, part):
    key = jax.random.fold_in(key, 23)
    rate_key, input_key, output_key = jax.random.split(key, 3)
    lowest = math.log(0.1) - 2.0 * math.log(SEQ)
    highest_log = -math.log(30.0)
    log_rates = jax.random.uniform(rate_key, (NS, D), jnp.float32, lowest, highest_log)
    input_gain = jax.random.truncated_normal(input_key, -4.0, 4.0, (NS, D), jnp.float32)
    output_gain = jax.random.truncated_normal(output_key, -4.0, 4.0, (NS, D), jnp.float32) * NS ** (-0.5)
    return jnp.stack([log_rates, input_gain, output_gain]).astype(jnp.float32)


def levels(stream_key, dims, cuts, smallest, top_value):
    def one(axis_at, parts):
        draws = jax.random.uniform(jax.random.fold_in(jax.random.fold_in(stream_key, 6), axis_at), (parts,), jnp.float32, smallest / len(cuts), top_value / len(cuts))
        return jnp.repeat(jnp.exp(draws), dims[axis_at] // parts).reshape((-1,) + (1,) * (len(dims) - axis_at - 1))

    level = one(*cuts[0])
    for cut in cuts[1:]:
        level = level * one(*cut)
    return level


def noise(stream_key, dims, spread, bound, shards=(), held_as=jnp.bfloat16):
    values = spread * jax.random.normal(stream_key, dims, jnp.float32)
    if shards:
        values = values * levels(stream_key, dims, shards, -0.22, 0.18)
    return jnp.clip(values, -bound, bound).astype(held_as)


def setup_inputs(seed: int = 0) -> dict:
    key_list = jax.random.split(jax.random.key(seed), 23)
    return {
        "tokens": noise(key_list[0], (ROWS, SEQ, D), 1.0, 6.0, ((0, 2), (1, 16))),
        "cotangent": noise(key_list[1], (ROWS, SEQ, D), 1.0, 6.0, ((0, 2), (1, 16))),
        "carry_in": noise(key_list[2], (ROWS, N_BLOCKS, NS, D), 1.0, 6.0, ((0, 2), (1, 16)), jnp.float32),
        "block_flags": draw_block_flags(jax.random.fold_in(key_list[22], 71), 0),
        "qkv_w": noise(key_list[4], (3, D, D), D ** -0.5, 0.1875, ((1, 16),), jnp.float32),
        "qkv_m": noise(key_list[5], (3, D, D), (0.022 * TOKENS ** 0.5), 24.0, ((1, 16),), jnp.float32),
        "qkv_v": jnp.clip(jnp.exp(math.log(275.2512) - 1.3862944 * jax.random.uniform(key_list[6], (3, D, D), jnp.float32) ** levels(key_list[6], (3, D, D), ((1, 16),), -0.2, 0.2)), 68.8128, 275.2512),
        "out_w": noise(key_list[7], (D, D), 4 ** -0.5, 3.0, ((0, 16),), jnp.float32),
        "out_m": noise(key_list[8], (D, D), (0.0078 * TOKENS ** 0.5), 6.0, ((0, 16),), jnp.float32),
        "out_v": jnp.clip(jnp.exp(math.log(32.768) - 1.3470737 * jax.random.uniform(key_list[9], (D, D), jnp.float32) ** levels(key_list[9], (D, D), ((0, 16),), -0.2, 0.2)), 8.51968, 32.768),
        "up_w": noise(key_list[10], (D, FF), D ** -0.5, 0.1875, ((0, 16),), jnp.float32),
        "up_m": noise(key_list[11], (D, FF), (0.033 * TOKENS ** 0.5), 32.0, ((0, 16),), jnp.float32),
        "up_v": jnp.clip(jnp.exp(math.log(622.592) - 1.3968765 * jax.random.uniform(key_list[12], (D, FF), jnp.float32) ** levels(key_list[12], (D, FF), ((0, 16),), -0.2, 0.2)), 154.0096, 622.592),
        "down_w": noise(key_list[13], (FF, D), FF ** -0.5, 0.09375, ((0, 16),), jnp.float32),
        "down_m": noise(key_list[14], (FF, D), (0.044 * TOKENS ** 0.5), 48.0, ((0, 16),), jnp.float32),
        "down_v": jnp.clip(jnp.exp(math.log(1114.112) - 1.3981289 * jax.random.uniform(key_list[15], (FF, D), jnp.float32) ** levels(key_list[15], (FF, D), ((0, 16),), -0.2, 0.2)), 275.2512, 1114.112),
        "gain_w": jnp.clip(1.0 + 0.1 * jax.random.normal(key_list[16], (2, D), jnp.float32), 0.5, 1.5),
        "gain_m": noise(key_list[17], (2, D), (0.033 * TOKENS ** 0.5), 32.0, ((1, 16),), jnp.float32),
        "gain_v": jnp.clip(jnp.exp(math.log(622.592) - 1.3968765 * jax.random.uniform(key_list[18], (2, D), jnp.float32) ** levels(key_list[18], (2, D), ((1, 16),), -0.2, 0.2)), 154.0096, 622.592),
        "ssm_w": draw_ssm_w(jax.random.fold_in(key_list[22], 71), 0),
        "ssm_m": noise(key_list[20], (3, NS, D), (0.0033 * TOKENS ** 0.5), 6.0, ((2, 16),), jnp.float32),
        "ssm_v": jnp.clip(jnp.exp(math.log(6.22592) - 1.3884019 * jax.random.uniform(key_list[21], (3, NS, D), jnp.float32) ** levels(key_list[21], (3, NS, D), ((2, 16),), -0.2, 0.2)), 1.5532032, 6.22592),
    }


@jax.custom_vjp
def low(v):
    return lax.optimization_barrier(v.astype(jnp.bfloat16)).astype(jnp.float32)

@jax.custom_vjp
def low_back(v):
    return v

def low_keep(v):
    return (low(v), None)

def low_pass(kept, grad):
    return (grad,)

def back_keep(v):
    return (v, None)

def back_low(kept, grad):
    return (low(grad),)
low.defvjp(low_keep, low_pass)
low_back.defvjp(back_keep, back_low)
highest = lax.Precision.HIGHEST

def layer_norm(values, gain):
    centered = values - lax.optimization_barrier(jnp.mean(values, axis=-1, keepdims=True))
    variance = lax.optimization_barrier(jnp.mean(centered * centered, axis=-1, keepdims=True))
    return centered * lax.rsqrt(variance + 1e-05) * gain

def ssm_block(ssm_params, inputs, begin_state):
    decay_rates = jnp.exp(ssm_params[0])
    drive_gain = jnp.sqrt(-jnp.expm1(-2.0 * decay_rates)) * ssm_params[1]
    before = BLOCK - CTX
    lag_steps = (before - 1 - jnp.arange(before)).astype(jnp.float32)
    weights = jnp.exp(-decay_rates[None] * lag_steps[:, None, None])
    settled = jnp.exp(-decay_rates * before) * begin_state + drive_gain * lax.optimization_barrier(jnp.sum(weights * inputs[:before, None, :], axis=0))
    offsets = jnp.arange(CTX).astype(jnp.float32)[:, None, None]
    rising = jnp.cumsum(jnp.exp(decay_rates[None] * offsets) * inputs[before:, None, :], axis=0)
    states = jnp.exp(-decay_rates[None] * (offsets + 1.0)) * settled[None] + drive_gain[None] * jnp.exp(-decay_rates[None] * offsets) * rising
    return (lax.optimization_barrier(jnp.sum(ssm_params[2][None] * states, axis=1)), states[-1])

def attend(queries, key_rows, value_rows, flag_value):
    query_heads = queries.reshape(BLOCK, HEADS, HEAD_DIM)
    key_heads = key_rows.reshape(CTX + 2 * BLOCK, HEADS, HEAD_DIM)
    value_heads = value_rows.reshape(CTX + 2 * BLOCK, HEADS, HEAD_DIM)
    scores = low_back(jnp.einsum('qhd,khd->hqk', query_heads, key_heads, precision=highest) * HEAD_DIM ** (-0.5))
    position = jnp.arange(CTX + 2 * BLOCK)[None, :] - CTX - BLOCK
    query_pos = jnp.arange(BLOCK)[:, None]
    allowed = jnp.where(position < 0, flag_value < 0.5, position <= query_pos)
    scores = jnp.where(allowed[None], scores, -1e+30)
    weights_soft = jax.nn.softmax(scores, axis=-1)
    mixed = jnp.einsum('hqk,khd->qhd', low(weights_soft), value_heads, precision=highest)
    return mixed.reshape(BLOCK, D)

def with_prev(own_rows, ctx_rows):
    prev_own = jnp.concatenate([jnp.zeros_like(own_rows[:1]), own_rows[:-1]], axis=0)
    prev_ctx = jnp.concatenate([jnp.zeros_like(ctx_rows[:1]), ctx_rows[:-1]], axis=0)
    return jnp.concatenate([prev_ctx, prev_own, own_rows], axis=1)

def row_forward(inputs, carried, flag_values, qkv_w, out_w, up_w, down_w, gain_w, ssm_w):
    normed = layer_norm(inputs, gain_w[0])
    by_block = normed.reshape(N_BLOCKS, BLOCK, D)

    def advance(running, pieces):
        block_in, given, marker = pieces
        begin_state = marker * given + (1.0 - marker) * running
        context, finish = jax.checkpoint(ssm_block)(ssm_w, block_in, begin_state)
        return (finish, context)
    _, context = lax.scan(advance, jnp.zeros((NS, D), jnp.float32), (by_block, carried, flag_values))
    context_low = low(context)
    weights_low = low(qkv_w)
    normed_low = low(normed)
    projected = low_back(low(jnp.einsum('td,kde->kte', normed_low, weights_low, precision=highest)))
    ctx_pair = low_back(low(jnp.einsum('bcd,kde->kbce', context_low, weights_low[1:], precision=highest)))
    queries = projected[0].reshape(N_BLOCKS, BLOCK, D)
    key_all = with_prev(projected[1].reshape(N_BLOCKS, BLOCK, D), ctx_pair[0])
    value_all = with_prev(projected[2].reshape(N_BLOCKS, BLOCK, D), ctx_pair[1])
    mixed = lax.map(lambda pieces: jax.checkpoint(attend)(*pieces), (queries, key_all, value_all, flag_values))
    mixed = low_back(low(mixed.reshape(SEQ, D)))
    branch = low_back(jnp.dot(mixed, low(out_w), precision=highest))
    middle = inputs + branch
    normed_two = low(layer_norm(middle, gain_w[1]))
    hidden = low_back(jnp.dot(normed_two, low(up_w), precision=highest))
    activated = low(jax.nn.gelu(hidden, approximate=True))
    return middle + jnp.dot(activated, low(down_w), precision=highest)

def adamw_step(weight, first, second, gradient, step_rate, shrink):
    new_first = 0.9 * first + 0.1 * gradient
    new_second = 0.95 * second + 0.05 * gradient * gradient
    scaled_first = new_first / (1.0 - 0.9 ** STEP)
    scaled_second = new_second / (1.0 - 0.95 ** STEP)
    update = scaled_first / (jnp.sqrt(scaled_second) + 1e-08) + shrink * weight
    return (new_first, new_second, weight - step_rate * update)

def reference(tokens, cotangent, carry_in, block_flags, qkv_w, qkv_m, qkv_v, out_w, out_m, out_v, up_w, up_m, up_v, down_w, down_m, down_v, gain_w, gain_m, gain_v, ssm_w, ssm_m, ssm_v):
    flag_values = block_flags.astype(jnp.float32)

    def forward(inputs, carried, w_qkv, w_out, w_up, w_down, w_gain, w_ssm):
        return jax.vmap(row_forward, in_axes=(0, 0, 0, None, None, None, None, None, None))(inputs, carried, flag_values, w_qkv, w_out, w_up, w_down, w_gain, w_ssm)
    result, pullback = jax.vjp(forward, tokens.astype(jnp.float32), carry_in, qkv_w, out_w, up_w, down_w, gain_w, ssm_w)
    grad_in, grad_carry, grad_qkv, grad_out, grad_up, grad_down, grad_gain, grad_ssm = pullback(cotangent.astype(jnp.float32))
    qkv_first, qkv_second, qkv_new = adamw_step(qkv_w, qkv_m, qkv_v, grad_qkv, 2.0 * D ** (-0.5), 0.1)
    out_first, out_second, out_new = adamw_step(out_w, out_m, out_v, grad_out, 1.0, 0.1)
    up_first, up_second, up_new = adamw_step(up_w, up_m, up_v, grad_up, 2.0 * D ** (-0.5), 0.1)
    down_first, down_second, down_new = adamw_step(down_w, down_m, down_v, grad_down, 2.0 * FF ** (-0.5), 0.1)
    gain_first, gain_second, gain_new = adamw_step(gain_w, gain_m, gain_v, grad_gain, 1.0, 0.0)
    ssm_first, ssm_second, ssm_new = adamw_step(ssm_w, ssm_m, ssm_v, grad_ssm, 4.0, 0.0)
    return (result.astype(jnp.bfloat16), grad_in, grad_carry, qkv_first, qkv_second, qkv_new, out_first, out_second, out_new, up_first, up_second, up_new, down_first, down_second, down_new, gain_first, gain_second, gain_new, ssm_first, ssm_second[1:], ssm_second[0], ssm_new)
```

```python
import functools

import jax
import jax.numpy as jnp
from jax import lax
from jax.experimental import pallas as pl
from jax.experimental.pallas import tpu as pltpu
from jax.sharding import PartitionSpec as P

D = 1024
FF = 4096
HEADS = 8
HEAD_DIM = 128
CTX = 128
BLOCK = 512
STEP = 10
CHUNKS = 2
TILES = 4
TILE = 256
VMEM_LIMIT = 60 * 1024 * 1024
LOG2E = 1.4426950408889634
GC = 0.79788456
GQ = 0.044715
NT = (((1,), (1,)), ((), ()))
TN = (((0,), (0,)), ((), ()))


def swap(value, axis, mask):
    count = lax.axis_size(axis)
    return lax.ppermute(value, axis, [(at, at ^ mask) for at in range(count)])


def masks_of(n):
    masks = [1 << at for at in range(n.bit_length() - 1)][::-1]
    if len(masks) >= 2:
        masks[0] |= masks[1]
    return masks


def shift_of(position, masks):
    total = 0
    for at, mask in enumerate(masks):
        if position >> at & 1:
            total ^= mask
    return total


def places(n):
    mine = lax.axis_index("blk")
    masks = masks_of(n)
    return jnp.stack([mine ^ shift_of(position, masks) for position in range(n)]).astype(jnp.int32)


def gather_pieces(piece):
    held = piece[None]
    masks = masks_of(lax.axis_size("blk"))
    for mask in masks[:-1]:
        held = jnp.concatenate([held, swap(held, "blk", mask)], axis=0)
    return held, swap(held, "blk", masks[-1])


def sum_over_win(value):
    mask = 1
    while mask < lax.axis_size("win"):
        low = value.astype(jnp.bfloat16)
        value = low.astype(jnp.float32) + swap(low, "win", mask).astype(jnp.float32)
        mask *= 2
    return value.astype(jnp.float32)


def reduce_pieces(keep, send):
    for mask in masks_of(lax.axis_size("blk"))[::-1]:
        came = swap(send, "blk", mask)
        half = keep.shape[0] // 2
        add = lambda a, b: (a.astype(jnp.float32) + b.astype(jnp.float32)).astype(jnp.bfloat16)
        if half:
            send = add(keep[half:], came[half:])
            keep = add(keep[:half], came[:half])
        else:
            keep = add(keep, came)
    return sum_over_win(keep[0])


def gather_columns(value):
    mine = lax.axis_index("blk")
    mask = 1
    while mask < lax.axis_size("blk"):
        came = swap(value, "blk", mask)
        upper = (mine & mask) != 0
        value = jnp.where(upper, jnp.concatenate([came, value], axis=-1), jnp.concatenate([value, came], axis=-1))
        mask *= 2
    return value


def reduce_columns(value):
    mine = lax.axis_index("blk")
    mask = lax.axis_size("blk") // 2
    while mask:
        half = value.shape[-1] // 2
        upper = (mine & mask) != 0
        low, high = value[:, :half], value[:, half:]
        value = jnp.where(upper, high, low) + swap(jnp.where(upper, low, high), "blk", mask)
        mask //= 2
    mask = 1
    while mask < lax.axis_size("win"):
        value = value + swap(value, "win", mask)
        mask *= 2
    return value


def carried_in(through, value, backward):
    mine = lax.axis_index("blk")

    def compose(earlier, later):
        return jnp.stack([earlier[0] * later[0], later[0] * earlier[1] + later[1]])

    total = jnp.stack([through, value])
    ahead = jnp.stack([jnp.ones_like(through), jnp.zeros_like(value)])
    mask = 1
    while mask < lax.axis_size("blk"):
        other = swap(total, "blk", mask)
        before = ((mine & mask) != 0) != backward
        ahead = jnp.where(before, compose(other, ahead), ahead)
        total = jnp.where(before, compose(other, total), compose(total, other))
        mask *= 2
    return ahead[1]


def place_kernel(n, base, parts, rows, place_ref, lower_ref, upper_ref, out_ref, sems):
    copies = []
    for position in range(n):
        src = (lower_ref if position < n // 2 else upper_ref).at[position % (n // 2)]
        first = pl.multiple_of(place_ref[position] * rows, rows)
        for part in range(parts):
            copies.append(
                pltpu.make_async_copy(
                    src.at[pl.ds(base + part * rows, rows)],
                    out_ref.at[part, pl.ds(first, rows)],
                    sems.at[len(copies)],
                )
            )
    for copy in copies:
        copy.start()
    for copy in copies:
        copy.wait()


def place_rows(place, lower, upper, base, parts, rows):
    n = 2 * lower.shape[0]
    anywhere = pl.BlockSpec(memory_space=pl.ANY)
    return pl.pallas_call(
        functools.partial(place_kernel, n, base, parts, rows),
        grid_spec=pltpu.PrefetchScalarGridSpec(
            num_scalar_prefetch=1,
            grid=(1,),
            in_specs=[anywhere] * 2,
            out_specs=anywhere,
            scratch_shapes=[pltpu.SemaphoreType.DMA((n * parts,))],
        ),
        out_shape=jax.ShapeDtypeStruct((parts, n * rows, lower.shape[-1]), lower.dtype),
        cost_estimate=pl.CostEstimate(flops=0, bytes_accessed=4 * n * parts * rows * lower.shape[-1], transcendentals=0),
        name="place_rows",
    )(place, lower, upper)


def spread_kernel(n, parts, rows, place_ref, src_ref, keep_ref, send_ref, sems):
    copies = []
    for position in range(n):
        dst = (keep_ref if position < n // 2 else send_ref).at[position % (n // 2)]
        first = pl.multiple_of(place_ref[position] * rows, rows)
        for part in range(parts):
            copies.append(
                pltpu.make_async_copy(
                    src_ref.at[part, pl.ds(first, rows)],
                    dst.at[pl.ds(part * rows, rows)],
                    sems.at[len(copies)],
                )
            )
    for copy in copies:
        copy.start()
    for copy in copies:
        copy.wait()


def spread_rows(place, value):
    n = place.shape[0]
    parts, total, columns = value.shape
    rows = total // n
    anywhere = pl.BlockSpec(memory_space=pl.ANY)
    return pl.pallas_call(
        functools.partial(spread_kernel, n, parts, rows),
        grid_spec=pltpu.PrefetchScalarGridSpec(
            num_scalar_prefetch=1,
            grid=(1,),
            in_specs=[anywhere],
            out_specs=[anywhere] * 2,
            scratch_shapes=[pltpu.SemaphoreType.DMA((n * parts,))],
        ),
        out_shape=[jax.ShapeDtypeStruct((n // 2, parts * rows, columns), value.dtype)] * 2,
        cost_estimate=pl.CostEstimate(flops=0, bytes_accessed=4 * value.size, transcendentals=0),
        name="spread_rows",
    )(place, value)


def layer_norm(values, gain):
    centered = values - jnp.mean(values, axis=-1, keepdims=True)
    variance = jnp.mean(centered * centered, axis=-1, keepdims=True)
    return centered * lax.rsqrt(variance + 1e-05) * gain


def ssm_block(ssm_params, inputs, begin_state):
    decay_rates = jnp.exp(ssm_params[0])
    drive_gain = jnp.sqrt(-jnp.expm1(-2.0 * decay_rates)) * ssm_params[1]
    before = BLOCK - CTX
    lag_steps = (before - 1 - jnp.arange(before)).astype(jnp.float32)
    weights = jnp.exp(-decay_rates[None] * lag_steps[:, None, None])
    settled = jnp.exp(-decay_rates * before) * begin_state + drive_gain * jnp.sum(
        weights * inputs[:before, None, :], axis=0
    )
    offsets = jnp.arange(CTX).astype(jnp.float32)[:, None, None]
    rising = jnp.cumsum(jnp.exp(decay_rates[None] * offsets) * inputs[before:, None, :], axis=0)
    states = (
        jnp.exp(-decay_rates[None] * (offsets + 1.0)) * settled[None]
        + drive_gain[None] * jnp.exp(-decay_rates[None] * offsets) * rising
    )
    return (jnp.sum(ssm_params[2][None] * states, axis=1), states[-1])


def local_states(ssm_params, normed, carried, markers):
    block_count = markers.shape[0]
    blocks = normed.reshape(block_count, BLOCK, normed.shape[-1])
    running = jnp.zeros(ssm_params.shape[1:], jnp.float32)
    contexts = []
    for block_at in range(block_count):
        begin_state = markers[block_at] * carried[block_at] + (1.0 - markers[block_at]) * running
        context, running = jax.checkpoint(ssm_block)(ssm_params, blocks[block_at], begin_state)
        contexts.append(context)
    return (jnp.stack(contexts), running)


def ff_kernel(n, tiles, base, place_ref, n2_ref, cot_ref, lower_ref, upper_ref, out_ref, gn2_ref, keep_ref, send_ref,
              up_v, down_v, n2t_v, pack_v, load_sem, store_sem):
    t = pl.program_id(0)
    width = n2_ref.shape[1]
    rows = width // n
    hidden = down_v.shape[0]
    share = hidden // n
    span = hidden // tiles
    halves = hidden // width
    masks = masks_of(n)

    def loads():
        copies = []
        for p in range(n):
            src = (lower_ref if p < n // 2 else upper_ref).at[p % (n // 2)]
            d = place_ref[p]
            for h in range(halves):
                copies.append(pltpu.make_async_copy(
                    src.at[pl.ds(base + h * rows, rows)],
                    up_v.at[pl.ds(pl.multiple_of(d * rows, rows), rows), pl.ds(h * width, width)], load_sem.at[len(copies)]))
            copies.append(pltpu.make_async_copy(
                src.at[pl.ds(base + halves * rows, share)],
                down_v.at[pl.ds(pl.multiple_of(d * share, share), share)], load_sem.at[len(copies)]))
        return copies

    @pl.when(t == 0)
    def _():
        copies = loads()
        for c in copies:
            c.start()
        n2t_v[...] = n2_ref[...].T
        out_ref[...] = jnp.zeros_like(out_ref)
        gn2_ref[...] = jnp.zeros_like(gn2_ref)
        for c in copies:
            c.wait()

    cols = pl.ds(pl.multiple_of(t * span, span), span)
    n2 = n2_ref[...]
    cot = cot_ref[...]
    up = up_v[:, cols]
    down = down_v[cols, :]
    f32 = jnp.float32
    hid = jnp.dot(n2, up, preferred_element_type=f32)
    gact = lax.dot_general(cot, down, (((1,), (1,)), ((), ())), preferred_element_type=f32)
    sq = hid * hid
    th = jnp.tanh(GC * hid * (1.0 + GQ * sq))
    half = 0.5 * (1.0 + th)
    act = (hid * half).astype(jnp.bfloat16)
    slope = half + (0.5 * GC) * hid * (1.0 - th * th) * (1.0 + (3.0 * GQ) * sq)
    gh = (gact * slope).astype(jnp.bfloat16)
    out_ref[...] += jnp.dot(act, down, preferred_element_type=f32)
    gn2_ref[...] += lax.dot_general(gh, up, (((1,), (1,)), ((), ())), preferred_element_type=f32)
    gdown = lax.dot_general(act, cot, (((0,), (0,)), ((), ())), preferred_element_type=f32).astype(jnp.bfloat16)
    gup = jnp.dot(n2t_v[...], gh, preferred_element_type=f32).astype(jnp.bfloat16)
    groups = span // 128
    up_rows = (hidden // 128) * rows
    for d in range(n):
        for g in range(groups):
            pack_v[d, pl.ds(pl.multiple_of((t * groups + g) * rows, rows), rows), :] = gup[d * rows:(d + 1) * rows, g * 128:(g + 1) * 128]
    owners = span // share
    for o in range(owners):
        for g in range(width // 128):
            pack_v[t * owners + o, up_rows + g * share:up_rows + (g + 1) * share, :] = gdown[o * share:(o + 1) * share, g * 128:(g + 1) * 128]

    @pl.when(t == tiles - 1)
    def _():
        copies = []
        for p in range(n):
            dst = (keep_ref if p < n // 2 else send_ref).at[p % (n // 2)]
            copies.append(pltpu.make_async_copy(pack_v.at[place_ref[p]], dst, store_sem.at[p]))
        for c in copies:
            c.start()
        for c in copies:
            c.wait()


def ff_call(n, place, n2, cot, lower, upper, base, tiles):
    tokens, width = n2.shape
    rows = width // n
    halves = 2
    hidden = halves * width
    share = hidden // n
    pack_rows = hidden // 128 * rows + width // 128 * share
    bf, f32 = jnp.bfloat16, jnp.float32
    whole = lambda: pl.BlockSpec((tokens, width), lambda t, *_: (0, 0))
    anyspec = pl.BlockSpec(memory_space=pl.ANY)
    grid_spec = pltpu.PrefetchScalarGridSpec(
        num_scalar_prefetch=1, grid=(tiles,),
        in_specs=[whole(), whole(), anyspec, anyspec],
        out_specs=[whole(), whole(), anyspec, anyspec],
        scratch_shapes=[
            pltpu.VMEM((width, hidden), bf), pltpu.VMEM((hidden, width), bf), pltpu.VMEM((width, tokens), bf),
            pltpu.VMEM((n, pack_rows, 128), bf),
            pltpu.SemaphoreType.DMA((n * (halves + 1),)), pltpu.SemaphoreType.DMA((n,))])
    return pl.pallas_call(
        functools.partial(ff_kernel, n, tiles, base),
        grid_spec=grid_spec,
        out_shape=[jax.ShapeDtypeStruct((tokens, width), f32)] * 2 + [jax.ShapeDtypeStruct((n // 2, pack_rows, 128), bf)] * 2,
        compiler_params=pltpu.CompilerParams(vmem_limit_bytes=VMEM_LIMIT),
        cost_estimate=pl.CostEstimate(flops=12 * tokens * width * hidden, bytes_accessed=30 << 20, transcendentals=tokens * hidden),
        name="feed_forward",
    )(place, n2, cot, lower, upper)


def causal(rows, cols, first):
    r = lax.broadcasted_iota(jnp.int32, (rows, cols), 0) + first
    c = lax.broadcasted_iota(jnp.int32, (rows, cols), 1)
    return c <= r

def attend_forward_kernel(flag_ref, q_ref, kc_ref, kp_ref, ko_ref, vc_ref, vp_ref, vo_ref, mixed_ref, total_ref):
    scale = HEAD_DIM ** -0.5
    f32 = jnp.float32
    def tile(at, earlier):
        rows = pl.ds(at * TILE, TILE)
        own = (at + 1) * TILE
        q = q_ref[rows, :]
        so = lax.dot_general(q, ko_ref[:own, :], NT, preferred_element_type=f32)
        so = jnp.where(causal(TILE, own, at * TILE), so, -1e30)
        parts = [so]
        values = [vo_ref[:own, :]]
        if earlier:
            parts = [lax.dot_general(q, kc_ref[...], NT, preferred_element_type=f32), lax.dot_general(q, kp_ref[...], NT, preferred_element_type=f32)] + parts
            values = [vc_ref[...], vp_ref[...]] + values
        top = functools.reduce(jnp.maximum, [jnp.max(s, axis=-1, keepdims=True) for s in parts])
        shift = top * (scale * LOG2E)
        soft = [jnp.exp2(s * (scale * LOG2E) - shift) for s in parts]
        total = sum(jnp.sum(s, axis=-1, keepdims=True) for s in soft)
        inverse = 1.0 / total
        mixed = sum(jnp.dot((s * inverse).astype(jnp.bfloat16), v, preferred_element_type=f32) for s, v in zip(soft, values))
        mixed_ref[rows, :] = mixed.astype(mixed_ref.dtype)
        total_ref[0, rows, :] = shift + jnp.log2(total)
    flagged = flag_ref[0] > 0
    for at in range(BLOCK // TILE):
        pl.when(flagged)(functools.partial(tile, at, False))
        pl.when(jnp.logical_not(flagged))(functools.partial(tile, at, True))

def head_spec(rows, row_at=0, lead=None):
    if lead is None:
        return pl.BlockSpec((rows, HEAD_DIM), lambda h, *_: (row_at, h))
    return pl.BlockSpec((None, rows, HEAD_DIM), lambda h, *_: (lead, row_at, h))

def attend_forward(flag, query, key_ctx, key_prev, key_own, value_ctx, value_prev, value_own):
    ops=[query,key_ctx,key_prev,key_own,value_ctx,value_prev,value_own]
    sizes=[BLOCK,CTX,BLOCK,BLOCK,CTX,BLOCK,BLOCK]
    return pl.pallas_call(
        attend_forward_kernel,
        grid_spec=pltpu.PrefetchScalarGridSpec(num_scalar_prefetch=1, grid=(HEADS,),
            in_specs=[head_spec(s, o[1], o[2] if len(o) > 2 else None) for o, s in zip(ops, sizes)],
            out_specs=[head_spec(BLOCK), pl.BlockSpec((1, BLOCK, 1), lambda h, *_: (h, 0, 0))]),
        out_shape=[jax.ShapeDtypeStruct((BLOCK, HEADS * HEAD_DIM), jnp.bfloat16), jax.ShapeDtypeStruct((HEADS, BLOCK, 1), jnp.float32)],
        compiler_params=pltpu.CompilerParams(vmem_limit_bytes=VMEM_LIMIT),
        cost_estimate=pl.CostEstimate(flops=4 * HEADS * BLOCK * 1152 * HEAD_DIM * 2, bytes_accessed=10 << 20, transcendentals=HEADS * BLOCK * 1152),
        name="attend_forward",
    )(flag, *[o[0] for o in ops])

def attend_backward_kernel(merge, flag_ref, q_ref, kc_ref, kp_ref, ko_ref, vc_ref, vp_ref, vo_ref, total_ref, g_ref, *rest):
    scale = HEAD_DIM ** -0.5
    f32, bf = jnp.float32, jnp.bfloat16
    if merge:
        kadd_ref, vadd_ref, dq_ref, dkc_ref, dkp_ref, dko_ref, dvc_ref, dvp_ref, dvo_ref, acc_k, acc_v = rest
    else:
        dq_ref, dkc_ref, dkp_ref, dko_ref, dvc_ref, dvp_ref, dvo_ref, acc_k, acc_v = rest
    lead = CTX + BLOCK
    acc_k[...] = jnp.zeros_like(acc_k)
    acc_v[...] = jnp.zeros_like(acc_v)
    def tile(at, earlier):
        rows = pl.ds(at * TILE, TILE)
        own = (at + 1) * TILE
        q = q_ref[rows, :]
        g = g_ref[rows, :]
        total = total_ref[0, rows, :]
        keys = [(ko_ref[:own, :], vo_ref[:own, :], lead, own)]
        if earlier:
            keys = [(kc_ref[...], vc_ref[...], 0, CTX), (kp_ref[...], vp_ref[...], CTX, BLOCK)] + keys
        softs, grads = [], []
        for k, v, first, size in keys:
            s = lax.dot_general(q, k, NT, preferred_element_type=f32)
            s = s * (scale * LOG2E) - total
            if first == lead:
                s = jnp.where(causal(TILE, own, at * TILE), s, -1e30)
            softs.append(jnp.exp2(s))
            grads.append(lax.dot_general(g, v, NT, preferred_element_type=f32))
        products = [p * d for p, d in zip(softs, grads)]
        rowsum = sum(jnp.sum(x, axis=-1, keepdims=True) for x in products)
        dq = 0.0
        for (k, v, first, size), p, x in zip(keys, softs, products):
            ds = (x - p * rowsum).astype(bf)
            dq += jnp.dot(ds, k, preferred_element_type=f32)
            at_rows = pl.ds(first, size)
            acc_k[at_rows, :] += lax.dot_general(ds, q, TN, preferred_element_type=f32)
            acc_v[at_rows, :] += lax.dot_general(p.astype(bf), g, TN, preferred_element_type=f32)
        dq_ref[rows, :] = (dq * scale).astype(dq_ref.dtype)
    flagged = flag_ref[0] > 0
    for at in range(BLOCK // TILE):
        pl.when(flagged)(functools.partial(tile, at, False))
        pl.when(jnp.logical_not(flagged))(functools.partial(tile, at, True))
    more_k = kadd_ref[...] if merge else 0.0
    more_v = vadd_ref[...] if merge else 0.0
    dkc_ref[...] = (acc_k[:CTX, :] * scale).astype(dkc_ref.dtype)
    dvc_ref[...] = acc_v[:CTX, :].astype(dvc_ref.dtype)
    dkp_ref[...] = (acc_k[CTX:lead, :] * scale + more_k).astype(dkp_ref.dtype)
    dvp_ref[...] = (acc_v[CTX:lead, :] + more_v).astype(dvp_ref.dtype)
    dko_ref[...] = (acc_k[lead:, :] * scale).astype(dko_ref.dtype)
    dvo_ref[...] = acc_v[lead:, :].astype(dvo_ref.dtype)

def attend_backward(flag, query, key_ctx, key_prev, key_own, value_ctx, value_prev, value_own, total, grad, add=None):
    ops=[query,key_ctx,key_prev,key_own,value_ctx,value_prev,value_own]
    sizes=[BLOCK,CTX,BLOCK,BLOCK,CTX,BLOCK,BLOCK]
    specs=[head_spec(s, o[1], o[2] if len(o) > 2 else None) for o, s in zip(ops, sizes)]
    specs+=[pl.BlockSpec((1, BLOCK, 1), lambda h, *_: (h, 0, 0)), head_spec(BLOCK, grad[1])]
    args=[o[0] for o in ops]+[total, grad[0]]
    if add is not None:
        specs+=[head_spec(BLOCK)]*2
        args+=list(add)
    width=HEADS*HEAD_DIM
    bf,f32=jnp.bfloat16,jnp.float32
    out=lambda r,t: jax.ShapeDtypeStruct((r,width),t)
    return pl.pallas_call(
        functools.partial(attend_backward_kernel, add is not None),
        grid_spec=pltpu.PrefetchScalarGridSpec(num_scalar_prefetch=1, grid=(HEADS,),
            in_specs=specs,
            out_specs=[head_spec(BLOCK), head_spec(CTX), head_spec(BLOCK), head_spec(BLOCK), head_spec(CTX), head_spec(BLOCK), head_spec(BLOCK)],
            scratch_shapes=[pltpu.VMEM((CTX+2*BLOCK,HEAD_DIM),f32)]*2),
        out_shape=[out(BLOCK,bf), out(CTX,bf), out(BLOCK,bf), out(BLOCK,f32), out(CTX,bf), out(BLOCK,bf), out(BLOCK,f32)],
        compiler_params=pltpu.CompilerParams(vmem_limit_bytes=VMEM_LIMIT),
        cost_estimate=pl.CostEstimate(flops=10 * HEADS * BLOCK * 1152 * HEAD_DIM * 2, bytes_accessed=20 << 20, transcendentals=HEADS * BLOCK * 1152),
        name="attend_backward",
    )(flag, *args)


def adamw_step(weight, first, second, gradient, step_rate, shrink):
    new_first = 0.9 * first + 0.1 * gradient
    new_second = 0.95 * second + 0.05 * gradient * gradient
    scaled_first = new_first / (1.0 - 0.9**STEP)
    scaled_second = new_second / (1.0 - 0.95**STEP)
    update = scaled_first / (jnp.sqrt(scaled_second) + 1e-08) + shrink * weight
    return (new_first, new_second, weight - step_rate * update)


def body(
    tokens,
    cotangent,
    carry_in,
    block_flags,
    qkv_w,
    qkv_m,
    qkv_v,
    out_w,
    out_m,
    out_v,
    up_w,
    up_m,
    up_v,
    down_w,
    down_m,
    down_v,
    gain_w,
    gain_m,
    gain_v,
    ssm_w,
    ssm_m,
    ssm_v,
):
    low_type = jnp.bfloat16
    n = lax.axis_size("blk")
    width = tokens.shape[-1]
    rows = width // n
    share = FF // n // CHUNKS
    place = places(n)
    small = gather_columns(jnp.concatenate([gain_w, ssm_w.reshape(-1, ssm_w.shape[-1])], axis=0))
    gain_all, ssm_all = small[:2], small[2:].reshape(ssm_w.shape[:2] + (width,))
    qkv_piece = qkv_w.astype(low_type).reshape(3 * rows, width)
    up_parts = up_w.astype(low_type).reshape(rows, n, CHUNKS, share).transpose(2, 0, 1, 3).reshape(CHUNKS, rows, -1, width)
    up_parts = up_parts.transpose(0, 2, 1, 3).reshape(CHUNKS, -1, width)
    down_parts = down_w.astype(low_type).reshape(CHUNKS, share, width)
    ff_pieces = [jnp.concatenate([up_parts[c], down_parts[c]], axis=0) for c in range(CHUNKS)]
    ff_pieces[0] = jnp.concatenate([out_w.astype(low_type), ff_pieces[0]], axis=0)
    qkv_lower, qkv_upper = gather_pieces(qkv_piece)
    ff_gathered = [gather_pieces(piece) for piece in ff_pieces]
    qkv_all = place_rows(place, qkv_lower, qkv_upper, 0, 3, rows)

    inputs = tokens[0].astype(jnp.float32)
    markers = block_flags[0].astype(jnp.float32)
    flags = block_flags[0]
    carried = carry_in[0]
    block_count = markers.shape[0]
    normed, norm_back = jax.vjp(layer_norm, inputs, gain_all[0])

    def zero_start(params, values, given):
        return local_states(params, values, given, markers)

    (local_ctx, local_end), ssm_back = jax.vjp(zero_start, ssm_all, normed, carried)
    surviving = jnp.cumprod(1.0 - markers)

    def inflow(params, entering):
        decay_rates = jnp.exp(params[0])
        lag_steps = (
            jnp.arange(block_count)[:, None] * BLOCK + (BLOCK - CTX + 1) + jnp.arange(CTX)[None, :]
        ).astype(jnp.float32)
        factors = jnp.exp(-decay_rates[None, None] * lag_steps[:, :, None, None])
        return surviving[:, None, None] * jnp.sum(
            params[2][None, None] * factors * entering[None, None], axis=2
        )

    def passing(params):
        return surviving[-1] * jnp.exp(-jnp.exp(params[0]) * (block_count * BLOCK))

    through, passing_back = jax.vjp(passing, ssm_all)
    entering = carried_in(through, local_end, False)
    correction, inflow_back = jax.vjp(inflow, ssm_all, entering)
    contexts_low = (local_ctx + correction).astype(low_type)
    normed_low = normed.astype(low_type)
    projected = jnp.einsum(
        "td,kde->kte", normed_low, qkv_all, preferred_element_type=jnp.float32
    ).astype(low_type)
    ctx_pair = jnp.einsum(
        "td,kde->kte", contexts_low.reshape(-1, width), qkv_all[1:], preferred_element_type=jnp.float32
    ).astype(low_type)
    last = block_count - 1
    sent = jnp.concatenate(
        [projected[1, -BLOCK:], projected[2, -BLOCK:], ctx_pair[0, -CTX:], ctx_pair[1, -CTX:]], axis=0
    )
    came = lax.ppermute(sent, "blk", [(at, at + 1) for at in range(n - 1)])

    def lists(at):
        own = [(projected, at, 1), (projected, at, 2)]
        if at:
            earlier = [(ctx_pair, at - 1, 0), (projected, at - 1, 1), (ctx_pair, at - 1, 1), (projected, at - 1, 2)]
        else:
            earlier = [(came, 2 * BLOCK // CTX), (came, 0), (came, 2 * BLOCK // CTX + 1), (came, 1)]
        return [(projected, at, 0), earlier[0], earlier[1], own[0], earlier[2], earlier[3], own[1]]

    attended = {}
    for at in range(block_count)[::-1]:
        attended[at] = attend_forward(flags[at : at + 1], *lists(at))
    mixed_low = jnp.concatenate([attended[at][0] for at in range(block_count)], axis=0)
    totals = [attended[at][1] for at in range(block_count)]
    out_all = place_rows(place, *ff_gathered[0], 0, 1, rows)[0]
    middle = inputs + jnp.dot(mixed_low, out_all, preferred_element_type=jnp.float32)
    normed_two, norm_two_back = jax.vjp(layer_norm, middle, gain_all[1])
    normed_two_low = normed_two.astype(low_type)
    grad_result = cotangent[0]
    ff = [
        ff_call(n, place, normed_two_low, grad_result, *ff_gathered[c], rows if c == 0 else 0, TILES)
        for c in range(CHUNKS)
    ]
    result = middle + sum(part[0] for part in ff)
    grad_normed_two = sum(part[1] for part in ff)
    sum_ff = [reduce_pieces(part[2], part[3]) for part in ff]
    grad_middle, grad_gain_two = norm_two_back(grad_normed_two)
    grad_middle = grad_middle + grad_result.astype(jnp.float32)
    grad_branch = grad_middle.astype(low_type)
    grad_outw = jnp.einsum("td,te->de", mixed_low, grad_branch, preferred_element_type=jnp.float32)
    sum_out = reduce_pieces(*spread_rows(place, grad_outw.astype(low_type)[None]))
    grad_mixed = jnp.einsum(
        "te,de->td", grad_branch, out_all, preferred_element_type=jnp.float32
    ).astype(low_type)
    grads = []
    for at in range(block_count):
        add = (grads[-1][3], grads[-1][6]) if at else None
        grads.append(attend_backward(flags[at : at + 1], *lists(at), totals[at], (grad_mixed, at), add))
    sent_back = jnp.concatenate([grads[0][2], grads[0][5], grads[0][1], grads[0][4]], axis=0)
    came_back = lax.ppermute(sent_back, "blk", [(at + 1, at) for at in range(n - 1)])
    key_last = (grads[last][3] + came_back[:BLOCK].astype(jnp.float32)).astype(low_type)
    value_last = (grads[last][6] + came_back[BLOCK : 2 * BLOCK].astype(jnp.float32)).astype(low_type)
    later = range(1, block_count)
    grad_proj = jnp.stack(
        [
            jnp.concatenate([part[0] for part in grads], axis=0),
            jnp.concatenate([grads[at][2] for at in later] + [key_last], axis=0),
            jnp.concatenate([grads[at][5] for at in later] + [value_last], axis=0),
        ]
    )
    grad_ctx_pair = jnp.stack(
        [
            jnp.concatenate([grads[at][1] for at in later] + [came_back[2 * BLOCK : 2 * BLOCK + CTX]], axis=0),
            jnp.concatenate([grads[at][4] for at in later] + [came_back[2 * BLOCK + CTX :]], axis=0),
        ]
    )
    contexts_flat = contexts_low.reshape(-1, width)
    both_rows = jnp.concatenate([normed_low, contexts_flat], axis=0)
    grad_qkv = jnp.stack(
        [jnp.einsum("td,te->de", normed_low, grad_proj[0], preferred_element_type=jnp.float32).astype(low_type)]
        + [
            jnp.einsum(
                "td,te->de",
                both_rows,
                jnp.concatenate([grad_proj[1 + i], grad_ctx_pair[i]], axis=0),
                preferred_element_type=jnp.float32,
            ).astype(low_type)
            for i in range(2)
        ]
    )
    sum_qkv = reduce_pieces(*spread_rows(place, grad_qkv))
    grad_normed = jnp.einsum("kte,kde->td", grad_proj, qkv_all, preferred_element_type=jnp.float32)
    grad_contexts = jnp.einsum(
        "kte,kde->td", grad_ctx_pair, qkv_all[1:], preferred_element_type=jnp.float32
    ).reshape(block_count, CTX, width)
    grad_params_inflow, grad_entering_own = inflow_back(grad_contexts)
    leaving = carried_in(through, grad_entering_own, True)
    grad_params_pass = passing_back(leaving * entering)[0]
    grad_params_local, grad_normed_ssm, grad_carried = ssm_back((grad_contexts, leaving))
    grad_ssm = grad_params_inflow + grad_params_pass + grad_params_local
    grad_inputs, grad_gain_one = norm_back(grad_normed + grad_normed_ssm)
    grad_tokens = grad_inputs + grad_middle
    sum_small = reduce_columns(
        jnp.concatenate([grad_gain_one[None], grad_gain_two[None], grad_ssm.reshape(-1, width)], axis=0)
    )
    sum_gain, sum_ssm = sum_small[:2], sum_small[2:].reshape(ssm_w.shape)
    sum_qkv = sum_qkv.reshape(3, rows, width)
    up_rows = FF // CHUNKS // 128 * rows
    sum_up = jnp.stack(
        [part[:up_rows].reshape(-1, rows, 128).transpose(1, 0, 2).reshape(rows, n, share) for part in sum_ff], axis=2
    ).reshape(rows, FF)
    sum_down = jnp.concatenate(
        [part[up_rows:].reshape(-1, share, 128).transpose(1, 0, 2).reshape(share, width) for part in sum_ff], axis=0
    )
    qkv_first, qkv_second, qkv_new = adamw_step(
        qkv_w, qkv_m, qkv_v, sum_qkv, 2.0 * D ** (-0.5), 0.1
    )
    out_first, out_second, out_new = adamw_step(out_w, out_m, out_v, sum_out, 1.0, 0.1)
    up_first, up_second, up_new = adamw_step(up_w, up_m, up_v, sum_up, 2.0 * D ** (-0.5), 0.1)
    down_first, down_second, down_new = adamw_step(
        down_w, down_m, down_v, sum_down, 2.0 * FF ** (-0.5), 0.1
    )
    gain_first, gain_second, gain_new = adamw_step(gain_w, gain_m, gain_v, sum_gain, 1.0, 0.0)
    ssm_first, ssm_second, ssm_new = adamw_step(ssm_w, ssm_m, ssm_v, sum_ssm, 4.0, 0.0)
    return (
        result.astype(low_type)[None],
        grad_tokens[None],
        grad_carried[None],
        qkv_first,
        qkv_second,
        qkv_new,
        out_first,
        out_second,
        out_new,
        up_first,
        up_second,
        up_new,
        down_first,
        down_second,
        down_new,
        gain_first,
        gain_second,
        gain_new,
        ssm_first,
        ssm_second[1:],
        ssm_second[0],
        ssm_new,
    )


def solution(mesh):
    in_specs = (
        P("win", "blk", None),
        P("win", "blk", None),
        P("win", "blk", None, None),
        P("win", "blk"),
        P(None, "blk", None),
        P(None, "blk", None),
        P(None, "blk", None),
        P("blk", None),
        P("blk", None),
        P("blk", None),
        P("blk", None),
        P("blk", None),
        P("blk", None),
        P("blk", None),
        P("blk", None),
        P("blk", None),
        P(None, "blk"),
        P(None, "blk"),
        P(None, "blk"),
        P(None, None, "blk"),
        P(None, None, "blk"),
        P(None, None, "blk"),
    )
    out_specs = (
        P("win", "blk", None),
        P("win", "blk", None),
        P("win", "blk", None, None),
        P(None, "blk", None),
        P(None, "blk", None),
        P(None, "blk", None),
        P("blk", None),
        P("blk", None),
        P("blk", None),
        P("blk", None),
        P("blk", None),
        P("blk", None),
        P("blk", None),
        P("blk", None),
        P("blk", None),
        P(None, "blk"),
        P(None, "blk"),
        P(None, "blk"),
        P(None, None, "blk"),
        P(None, None, "blk"),
        P(None, "blk"),
        P(None, None, "blk"),
    )
    return jax.shard_map(body, mesh=mesh, in_specs=in_specs, out_specs=out_specs, check_vma=False)
```

```python
import functools

import jax
import jax.numpy as jnp
from jax import lax
from jax.experimental import pallas as pl
from jax.experimental.pallas import tpu as pltpu
from jax.sharding import PartitionSpec as P

D = 1024
FF = 4096
HEADS = 8
HEAD_DIM = 128
CTX = 128
BLOCK = 512
STEP = 10
CHUNKS = 2
TILES = 2
TILE = 256
BEFORE = BLOCK - CTX
LANES = 512
VMEM_LIMIT = 60 * 1024 * 1024
LOG2E = 1.4426950408889634
GC = 0.79788456
GQ = 0.044715
LIGHT = pl.CostEstimate(flops=1000, bytes_accessed=1000, transcendentals=0)
NT = (((1,), (1,)), ((), ()))
TN = (((0,), (0,)), ((), ()))

def swap(value, axis, mask):
    count = lax.axis_size(axis)
    return lax.ppermute(value, axis, [(at, at ^ mask) for at in range(count)])


def tie(value, *after):
    return lax.optimization_barrier((value, after))[0]


def far_masks(n):
    masks = [1 << at for at in range(2, n.bit_length() - 1)][::-1]
    if len(masks) >= 2:
        masks[0] |= masks[1]
    return masks


def shift_of(position, masks):
    total = 0
    for at, mask in enumerate(masks):
        if position >> at & 1:
            total ^= mask
    return total


def places(masks):
    mine = lax.axis_index("blk")
    return jnp.stack([mine ^ shift_of(position, masks) for position in range(1 << len(masks))]).astype(jnp.int32)


def widen(held, mask, *after):
    return jnp.concatenate([held, swap(tie(held, *after), "blk", mask)], axis=0)


def add_low(a, b):
    return (a.astype(jnp.float32) + b.astype(jnp.float32)).astype(jnp.bfloat16)


def fold(keep, came):
    half = keep.shape[0] // 2
    return add_low(keep[:half], came[:half]), add_low(keep[half:], came[half:])


def sum_over_win(value, mask):
    while mask < lax.axis_size("win"):
        value = add_low(value, swap(value, "win", mask))
        mask *= 2
    return value


def both_sides(side, mine, other):
    return jnp.stack([jnp.where(side == 1, other, mine), jnp.where(side == 1, mine, other)])


def gather_round(value, mask):
    came = swap(value, "blk", mask)
    upper = (lax.axis_index("blk") & mask) != 0
    return jnp.stack([jnp.where(upper, came, value), jnp.where(upper, value, came)])


def joined_columns(value):
    bits = value.ndim - 2
    value = value.transpose((bits,) + tuple(range(bits))[::-1] + (bits + 1,))
    return value.reshape(value.shape[0], -1)


def reduce_columns(value):
    mine = lax.axis_index("blk")
    mask = lax.axis_size("blk") // 2
    while mask:
        half = value.shape[-1] // 2
        upper = (mine & mask) != 0
        low, high = value[:, :half], value[:, half:]
        value = jnp.where(upper, high, low) + swap(jnp.where(upper, low, high), "blk", mask)
        mask //= 2
    mask = 1
    while mask < lax.axis_size("win"):
        value = value + swap(value, "win", mask)
        mask *= 2
    return value


def carried_in(through, value, backward):
    mine = lax.axis_index("blk")

    def compose(earlier, later):
        return jnp.stack([earlier[0] * later[0], later[0] * earlier[1] + later[1]])

    total = jnp.stack([through, value])
    ahead = jnp.stack([jnp.ones_like(through), jnp.zeros_like(value)])
    mask = 1
    hooks = []
    while mask < lax.axis_size("blk"):
        other = swap(total, "blk", mask)
        before = ((mine & mask) != 0) != backward
        ahead = jnp.where(before, compose(other, ahead), ahead)
        total = jnp.where(before, compose(other, total), compose(total, other))
        hooks.append(other)
        mask *= 2
    return ahead[1], hooks


def layer_norm(values, gain):
    centered = values - jnp.mean(values, axis=-1, keepdims=True)
    variance = jnp.mean(centered * centered, axis=-1, keepdims=True)
    return centered * lax.rsqrt(variance + 1e-05) * gain


def lane_spec(shape):
    lead = len(shape) - 1
    return pl.BlockSpec(tuple(shape[:-1]) + (LANES,), lambda i: (0,) * lead + (i,))

def lane_call(kernel, name, inputs, outputs, scratch, flops):
    width = inputs[0].shape[-1]
    return pl.pallas_call(
        kernel,
        grid=(width // LANES,),
        in_specs=[lane_spec(v.shape) for v in inputs],
        out_specs=[lane_spec(s) for s, _ in outputs],
        out_shape=[jax.ShapeDtypeStruct(s, t) for s, t in outputs],
        scratch_shapes=scratch,
        compiler_params=pltpu.CompilerParams(vmem_limit_bytes=VMEM_LIMIT),
        cost_estimate=LIGHT,
        name=name,
    )(*inputs)

def scan_kernel(x_ref, a_ref, mix_ref, ctx_ref, mid_ref, slope_ref, end_ref):
    blocks = ctx_ref.shape[0]
    a = a_ref[...]
    mix = mix_ref[...]
    zero = jnp.zeros_like(a)
    def before(group, state):
        state = list(state)
        for j in range(blocks):
            u, d = state[j]
            first = pl.multiple_of(j * BLOCK + group * 8, 8)
            rows = x_ref[pl.ds(first, 8), :]
            for k in range(8):
                d = a * d + u
                u = a * u + rows[k:k + 1, :]
            state[j] = (u, d)
        return tuple(state)
    state = lax.fori_loop(0, BEFORE // 8, before, tuple((zero, zero) for _ in range(blocks)))
    for j in range(blocks):
        mid_ref[j] = state[j][0]
        slope_ref[j] = state[j][1]
    def inside(group, state):
        state = list(state)
        for j in range(blocks):
            u = state[j]
            first = pl.multiple_of(j * BLOCK + BEFORE + group * 8, 8)
            rows = x_ref[pl.ds(first, 8), :]
            made = []
            for k in range(8):
                u = a * u + rows[k:k + 1, :]
                made.append(jnp.sum(mix * u, axis=0, keepdims=True))
            ctx_ref[j, pl.ds(pl.multiple_of(group * 8, 8), 8), :] = jnp.concatenate(made, axis=0)
            state[j] = u
        return tuple(state)
    state = lax.fori_loop(0, CTX // 8, inside, tuple(s[0] for s in state))
    for j in range(blocks):
        end_ref[j] = state[j]

def scan_states(x, a, mix):
    width = x.shape[-1]
    blocks = x.shape[0] // BLOCK
    states = ((blocks,) + a.shape, jnp.float32)
    return lane_call(scan_kernel, "scan_states", [x, a, mix], [((blocks, CTX, width), jnp.float32), states, states, states], [], 8 * x.size * a.shape[0])

def fan(rate, weight, lag, rows, store):
    count = rate.shape[0]
    for c in range(rate.shape[1] // 128):
        lanes = slice(c * 128, (c + 1) * 128)
        row = lax.broadcasted_iota(jnp.int32, (8, 128), 0).astype(jnp.float32)
        values = tuple(weight[s:s + 1, lanes] * jnp.exp(-rate[s:s + 1, lanes] * (lag(row))) for s in range(count))
        steps = [jnp.broadcast_to(jnp.exp(-8.0 * rate[s:s + 1, lanes]), (8, 128)) for s in range(count)]
        def group_of(group, values):
            total = values[0]
            for v in values[1:]:
                total = total + v
            store(group, lanes, total)
            return tuple(v * s for v, s in zip(values, steps))
        lax.fori_loop(0, rows // 8, group_of, values)

def context_kernel(base_ref, rate_ref, weight_ref, out_ref):
    for j in range(base_ref.shape[0]):
        def store(group, lanes, total, j=j):
            rows = pl.ds(pl.multiple_of(group * 8, 8), 8)
            out_ref[j, rows, lanes] = base_ref[j, rows, lanes] + total
        fan(rate_ref[...], weight_ref[j], lambda row: row + (BEFORE + 1.0), CTX, store)

def finish_contexts(base, rate, weight):
    return lane_call(context_kernel, "finish_contexts", [base, rate, weight], [(base.shape, jnp.float32)], [], 4 * base.size * rate.shape[0])[0]

def adjoint_kernel(g_ref, a_ref, out_ref):
    blocks = g_ref.shape[0]
    a = a_ref[...]
    def step(group, state):
        state = list(state)
        for j in range(blocks):
            first = pl.multiple_of(CTX - 8 - group * 8, 8)
            rows = g_ref[j, pl.ds(first, 8), :]
            for k in range(7, -1, -1):
                state[j] = a * state[j] + rows[k:k + 1, :]
        return tuple(state)
    state = lax.fori_loop(0, CTX // 8, step, tuple(jnp.zeros_like(a) for _ in range(blocks)))
    for j in range(blocks):
        out_ref[j] = state[j]

def adjoint_sums(g, a):
    return lane_call(adjoint_kernel, "adjoint_sums", [g, a], [((g.shape[0],) + a.shape, jnp.float32)], [], 4 * g.size * a.shape[0])[0]

def back_kernel(x_ref, g_ref, mid_ref, enter_ref, rate_ref, a_ref, beta_ref, mix_ref, gx_ref, gmix_ref, gbeta_ref, ga_ref, leave_ref, held):
    blocks = g_ref.shape[0]
    a = a_ref[...]
    beta = beta_ref[...]
    mix = mix_ref[...]
    zero = jnp.zeros_like(a)
    gmix_ref[...] = zero
    gbeta_ref[...] = zero
    ga_ref[...] = zero
    for j in range(blocks):
        def ahead(group, s):
            first = pl.multiple_of(j * BLOCK + BEFORE + group * 8, 8)
            rows = x_ref[pl.ds(first, 8), :]
            for k in range(8):
                held[group * 8 + k] = s
                s = a * s + beta * rows[k:k + 1, :]
            return s
        last = lax.fori_loop(0, CTX // 8, ahead, mid_ref[j])
        def back(at, state):
            carry, cur, gmix, gbeta, ga = state
            group = CTX // 8 - 1 - at
            first = pl.multiple_of(group * 8, 8)
            xs = x_ref[pl.ds(pl.multiple_of(j * BLOCK + BEFORE + group * 8, 8), 8), :]
            gs = g_ref[j, pl.ds(first, 8), :]
            made = [None] * 8
            for k in range(7, -1, -1):
                g = gs[k:k + 1, :]
                lam = carry + mix * g
                prev = held[group * 8 + k]
                gmix = gmix + g * cur
                gbeta = gbeta + lam * xs[k:k + 1, :]
                ga = ga + lam * prev
                made[k] = jnp.sum(beta * lam, axis=0, keepdims=True)
                carry = a * lam
                cur = prev
            gx_ref[pl.ds(pl.multiple_of(j * BLOCK + BEFORE + group * 8, 8), 8), :] = jnp.concatenate(made, axis=0)
            return carry, cur, gmix, gbeta, ga
        carry, _, gmix, gbeta, ga = lax.fori_loop(0, CTX // 8, back, (enter_ref[j], last, zero, zero, zero))
        gmix_ref[...] += gmix
        gbeta_ref[...] += gbeta
        ga_ref[...] += ga
        leave_ref[j] = carry
        def store(group, lanes, total, j=j):
            rows = pl.ds(pl.multiple_of(j * BLOCK + BEFORE - 8 - group * 8, 8), 8)
            gx_ref[rows, lanes] = total
        fan(rate_ref[...], beta * carry, lambda row: 7.0 - row, BEFORE, store)

def back_states(x, g, mid, enter, rate, a, beta, mix):
    states = (a.shape, jnp.float32)
    return lane_call(back_kernel, "back_states", [x, g, mid, enter, rate, a, beta, mix],
        [(x.shape, jnp.float32), states, states, states, (mid.shape, jnp.float32)],
        [pltpu.VMEM((CTX, a.shape[0], LANES), jnp.float32)], 20 * g.size * a.shape[0])

def state_ahead(begin, markers, carried, ends, decay):
    begins = []
    for j in range(carried.shape[0]):
        begin = jnp.where(markers[j] > 0, carried[j], begin)
        begins.append(begin)
        begin = decay * begin + ends[j]
    return jnp.stack(begins), begin

def adjoint_behind(enter, markers, locals_, decay):
    enters, starts = [], []
    for j in range(locals_.shape[0])[::-1]:
        enters.append(enter)
        start = decay * enter + locals_[j]
        starts.append(start)
        enter = jnp.where(markers[j] > 0, 0.0, start)
    return jnp.stack(enters[::-1]), jnp.stack(starts[::-1]), enter


def load_pieces(n, parts, rows, place_ref, refs, skip, target, sems):
    lists = [[] for _ in range(parts)]
    count = n // len(refs)
    for position in range(n):
        src = refs[position // count].at[position % count]
        first = pl.multiple_of(place_ref[position] * (target.shape[1] // n) + skip, rows)
        for part in range(parts):
            lists[part].append(
                pltpu.make_async_copy(
                    src.at[pl.ds(part * rows, rows)],
                    target.at[part, pl.ds(first, rows)],
                    sems.at[part * n + position],
                )
            )
    return lists


def project_kernel(n, rows, place_ref, x_ref, *refs):
    mine, theirs = refs[:4], refs[4:8]
    out_ref, weights_ref, held, load_sems, store_sems = refs[8:]
    at = pl.program_id(0)
    parts = 3
    half = rows // 2
    lists = load_pieces(n, parts, half, place_ref, mine, place_ref[n], held, load_sems.at[pl.ds(0, 3 * n)])
    more = load_pieces(n, parts, half, place_ref, theirs, place_ref[n + 1], held, load_sems.at[pl.ds(3 * n, 3 * n)])
    lists = [a + b for a, b in zip(lists, more)]
    stores = [pltpu.make_async_copy(held.at[part], weights_ref.at[part], store_sems.at[part]) for part in range(parts)]

    @pl.when(at == 0)
    def _():
        for part in range(parts):
            for copy in lists[part]:
                copy.start()

    for part in range(parts):
        @pl.when(at == part)
        def _(part=part):
            for copy in lists[part]:
                copy.wait()
            stores[part].start()

    out_ref[0] = jnp.dot(x_ref[...], held[at], preferred_element_type=jnp.float32).astype(out_ref.dtype)

    @pl.when(at == parts - 1)
    def _():
        for store in stores:
            store.wait()


def project(place, x, mine, theirs):
    n = place.shape[0] - 2
    tokens, width = x.shape
    rows = width // n
    parts = 3
    anywhere = pl.BlockSpec(memory_space=pl.ANY)
    return pl.pallas_call(
        functools.partial(project_kernel, n, rows),
        grid_spec=pltpu.PrefetchScalarGridSpec(
            num_scalar_prefetch=1,
            grid=(parts,),
            in_specs=[pl.BlockSpec((tokens, width), lambda i, *_: (0, 0))] + [anywhere] * 8,
            out_specs=[pl.BlockSpec((1, tokens, width), lambda i, *_: (i, 0, 0)), anywhere],
            scratch_shapes=[
                pltpu.VMEM((parts, width, width), jnp.bfloat16),
                pltpu.SemaphoreType.DMA((2 * n * parts,)),
                pltpu.SemaphoreType.DMA((parts,)),
            ],
        ),
        out_shape=[
            jax.ShapeDtypeStruct((parts, tokens, width), jnp.bfloat16),
            jax.ShapeDtypeStruct((parts, width, width), jnp.bfloat16),
        ],
        compiler_params=pltpu.CompilerParams(vmem_limit_bytes=VMEM_LIMIT),
        cost_estimate=LIGHT,
        name="project",
    )(place, x, *mine, *theirs)


def branch_kernel(n, rows, place_ref, x_ref, mixed_ref, gain_ref, *refs):
    middle_ref, normed_ref, weights_ref, held, load_sems, store_sem = refs[4:]
    at = pl.program_id(0)
    copies = load_pieces(n, 1, rows, place_ref, refs[:4], 0, held, load_sems)[0]
    store = pltpu.make_async_copy(held.at[0], weights_ref, store_sem.at[0])

    @pl.when(at == 0)
    def _():
        for copy in copies:
            copy.start()
        for copy in copies:
            copy.wait()
        store.start()

    middle = x_ref[...].astype(jnp.float32) + jnp.dot(mixed_ref[...], held[0], preferred_element_type=jnp.float32)
    middle_ref[...] = middle
    normed_ref[...] = layer_norm(middle, gain_ref[...]).astype(normed_ref.dtype)

    @pl.when(at == pl.num_programs(0) - 1)
    def _():
        store.wait()


def branch(place, x, mixed, gain, pieces):
    n = place.shape[0]
    tokens, width = x.shape
    rows = width // n
    tile = 256
    anywhere = pl.BlockSpec(memory_space=pl.ANY)
    strip = pl.BlockSpec((tile, width), lambda i, *_: (i, 0))
    return pl.pallas_call(
        functools.partial(branch_kernel, n, rows),
        grid_spec=pltpu.PrefetchScalarGridSpec(
            num_scalar_prefetch=1,
            grid=(tokens // tile,),
            in_specs=[strip, strip, pl.BlockSpec((1, width), lambda i, *_: (0, 0))] + [anywhere] * 4,
            out_specs=[strip, strip, anywhere],
            scratch_shapes=[
                pltpu.VMEM((1, width, width), jnp.bfloat16),
                pltpu.SemaphoreType.DMA((n,)),
                pltpu.SemaphoreType.DMA((1,)),
            ],
        ),
        out_shape=[
            jax.ShapeDtypeStruct((tokens, width), jnp.float32),
            jax.ShapeDtypeStruct((tokens, width), jnp.bfloat16),
            jax.ShapeDtypeStruct((width, width), jnp.bfloat16),
        ],
        compiler_params=pltpu.CompilerParams(vmem_limit_bytes=VMEM_LIMIT),
        cost_estimate=LIGHT,
        name="branch",
    )(place, x, mixed, gain, *pieces)


def weight_grad_kernel(n, rows, lefts, rights, place_ref, *refs):
    x_refs, g_refs = refs[:lefts], refs[lefts : lefts + rights]
    keep_ref, send_ref, x_v, g_v, turned, held, sems = refs[lefts + rights :]
    at = pl.program_id(0)
    loads = [pltpu.make_async_copy(ref, x_v.at[i], sems.at[i]) for i, ref in enumerate(x_refs)]
    loads += [pltpu.make_async_copy(ref, g_v.at[i], sems.at[lefts + i]) for i, ref in enumerate(g_refs)]

    @pl.when(at == 0)
    def _():
        for copy in loads:
            copy.start()

    for i in range(rights):
        @pl.when(at == i)
        def _(i=i):
            if i < lefts:
                loads[i].wait()
                turned[...] = x_v[i].T
            loads[lefts + i].wait()

    held[...] = jnp.dot(turned[...], g_v[at], preferred_element_type=jnp.float32).astype(held.dtype)
    for position in range(n):
        first = pl.multiple_of(place_ref[position] * rows, rows)
        target = keep_ref if position < n // 2 else send_ref
        target[position % (n // 2)] = held[pl.ds(first, rows), :]


def weight_grad(place, x, g):
    n = place.shape[0]
    tokens, width = x[0].shape
    parts = len(g)
    rows = width // n
    half = pl.BlockSpec((n // 2, rows, width), lambda i, *_: (0, i, 0))
    anywhere = pl.BlockSpec(memory_space=pl.ANY)
    return pl.pallas_call(
        functools.partial(weight_grad_kernel, n, rows, len(x), parts),
        grid_spec=pltpu.PrefetchScalarGridSpec(
            num_scalar_prefetch=1,
            grid=(parts,),
            in_specs=[anywhere] * (len(x) + parts),
            out_specs=[half, half],
            scratch_shapes=[
                pltpu.VMEM((len(x), tokens, width), jnp.bfloat16),
                pltpu.VMEM((parts, tokens, width), jnp.bfloat16),
                pltpu.VMEM((width, tokens), jnp.bfloat16),
                pltpu.VMEM((width, width), jnp.bfloat16),
                pltpu.SemaphoreType.DMA((len(x) + parts,)),
            ],
        ),
        out_shape=[jax.ShapeDtypeStruct((n // 2, parts * rows, width), jnp.bfloat16)] * 2,
        compiler_params=pltpu.CompilerParams(vmem_limit_bytes=VMEM_LIMIT),
        cost_estimate=LIGHT,
        name="weight_grad",
    )(place, *x, *g)


def ff_kernel(n, tiles, table_ref, n2_ref, n2s_ref, cot_ref, cots_ref, *rest):
    (mine_low, mine_high, theirs_low, theirs_high, out_ref, gn2_ref, outs_ref, gn2s_ref, mine_ref, theirs_ref,
     n2_v, n2t_v, cot_v, weights_v, out_v, gn2_v, low_v, pack_v, sems, load_sems, store_sems) = rest
    f32, bf = jnp.float32, jnp.bfloat16
    t = pl.program_id(0)
    hidden = width = n2_ref.shape[1]
    rows, span = width // n, hidden // tiles
    half_rows = pack_v.shape[1] // 2
    side = table_ref[2 * n]
    kinds = (side, 1 - side)

    def pieces(refs, which):
        copies = []
        for position in range(n):
            src = refs[position // (n // 2)].at[position % (n // 2)]
            first = pl.multiple_of(table_ref[kinds[which] * n + position] * rows, rows)
            copies.append(pltpu.make_async_copy(
                src, weights_v.at[kinds[which], pl.ds(first, rows)], load_sems.at[which * n + position]))
        return copies

    @pl.when(t == 0)
    def _():
        weights = pieces((mine_low, mine_high), 0) + pieces((theirs_low, theirs_high), 1)
        first = [pltpu.make_async_copy(n2_ref, n2_v.at[0], sems.at[0]), pltpu.make_async_copy(n2s_ref, n2_v.at[1], sems.at[1])]
        second = [pltpu.make_async_copy(cot_ref, cot_v.at[0], sems.at[2]), pltpu.make_async_copy(cots_ref, cot_v.at[1], sems.at[3])]
        for copy in first + weights + second:
            copy.start()
        out_v[...] = jnp.zeros_like(out_v)
        gn2_v[...] = jnp.zeros_like(gn2_v)
        for copy in first:
            copy.wait()
        for at in range(2):
            n2t_v[at] = n2_v[at].T
        for copy in weights + second:
            copy.wait()

    cols = pl.ds(pl.multiple_of(t * span, span), span)
    up = weights_v[0, :, cols]
    down = weights_v[1, cols, :]
    gup = gdown = 0.0
    for at in range(2):
        cot = cot_v[at]
        hid = jnp.dot(n2_v[at], up, preferred_element_type=f32)
        gact = lax.dot_general(cot, down, NT, preferred_element_type=f32)
        sq = hid * hid
        th = jnp.tanh(GC * hid * (1.0 + GQ * sq))
        half = 0.5 * (1.0 + th)
        act = (hid * half).astype(bf)
        slope = half + (0.5 * GC) * hid * (1.0 - th * th) * (1.0 + (3.0 * GQ) * sq)
        gh = (gact * slope).astype(bf)
        out_v[at] += jnp.dot(act, down, preferred_element_type=f32)
        gn2_v[at] += lax.dot_general(gh, up, NT, preferred_element_type=f32)
        gdown += lax.dot_general(act, cot, TN, preferred_element_type=f32)
        gup += jnp.dot(n2t_v[at], gh, preferred_element_type=f32)
    gup = gup.astype(bf)
    gdown = gdown.astype(bf)
    groups = span // 128
    for d in range(n):
        for g in range(groups):
            first = pl.multiple_of((t * groups + g) * rows, rows)
            pack_v[d, pl.ds(first, rows), :] = gup[d * rows : (d + 1) * rows, g * 128 : (g + 1) * 128]
    slots = span // rows
    for o in range(slots):
        for g in range(width // 128):
            first = half_rows + g * rows
            pack_v[t * slots + o, first : first + rows, :] = gdown[o * rows : (o + 1) * rows, g * 128 : (g + 1) * 128]

    @pl.when(t == tiles - 1)
    def _():
        copies = []
        for which, ref in enumerate((mine_ref, theirs_ref)):
            for position in range(n):
                slot = table_ref[kinds[which] * n + position]
                src = pack_v.at[slot, pl.ds(pl.multiple_of(kinds[which] * half_rows, half_rows), half_rows)]
                copies.append(pltpu.make_async_copy(src, ref.at[position], store_sems.at[which * n + position]))
        copies.append(pltpu.make_async_copy(out_v.at[0], out_ref, sems.at[0]))
        copies.append(pltpu.make_async_copy(gn2_v.at[0], gn2_ref, sems.at[1]))
        for copy in copies:
            copy.start()
        low_v[0] = gn2_v[1].astype(bf)
        low_v[1] = out_v[1].astype(bf)
        for at, ref in enumerate((gn2s_ref, outs_ref)):
            copy = pltpu.make_async_copy(low_v.at[at], ref, sems.at[2 + at])
            copy.start()
            copies.append(copy)
        for copy in copies:
            copy.wait()


def feed_forward(table, n2, n2_other, cot, cot_other, mine, theirs, tiles):
    n = (table.shape[0] - 1) // 2
    tokens, width = n2.shape
    rows = width // n
    half_rows = width // 128 * rows
    bf, f32 = jnp.bfloat16, jnp.float32
    anywhere = pl.BlockSpec(memory_space=pl.ANY)
    shape = jax.ShapeDtypeStruct
    return pl.pallas_call(
        functools.partial(ff_kernel, n, tiles),
        grid_spec=pltpu.PrefetchScalarGridSpec(
            num_scalar_prefetch=1,
            grid=(tiles,),
            in_specs=[anywhere] * 8,
            out_specs=[anywhere] * 6,
            scratch_shapes=[
                pltpu.VMEM((2, tokens, width), bf),
                pltpu.VMEM((2, width, tokens), bf),
                pltpu.VMEM((2, tokens, width), bf),
                pltpu.VMEM((2, width, width), bf),
                pltpu.VMEM((2, tokens, width), f32),
                pltpu.VMEM((2, tokens, width), f32),
                pltpu.VMEM((2, tokens, width), bf),
                pltpu.VMEM((n, 2 * half_rows, 128), bf),
                pltpu.SemaphoreType.DMA((4,)),
                pltpu.SemaphoreType.DMA((2 * n,)),
                pltpu.SemaphoreType.DMA((2 * n,)),
            ],
        ),
        out_shape=[shape((tokens, width), f32)] * 2 + [shape((tokens, width), bf)] * 2 + [shape((n, half_rows, 128), bf)] * 2,
        compiler_params=pltpu.CompilerParams(vmem_limit_bytes=VMEM_LIMIT),
        cost_estimate=pl.CostEstimate(flops=24 * tokens * width * width, bytes_accessed=32 << 20, transcendentals=2 * tokens * width),
        name="feed_forward",
    )(table, n2, n2_other, cot, cot_other, *mine, *theirs)


def causal(rows, cols, first):
    r = lax.broadcasted_iota(jnp.int32, (rows, cols), 0) + first
    c = lax.broadcasted_iota(jnp.int32, (rows, cols), 1)
    return c <= r

def attend_forward_kernel(flag_ref, q_ref, kc_ref, kp_ref, ko_ref, vc_ref, vp_ref, vo_ref, mixed_ref, total_ref):
    scale = HEAD_DIM ** -0.5
    f32 = jnp.float32
    def tile(at, earlier):
        rows = pl.ds(at * TILE, TILE)
        own = (at + 1) * TILE
        q = q_ref[rows, :]
        so = lax.dot_general(q, ko_ref[:own, :], NT, preferred_element_type=f32)
        so = jnp.where(causal(TILE, own, at * TILE), so, -1e30)
        parts = [so]
        values = [vo_ref[:own, :]]
        if earlier:
            parts = [lax.dot_general(q, kc_ref[...], NT, preferred_element_type=f32), lax.dot_general(q, kp_ref[...], NT, preferred_element_type=f32)] + parts
            values = [vc_ref[...], vp_ref[...]] + values
        top = functools.reduce(jnp.maximum, [jnp.max(s, axis=-1, keepdims=True) for s in parts])
        shift = top * (scale * LOG2E)
        soft = [jnp.exp2(s * (scale * LOG2E) - shift) for s in parts]
        total = sum(jnp.sum(s, axis=-1, keepdims=True) for s in soft)
        inverse = 1.0 / total
        mixed = sum(jnp.dot((s * inverse).astype(jnp.bfloat16), v, preferred_element_type=f32) for s, v in zip(soft, values))
        mixed_ref[rows, :] = mixed.astype(mixed_ref.dtype)
        total_ref[0, rows, :] = shift + jnp.log2(total)
    flagged = flag_ref[0] > 0
    for at in range(BLOCK // TILE):
        pl.when(flagged)(functools.partial(tile, at, False))
        pl.when(jnp.logical_not(flagged))(functools.partial(tile, at, True))

def head_spec(rows, row_at=0, lead=None):
    if lead is None:
        return pl.BlockSpec((rows, HEAD_DIM), lambda h, *_: (row_at, h))
    return pl.BlockSpec((None, rows, HEAD_DIM), lambda h, *_: (lead, row_at, h))

def attend_forward(flag, query, key_ctx, key_prev, key_own, value_ctx, value_prev, value_own):
    ops=[query,key_ctx,key_prev,key_own,value_ctx,value_prev,value_own]
    sizes=[BLOCK,CTX,BLOCK,BLOCK,CTX,BLOCK,BLOCK]
    return pl.pallas_call(
        attend_forward_kernel,
        grid_spec=pltpu.PrefetchScalarGridSpec(num_scalar_prefetch=1, grid=(HEADS,),
            in_specs=[head_spec(s, o[1], o[2] if len(o) > 2 else None) for o, s in zip(ops, sizes)],
            out_specs=[head_spec(BLOCK), pl.BlockSpec((1, BLOCK, 1), lambda h, *_: (h, 0, 0))]),
        out_shape=[jax.ShapeDtypeStruct((BLOCK, HEADS * HEAD_DIM), jnp.bfloat16), jax.ShapeDtypeStruct((HEADS, BLOCK, 1), jnp.float32)],
        compiler_params=pltpu.CompilerParams(vmem_limit_bytes=VMEM_LIMIT),
        cost_estimate=LIGHT,
        name="attend_forward",
    )(flag, *[o[0] for o in ops])

def attend_backward_kernel(merge, flag_ref, q_ref, kc_ref, kp_ref, ko_ref, vc_ref, vp_ref, vo_ref, total_ref, g_ref, *rest):
    scale = HEAD_DIM ** -0.5
    f32, bf = jnp.float32, jnp.bfloat16
    if merge:
        kadd_ref, vadd_ref, dq_ref, dkc_ref, dkp_ref, dko_ref, dvc_ref, dvp_ref, dvo_ref, acc_k, acc_v = rest
    else:
        dq_ref, dkc_ref, dkp_ref, dko_ref, dvc_ref, dvp_ref, dvo_ref, acc_k, acc_v = rest
    lead = CTX + BLOCK
    acc_k[...] = jnp.zeros_like(acc_k)
    acc_v[...] = jnp.zeros_like(acc_v)
    def tile(at, earlier):
        rows = pl.ds(at * TILE, TILE)
        own = (at + 1) * TILE
        q = q_ref[rows, :]
        g = g_ref[rows, :]
        total = total_ref[0, rows, :]
        keys = [(ko_ref[:own, :], vo_ref[:own, :], lead, own)]
        if earlier:
            keys = [(kc_ref[...], vc_ref[...], 0, CTX), (kp_ref[...], vp_ref[...], CTX, BLOCK)] + keys
        softs, grads = [], []
        for k, v, first, size in keys:
            s = lax.dot_general(q, k, NT, preferred_element_type=f32)
            s = s * (scale * LOG2E) - total
            if first == lead:
                s = jnp.where(causal(TILE, own, at * TILE), s, -1e30)
            softs.append(jnp.exp2(s))
            grads.append(lax.dot_general(g, v, NT, preferred_element_type=f32))
        products = [p * d for p, d in zip(softs, grads)]
        rowsum = sum(jnp.sum(x, axis=-1, keepdims=True) for x in products)
        dq = 0.0
        for (k, v, first, size), p, x in zip(keys, softs, products):
            ds = (x - p * rowsum).astype(bf)
            dq += jnp.dot(ds, k, preferred_element_type=f32)
            at_rows = pl.ds(first, size)
            acc_k[at_rows, :] += lax.dot_general(ds, q, TN, preferred_element_type=f32)
            acc_v[at_rows, :] += lax.dot_general(p.astype(bf), g, TN, preferred_element_type=f32)
        dq_ref[rows, :] = (dq * scale).astype(dq_ref.dtype)
    flagged = flag_ref[0] > 0
    for at in range(BLOCK // TILE):
        pl.when(flagged)(functools.partial(tile, at, False))
        pl.when(jnp.logical_not(flagged))(functools.partial(tile, at, True))
    more_k = kadd_ref[...] if merge else 0.0
    more_v = vadd_ref[...] if merge else 0.0
    dkc_ref[...] = (acc_k[:CTX, :] * scale).astype(dkc_ref.dtype)
    dvc_ref[...] = acc_v[:CTX, :].astype(dvc_ref.dtype)
    dkp_ref[...] = (acc_k[CTX:lead, :] * scale + more_k).astype(dkp_ref.dtype)
    dvp_ref[...] = (acc_v[CTX:lead, :] + more_v).astype(dvp_ref.dtype)
    dko_ref[...] = (acc_k[lead:, :] * scale).astype(dko_ref.dtype)
    dvo_ref[...] = acc_v[lead:, :].astype(dvo_ref.dtype)

def attend_backward(flag, query, key_ctx, key_prev, key_own, value_ctx, value_prev, value_own, total, grad, add=None):
    ops=[query,key_ctx,key_prev,key_own,value_ctx,value_prev,value_own]
    sizes=[BLOCK,CTX,BLOCK,BLOCK,CTX,BLOCK,BLOCK]
    specs=[head_spec(s, o[1], o[2] if len(o) > 2 else None) for o, s in zip(ops, sizes)]
    specs+=[pl.BlockSpec((1, BLOCK, 1), lambda h, *_: (h, 0, 0)), head_spec(BLOCK, grad[1])]
    args=[o[0] for o in ops]+[total, grad[0]]
    if add is not None:
        specs+=[head_spec(BLOCK)]*2
        args+=list(add)
    width=HEADS*HEAD_DIM
    bf,f32=jnp.bfloat16,jnp.float32
    out=lambda r,t: jax.ShapeDtypeStruct((r,width),t)
    return pl.pallas_call(
        functools.partial(attend_backward_kernel, add is not None),
        grid_spec=pltpu.PrefetchScalarGridSpec(num_scalar_prefetch=1, grid=(HEADS,),
            in_specs=specs,
            out_specs=[head_spec(BLOCK), head_spec(CTX), head_spec(BLOCK), head_spec(BLOCK), head_spec(CTX), head_spec(BLOCK), head_spec(BLOCK)],
            scratch_shapes=[pltpu.VMEM((CTX+2*BLOCK,HEAD_DIM),f32)]*2),
        out_shape=[out(BLOCK,bf), out(CTX,bf), out(BLOCK,bf), out(BLOCK,f32), out(CTX,bf), out(BLOCK,bf), out(BLOCK,f32)],
        compiler_params=pltpu.CompilerParams(vmem_limit_bytes=VMEM_LIMIT),
        cost_estimate=LIGHT,
        name="attend_backward",
    )(flag, *args)


def adamw_step(weight, first, second, gradient, step_rate, shrink):
    new_first = 0.9 * first + 0.1 * gradient
    new_second = 0.95 * second + 0.05 * gradient * gradient
    scaled_first = new_first / (1.0 - 0.9**STEP)
    scaled_second = new_second / (1.0 - 0.95**STEP)
    update = scaled_first / (jnp.sqrt(scaled_second) + 1e-08) + shrink * weight
    return (new_first, new_second, weight - step_rate * update)


def body(
    tokens,
    cotangent,
    carry_in,
    block_flags,
    qkv_w,
    qkv_m,
    qkv_v,
    out_w,
    out_m,
    out_v,
    up_w,
    up_m,
    up_v,
    down_w,
    down_m,
    down_v,
    gain_w,
    gain_m,
    gain_v,
    ssm_w,
    ssm_m,
    ssm_v,
):
    low_type = jnp.bfloat16
    n = lax.axis_size("blk")
    width = tokens.shape[-1]
    rows = width // n
    span = FF // n // 2
    far = far_masks(n)
    place = places(far + [2, 1])
    ff_place = places([1] + far + [2])
    side = lax.axis_index("win") & 1
    slots = 2 * (ff_place // 2) + jnp.arange(n, dtype=jnp.int32) % 2
    ff_table = jnp.concatenate([ff_place, slots, side[None].astype(jnp.int32)])
    upper_core = (lax.axis_index("blk") & 1) != 0


    small = jnp.concatenate([gain_w, ssm_w.reshape(-1, ssm_w.shape[-1])], axis=0)
    small = gather_round(small, n // 2)
    qkv_half = qkv_w.astype(low_type).reshape(3, 2, rows // 2, width)
    held = jnp.where(side == 1, qkv_half[:, 1], qkv_half[:, 0]).reshape(1, -1, width)
    for mask in far[:-1]:
        held = widen(held, mask)
    mask = n // 4
    while mask > 2:
        small = gather_round(small, mask)
        mask //= 2
    small = gather_round(tie(small, held), 2)
    small = gather_round(small, 1)
    small = joined_columns(small)
    near = widen(held, far[-1])
    across = swap(near, "blk", 2)
    near_y = swap(near, "win", 1)
    near_c = swap(near, "blk", 1)

    gain_all, ssm_all = small[:2], small[2:].reshape(ssm_w.shape[:2] + (width,))
    inputs = tokens[0].astype(jnp.float32)
    flags = block_flags[0]
    markers = flags.astype(jnp.float32)
    carried = carry_in[0]
    block_count = markers.shape[0]
    last = block_count - 1
    forward_pairs = [(at, at + 1) for at in range(n - 1)]
    normed, norm_back = jax.vjp(layer_norm, inputs, gain_all[0])
    normed_low = normed.astype(low_type)
    rate = jnp.exp(ssm_all[0])
    decay = jnp.exp(-rate)
    root = jnp.sqrt(-jnp.expm1(-2.0 * rate))
    beta = root * ssm_all[1]
    over_block = jnp.exp(-rate * BLOCK)
    through = jnp.prod(1.0 - markers) * jnp.exp(-rate * (block_count * BLOCK))
    up_parts = up_w.astype(low_type).reshape(rows, n // 2, 2, 2, span).transpose(3, 2, 0, 1, 4).reshape(2, 2 * rows, width)
    down_parts = down_w.astype(low_type).reshape(2, span, width)
    halves = jnp.concatenate([up_parts, down_parts], axis=1)
    own_half = jnp.where(upper_core, halves[1], halves[0])
    other_half = jnp.where(upper_core, halves[0], halves[1])
    came_half = swap(other_half, "blk", 1)
    cot = cotangent[0]
    cot_other = swap(cot, "blk", 1)

    def chunk(c):
        ups = [own_half[c * rows : (c + 1) * rows], came_half[c * rows : (c + 1) * rows]]
        is_own = upper_core == (c == 1)
        down = jnp.where(is_own, own_half[2 * rows :], came_half[2 * rows :])
        return jnp.where(side == 1, down, jnp.concatenate(ups, axis=0))

    first = jnp.concatenate([out_w.astype(low_type), chunk(0)], axis=0)[None]
    second = chunk(1)[None]
    first_came = swap(tie(first, near), "blk", far[0])
    base_ctx, middles, slopes, ends = scan_states(tie(normed, near, first), decay, ssm_all[2] * beta)
    nothing = jnp.zeros_like(rate)
    _, local_end = state_ahead(nothing, markers, carried, beta * tie(ends, first_came), over_block)
    across = tie(across, ends)
    across_y = swap(across, "win", 1)
    across_c = swap(across, "blk", 1)
    near_yc = swap(near_y, "blk", 1)
    entering, hooks = carried_in(through, tie(local_end, across), False)
    first = jnp.concatenate([first, tie(first_came, entering)], axis=0)
    for mask in far[1:-1]:
        first = widen(first, mask)
    first_came = swap(first, "blk", far[-1])
    sent = tie(normed_low[-BLOCK:], hooks[1])
    came_normed = lax.ppermute(sent, "blk", forward_pairs)
    second = tie(second, first)
    second_came = swap(second, "blk", far[0])
    begins, _ = state_ahead(tie(entering, across_y), markers, carried, beta * ends, over_block)
    contexts_low = finish_contexts(base_ctx, rate, ssm_all[2] * begins).astype(low_type).reshape(-1, width)
    came_ctx = lax.ppermute(contexts_low[-CTX:], "blk", forward_pairs)
    across_yc = swap(tie(across_y, contexts_low), "blk", 1)
    table = jnp.concatenate([place, jnp.stack([side, 1 - side]).astype(jnp.int32) * (rows // 2)])
    projected, qkv_all = project(
        table, tie(normed_low, contexts_low, came_ctx), [near, across, near_c, across_c], [near_y, across_y, near_yc, across_yc]
    )
    first_came = tie(first_came, projected)
    first = jnp.concatenate([first, first_came], axis=0)

    out_near = first[:, :rows]
    out_across = swap(out_near, "blk", 2)
    out_near_c = swap(out_near, "blk", 1)
    mine0 = [first[:, rows:].reshape(-1, rows, width)]
    theirs0 = [swap(mine0[0], "win", 1)]
    mine0.append(swap(tie(mine0[0], out_near), "blk", 2))
    second = jnp.concatenate([second, tie(second_came, projected)], axis=0)
    for mask in far[1:-1]:
        second = widen(second, mask)
    second_came = swap(second, "blk", far[-1])
    extra = jnp.concatenate([came_normed, contexts_low, came_ctx], axis=0)
    extra = tie(extra, out_near, mine0[0], second)
    extra_pair = jnp.einsum("td,kde->kte", extra, qkv_all[1:], preferred_element_type=jnp.float32).astype(low_type)

    context_rows = BLOCK // CTX

    def lists(at):
        own = [(projected, at, 1), (projected, at, 2)]
        ctx_at = context_rows + (at - 1 if at else block_count)
        if at:
            earlier = [(extra_pair, ctx_at, 0), (projected, at - 1, 1), (extra_pair, ctx_at, 1), (projected, at - 1, 2)]
        else:
            earlier = [(extra_pair, ctx_at, 0), (extra_pair, 0, 0), (extra_pair, ctx_at, 1), (extra_pair, 0, 1)]
        return [(projected, at, 0), earlier[0], earlier[1], own[0], earlier[2], earlier[3], own[1]]

    attended = {}
    place_flags = flags
    for at in range(block_count)[::-1]:
        attended[at] = attend_forward(place_flags[at : at + 1], *lists(at))
        if at == last:
            out_across = tie(out_across, attended[at][0])
            out_across_c = swap(out_across, "blk", 1)
            theirs0.append(swap(tie(mine0[1], attended[at][0]), "win", 1))
            second = jnp.concatenate([second, tie(second_came, attended[at][0])], axis=0)
            mine1 = [second.reshape(-1, rows, width)]
            theirs1 = [swap(tie(mine1[0], mine0[1]), "win", 1)]
            mine1.append(swap(mine1[0], "blk", 2))
            place_flags = tie(flags, out_across, mine0[1], mine1[0])
    mixed_low = jnp.concatenate([attended[at][0] for at in range(block_count)], axis=0)
    totals = [attended[at][1] for at in range(block_count)]
    theirs1.append(swap(tie(mine1[1], mixed_low), "win", 1))
    middle, normed_two_low, out_all = branch(
        place, tokens[0], tie(mixed_low, theirs0[0], theirs0[1], mine1[1]), gain_all[1:], [out_near, out_across, out_near_c, out_across_c]
    )
    _, norm_two_back = jax.vjp(layer_norm, middle, gain_all[1])
    n2_other = swap(normed_two_low, "blk", 1)
    ff = [feed_forward(ff_table, normed_two_low, n2_other, cot, cot_other, mine0, theirs0, TILES)]
    keep0, send0 = ff[0][4:]
    came0 = swap(send0, "win", 1)
    backs = [swap(ff[0][3], "blk", 1), swap(ff[0][2], "blk", 1)]
    ff.append(feed_forward(ff_table, tie(normed_two_low, send0, ff[0][3]), n2_other, cot, cot_other, mine1, theirs1, TILES))
    keep1, send1 = ff[1][4:]
    came1 = swap(tie(send1, came0), "win", 1)
    keep0, came0 = tie((keep0, came0), keep1)
    keep0, send0 = fold(keep0, came0)
    came0 = swap(send0, "blk", 2)
    own_grad, other_grad, other_out = tie((ff[1][1], ff[1][3], ff[1][2]), send0)
    backs += [swap(other_grad, "blk", 1), swap(other_out, "blk", 1)]
    f32 = jnp.float32
    grad_normed_two = ff[0][1] + own_grad + (backs[0].astype(f32) + backs[2].astype(f32))
    grad_middle, grad_gain_two = norm_two_back(grad_normed_two)
    grad_middle = grad_middle + cot.astype(f32)
    grad_branch = grad_middle.astype(low_type)
    result = middle + ff[0][0] + ff[1][0] + (backs[1].astype(f32) + backs[3].astype(f32))
    grad_mixed = jnp.einsum(
        "te,de->td", grad_branch, out_all, preferred_element_type=jnp.float32
    ).astype(low_type)
    keep0, came0 = tie((keep0, came0), grad_mixed)
    keep0, send0 = fold(keep0, came0)
    came0 = swap(send0, "blk", far[-1])
    grad_mixed = tie(grad_mixed, send0)

    back_dot = lambda a, b: lax.dot_general(a, b, NT, preferred_element_type=jnp.float32)
    grads = []
    for at in range(block_count):
        add = (grads[-1][3], grads[-1][6]) if at else None
        query, *others = lists(at)
        if at:
            grad_mixed = tie(grad_mixed, grads[-1][0])
        grads.append(attend_backward(flags[at : at + 1], query, *others, totals[at], (grad_mixed, at), add))
        if not at:
            earlier_k = jnp.concatenate([grads[0][2], grads[0][1]], axis=0)
            earlier_v = jnp.concatenate([grads[0][5], grads[0][4]], axis=0)
            sent_back = (back_dot(earlier_k, qkv_all[1]) + back_dot(earlier_v, qkv_all[2])).astype(low_type)
            came_back = lax.ppermute(sent_back, "blk", [(at + 1, at) for at in range(n - 1)])
            keep1, came1 = tie((keep1, came1), grads[0][0])
            keep1, send1 = fold(keep1, came1)
            came1 = swap(send1, "blk", 2)
            keep0, came0 = tie((keep0, came0), send1)
            for mask in far[:-1][::-1]:
                keep0, send0 = fold(keep0, came0)
                came0 = swap(send0, "blk", mask)
            grad_mixed = tie(grad_mixed, send1, sent_back)
    keep0, came0, keep1, came1 = tie((keep0, came0, keep1, came1), grads[-1][0], came_back)
    for mask in far[::-1]:
        keep1, send1 = fold(keep1, came1)
        came1 = swap(send1, "blk", mask)
    sum0 = sum_over_win(add_low(keep0, came0), 2)
    later = range(1, block_count)
    q_grads = jnp.concatenate([part[0] for part in grads], axis=0)
    keep2, send2 = weight_grad(place, [mixed_low, normed_low], [grad_branch, q_grads])
    came2 = swap(send2, "blk", 1)
    kv_grads = [
        jnp.concatenate(
            [grads[at][own - 1] for at in later] + [grads[last][own].astype(low_type), grads[0][own - 1]]
            + [grads[at][own - 2] for at in range(block_count)], axis=0)
        for own in (3, 6)
    ]
    token_count = block_count * BLOCK
    context_count = last * CTX
    first_context = token_count + BLOCK + CTX
    own_contexts = back_dot(kv_grads[0][first_context:], qkv_all[1]) + back_dot(kv_grads[1][first_context:], qkv_all[2])
    grad_contexts = jnp.concatenate([own_contexts, came_back[BLOCK:].astype(jnp.float32)], axis=0)
    grad_contexts = grad_contexts.reshape(block_count, CTX, width)
    sums = adjoint_sums(grad_contexts, decay)
    local_starts = jnp.exp(-rate * (BEFORE + 1)) * ssm_all[2] * sums
    _, _, leaving_own = adjoint_behind(nothing, markers, local_starts, over_block)
    leaving, hooks = carried_in(through, leaving_own, True)
    both_rows = jnp.concatenate([normed_low, came_normed, came_ctx, contexts_low[:context_count]], axis=0)
    kv_left = tie(both_rows, leaving_own)
    keep3, send3 = weight_grad(place, [kv_left], kv_grads)
    came3 = swap(send3, "blk", 1)
    whole2 = add_low(keep2, tie(came2, kv_left))
    keep2 = jnp.where(side == 1, whole2[:, rows:], whole2[:, :rows])
    send2 = jnp.where(side == 1, whole2[:, :rows], whole2[:, rows:])
    came2 = swap(send2, "win", 1)
    keep3, send3 = fold(keep3, tie(came3, hooks[1]))
    came3 = swap(send3, "blk", 2)
    leaving = tie(leaving, send2, send3)
    enters, starts, _ = adjoint_behind(leaving, markers, local_starts, over_block)
    grad_carried = markers[:, None, None] * starts
    at_context = beta * middles + jnp.exp(-rate * BEFORE) * begins
    grad_normed_ssm, grad_mix, grad_beta, grad_decay, passed = back_states(
        normed, grad_contexts, at_context, enters, rate, decay, beta, ssm_all[2]
    )
    keep2, send2 = fold(keep2, tie(came2, grad_normed_ssm))
    came2 = swap(send2, "blk", 2)
    grad_normed = (
        back_dot(tie(q_grads, send2), qkv_all[0])
        + back_dot(kv_grads[0][:token_count], qkv_all[1])
        + back_dot(kv_grads[1][:token_count], qkv_all[2])
    )
    keep3, send3 = fold(keep3, tie(came3, grad_normed))
    came3 = swap(send3, "blk", far[-1])
    grad_normed = tie(grad_normed, send3)
    grad_normed = grad_normed.at[-BLOCK:].add(came_back[:BLOCK].astype(jnp.float32))
    grad_beta = grad_beta + jnp.sum(passed * middles, axis=0)
    grad_decay = grad_decay + jnp.sum(
        passed * (BEFORE * jnp.exp(-rate * (BEFORE - 1)) * begins + beta * slopes), axis=0
    )
    grad_rate = grad_beta * ssm_all[1] * jnp.exp(-2.0 * rate) / root - decay * grad_decay
    grad_ssm = jnp.stack([grad_rate * rate, grad_beta * root, grad_mix])
    grad_inputs, grad_gain_one = norm_back(grad_normed + grad_normed_ssm)
    grad_tokens = grad_inputs + grad_middle
    sum_small = reduce_columns(
        jnp.concatenate([grad_gain_one[None], grad_gain_two[None], grad_ssm.reshape(-1, width)], axis=0)
    )
    sum_gain, sum_ssm = sum_small[:2], sum_small[2:].reshape(ssm_w.shape)

    for mask in far[:-1][::-1]:
        keep3, send3 = fold(keep3, came3)
        came3 = swap(send3, "blk", mask)
    for mask in far[::-1]:
        keep2, send2 = fold(keep2, came2)
        came2 = swap(send2, "blk", mask)
    sum3 = sum_over_win(add_low(keep3, came3), 1)[0].astype(f32)
    sum2 = sum_over_win(add_low(keep2, came2), 2)[0]
    sum2 = both_sides(side, sum2, swap(sum2, "win", 1)).reshape(-1, width).astype(f32)
    sum1 = sum_over_win(add_low(keep1, came1), 2)
    sum0, sum1 = tie((sum0, sum1), grad_normed)
    mine_ff = jnp.stack([sum0, sum1])
    ups, downs = both_sides(side, mine_ff, swap(mine_ff, "win", 1))
    chunk_at = upper_core.astype(jnp.int32)
    own_down = jnp.where(upper_core, downs[1], downs[0])
    other_down = jnp.where(upper_core, downs[0], downs[1])
    came_ff = swap(jnp.concatenate([ups[:, 1], other_down], axis=0), "blk", 1)
    up_halves = both_sides(chunk_at, ups[:, 0], came_ff[:2])
    down_halves = both_sides(chunk_at, own_down, came_ff[2:])
    columns = lambda v: v.reshape(v.shape[:-2] + (-1, rows, 128)).swapaxes(-3, -2).reshape(v.shape[:-2] + (rows, width))
    sum_up = columns(up_halves).reshape(2, 2, rows, n // 2, span).transpose(2, 3, 1, 0, 4).reshape(rows, FF).astype(f32)
    sum_down = columns(down_halves).reshape(-1, width).astype(f32)
    sum_out = sum2[:rows]
    sum_qkv = jnp.concatenate([sum2[rows:], sum3], axis=0).reshape(3, rows, width)
    qkv_first, qkv_second, qkv_new = adamw_step(
        qkv_w, qkv_m, qkv_v, sum_qkv, 2.0 * D ** (-0.5), 0.1
    )
    out_first, out_second, out_new = adamw_step(out_w, out_m, out_v, sum_out, 1.0, 0.1)
    up_first, up_second, up_new = adamw_step(up_w, up_m, up_v, sum_up, 2.0 * D ** (-0.5), 0.1)
    down_first, down_second, down_new = adamw_step(
        down_w, down_m, down_v, sum_down, 2.0 * FF ** (-0.5), 0.1
    )
    gain_first, gain_second, gain_new = adamw_step(gain_w, gain_m, gain_v, sum_gain, 1.0, 0.0)
    ssm_first, ssm_second, ssm_new = adamw_step(ssm_w, ssm_m, ssm_v, sum_ssm, 4.0, 0.0)
    return (
        result.astype(low_type)[None],
        grad_tokens[None],
        grad_carried[None],
        qkv_first,
        qkv_second,
        qkv_new,
        out_first,
        out_second,
        out_new,
        up_first,
        up_second,
        up_new,
        down_first,
        down_second,
        down_new,
        gain_first,
        gain_second,
        gain_new,
        ssm_first,
        ssm_second[1:],
        ssm_second[0],
        ssm_new,
    )


def solution(mesh):
    in_specs = (
        P("win", "blk", None),
        P("win", "blk", None),
        P("win", "blk", None, None),
        P("win", "blk"),
        P(None, "blk", None),
        P(None, "blk", None),
        P(None, "blk", None),
        P("blk", None),
        P("blk", None),
        P("blk", None),
        P("blk", None),
        P("blk", None),
        P("blk", None),
        P("blk", None),
        P("blk", None),
        P("blk", None),
        P(None, "blk"),
        P(None, "blk"),
        P(None, "blk"),
        P(None, None, "blk"),
        P(None, None, "blk"),
        P(None, None, "blk"),
    )
    out_specs = (
        P("win", "blk", None),
        P("win", "blk", None),
        P("win", "blk", None, None),
        P(None, "blk", None),
        P(None, "blk", None),
        P(None, "blk", None),
        P("blk", None),
        P("blk", None),
        P("blk", None),
        P("blk", None),
        P("blk", None),
        P("blk", None),
        P("blk", None),
        P("blk", None),
        P("blk", None),
        P(None, "blk"),
        P(None, "blk"),
        P(None, "blk"),
        P(None, None, "blk"),
        P(None, None, "blk"),
        P(None, "blk"),
        P(None, None, "blk"),
    )
    return jax.shard_map(body, mesh=mesh, in_specs=in_specs, out_specs=out_specs, check_vma=False)
```

```python
import functools

import jax
import jax.numpy as jnp
from jax import lax
from jax.experimental import pallas as pl
from jax.experimental.pallas import tpu as pltpu
from jax.sharding import PartitionSpec as P

D = 1024
FF = 4096
HEADS = 8
HEAD_DIM = 128
CTX = 128
BLOCK = 512
STEP = 10
CHUNKS = 2
TILES = 2
TILE = 256
BEFORE = BLOCK - CTX
LANES = 512
VMEM_LIMIT = 60 * 1024 * 1024
LOG2E = 1.4426950408889634
GC = 0.79788456
GQ = 0.044715
LIGHT = pl.CostEstimate(flops=1000, bytes_accessed=1000, transcendentals=0)
NT = (((1,), (1,)), ((), ()))
TN = (((0,), (0,)), ((), ()))

def swap(value, axis, mask):
    count = lax.axis_size(axis)
    return lax.ppermute(value, axis, [(at, at ^ mask) for at in range(count)])


def tie(value, *after):
    return lax.optimization_barrier((value, after))[0]


def far_masks(n):
    masks = [1 << at for at in range(2, n.bit_length() - 1)][::-1]
    if len(masks) >= 2:
        masks[0] |= masks[1]
    return masks


def shift_of(position, masks):
    total = 0
    for at, mask in enumerate(masks):
        if position >> at & 1:
            total ^= mask
    return total


def places(masks):
    mine = lax.axis_index("blk")
    return jnp.stack([mine ^ shift_of(position, masks) for position in range(1 << len(masks))]).astype(jnp.int32)


def widen(held, mask, *after):
    return jnp.concatenate([held, swap(tie(held, *after), "blk", mask)], axis=0)


def add_low(a, b):
    return (a.astype(jnp.float32) + b.astype(jnp.float32)).astype(jnp.bfloat16)


def fold(keep, came):
    half = keep.shape[0] // 2
    return add_low(keep[:half], came[:half]), add_low(keep[half:], came[half:])


def sum_over_win(value, mask):
    while mask < lax.axis_size("win"):
        value = add_low(value, swap(value, "win", mask))
        mask *= 2
    return value


def both_sides(side, mine, other):
    return jnp.stack([jnp.where(side == 1, other, mine), jnp.where(side == 1, mine, other)])


def gather_round(value, mask):
    came = swap(value, "blk", mask)
    upper = (lax.axis_index("blk") & mask) != 0
    return jnp.stack([jnp.where(upper, came, value), jnp.where(upper, value, came)])


def joined_columns(value):
    bits = value.ndim - 2
    value = value.transpose((bits,) + tuple(range(bits))[::-1] + (bits + 1,))
    return value.reshape(value.shape[0], -1)


def reduce_round(value, mask):
    half = value.shape[-1] // 2
    upper = (lax.axis_index("blk") & mask) != 0
    low, high = value[:, :half], value[:, half:]
    return jnp.where(upper, high, low) + swap(jnp.where(upper, low, high), "blk", mask)


def carried_in(through, value, backward):
    mine = lax.axis_index("blk")

    def compose(earlier, later):
        return jnp.stack([earlier[0] * later[0], later[0] * earlier[1] + later[1]])

    total = jnp.stack([through, value])
    ahead = jnp.stack([jnp.ones_like(through), jnp.zeros_like(value)])
    mask = 1
    hooks = []
    while mask < lax.axis_size("blk"):
        other = swap(total, "blk", mask)
        before = ((mine & mask) != 0) != backward
        ahead = jnp.where(before, compose(other, ahead), ahead)
        total = jnp.where(before, compose(other, total), compose(total, other))
        hooks.append(total)
        mask *= 2
    return ahead[1], hooks


def layer_norm(values, gain):
    centered = values - jnp.mean(values, axis=-1, keepdims=True)
    variance = jnp.mean(centered * centered, axis=-1, keepdims=True)
    return centered * lax.rsqrt(variance + 1e-05) * gain


def lane_spec(shape, lanes):
    lead = len(shape) - 1
    return pl.BlockSpec(tuple(shape[:-1]) + (lanes,), lambda i: (0,) * lead + (i,))

def lane_call(kernel, name, inputs, outputs, scratch, lanes):
    width = inputs[0].shape[-1]
    return pl.pallas_call(
        kernel,
        grid=(width // lanes,),
        in_specs=[lane_spec(v.shape, lanes) for v in inputs],
        out_specs=[lane_spec(s, lanes) for s, _ in outputs],
        out_shape=[jax.ShapeDtypeStruct(s, t) for s, t in outputs],
        scratch_shapes=scratch,
        compiler_params=pltpu.CompilerParams(vmem_limit_bytes=VMEM_LIMIT),
        cost_estimate=LIGHT,
        name=name,
    )(*inputs)

def scan_kernel(x_ref, a_ref, mix_ref, ctx_ref, mid_ref, slope_ref, end_ref):
    blocks = ctx_ref.shape[0]
    a = a_ref[...]
    mix = mix_ref[...]
    zero = jnp.zeros_like(a)
    def before(group, state):
        state = list(state)
        for j in range(blocks):
            u, d = state[j]
            first = pl.multiple_of(j * BLOCK + group * 8, 8)
            rows = x_ref[pl.ds(first, 8), :]
            for k in range(8):
                d = a * d + u
                u = a * u + rows[k:k + 1, :]
            state[j] = (u, d)
        return tuple(state)
    state = lax.fori_loop(0, BEFORE // 8, before, tuple((zero, zero) for _ in range(blocks)))
    for j in range(blocks):
        mid_ref[j] = state[j][0]
        slope_ref[j] = state[j][1]
    def inside(group, state):
        state = list(state)
        for j in range(blocks):
            u = state[j]
            first = pl.multiple_of(j * BLOCK + BEFORE + group * 8, 8)
            rows = x_ref[pl.ds(first, 8), :]
            made = []
            for k in range(8):
                u = a * u + rows[k:k + 1, :]
                made.append(jnp.sum(mix * u, axis=0, keepdims=True))
            ctx_ref[j, pl.ds(pl.multiple_of(group * 8, 8), 8), :] = jnp.concatenate(made, axis=0)
            state[j] = u
        return tuple(state)
    state = lax.fori_loop(0, CTX // 8, inside, tuple(s[0] for s in state))
    for j in range(blocks):
        end_ref[j] = state[j]

def scan_states(x, a, mix):
    width = x.shape[-1]
    blocks = x.shape[0] // BLOCK
    states = ((blocks,) + a.shape, jnp.float32)
    return lane_call(scan_kernel, "scan_states", [x, a, mix], [((blocks, CTX, width), jnp.float32), states, states, states], [], 512)

def fan(rate, weight, lag, rows, store):
    count = rate.shape[0]
    for c in range(rate.shape[1] // 128):
        lanes = slice(c * 128, (c + 1) * 128)
        row = lax.broadcasted_iota(jnp.int32, (8, 128), 0).astype(jnp.float32)
        values = tuple(weight[s:s + 1, lanes] * jnp.exp(-rate[s:s + 1, lanes] * (lag(row))) for s in range(count))
        steps = [jnp.broadcast_to(jnp.exp(-8.0 * rate[s:s + 1, lanes]), (8, 128)) for s in range(count)]
        def group_of(group, values):
            total = values[0]
            for v in values[1:]:
                total = total + v
            store(group, lanes, total)
            return tuple(v * s for v, s in zip(values, steps))
        lax.fori_loop(0, rows // 8, group_of, values)

def context_kernel(base_ref, rate_ref, weight_ref, out_ref):
    for j in range(base_ref.shape[0]):
        def store(group, lanes, total, j=j):
            rows = pl.ds(pl.multiple_of(group * 8, 8), 8)
            out_ref[j, rows, lanes] = (base_ref[j, rows, lanes] + total).astype(out_ref.dtype)
        fan(rate_ref[...], weight_ref[j], lambda row: row + (BEFORE + 1.0), CTX, store)

def finish_contexts(base, rate, weight):
    return lane_call(context_kernel, "finish_contexts", [base, rate, weight], [(base.shape, jnp.bfloat16)], [], 512)[0]

def adjoint_kernel(g_ref, a_ref, out_ref):
    blocks = g_ref.shape[0]
    a = a_ref[...]
    def step(group, state):
        state = list(state)
        for j in range(blocks):
            first = pl.multiple_of(CTX - 8 - group * 8, 8)
            rows = g_ref[j, pl.ds(first, 8), :]
            for k in range(7, -1, -1):
                state[j] = a * state[j] + rows[k:k + 1, :]
        return tuple(state)
    state = lax.fori_loop(0, CTX // 8, step, tuple(jnp.zeros_like(a) for _ in range(blocks)))
    for j in range(blocks):
        out_ref[j] = state[j]

def adjoint_sums(g, a):
    return lane_call(adjoint_kernel, "adjoint_sums", [g, a], [((g.shape[0],) + a.shape, jnp.float32)], [], 512)[0]

def back_kernel(x_ref, g_ref, mid_ref, enter_ref, rate_ref, a_ref, beta_ref, mix_ref, gx_ref, gmix_ref, gbeta_ref, ga_ref, leave_ref, held):
    blocks = g_ref.shape[0]
    a = a_ref[...]
    beta = beta_ref[...]
    mix = mix_ref[...]
    zero = jnp.zeros_like(a)

    def ahead(group, states):
        states = list(states)
        for j in range(blocks):
            rows = x_ref[pl.ds(pl.multiple_of(j * BLOCK + BEFORE + group * 8, 8), 8), :]
            for k in range(8):
                held[j, group * 8 + k] = states[j]
                states[j] = a * states[j] + beta * rows[k:k + 1, :]
        return tuple(states)

    lasts = lax.fori_loop(0, CTX // 8, ahead, tuple(mid_ref[j] for j in range(blocks)))

    def back(at, state):
        carries, curs, gmix, gbeta, ga = state
        carries, curs = list(carries), list(curs)
        group = CTX // 8 - 1 - at
        first = pl.multiple_of(group * 8, 8)
        for j in range(blocks):
            here = pl.ds(pl.multiple_of(j * BLOCK + BEFORE + group * 8, 8), 8)
            xs = x_ref[here, :]
            gs = g_ref[j, pl.ds(first, 8), :]
            made = [None] * 8
            for k in range(7, -1, -1):
                g = gs[k:k + 1, :]
                lam = carries[j] + mix * g
                prev = held[j, group * 8 + k]
                gmix = gmix + g * curs[j]
                gbeta = gbeta + lam * xs[k:k + 1, :]
                ga = ga + lam * prev
                made[k] = jnp.sum(beta * lam, axis=0, keepdims=True)
                carries[j] = a * lam
                curs[j] = prev
            gx_ref[here, :] = jnp.concatenate(made, axis=0)
        return tuple(carries), tuple(curs), gmix, gbeta, ga

    carries, _, gmix, gbeta, ga = lax.fori_loop(
        0, CTX // 8, back, (tuple(enter_ref[j] for j in range(blocks)), lasts, zero, zero, zero))
    gmix_ref[...] = gmix
    gbeta_ref[...] = gbeta
    ga_ref[...] = ga
    for j in range(blocks):
        leave_ref[j] = carries[j]

        def store(group, lanes, total, j=j):
            rows = pl.ds(pl.multiple_of(j * BLOCK + BEFORE - 8 - group * 8, 8), 8)
            gx_ref[rows, lanes] = total

        fan(rate_ref[...], beta * carries[j], lambda row: 7.0 - row, BEFORE, store)


def back_states(x, g, mid, enter, rate, a, beta, mix):
    states = (a.shape, jnp.float32)
    return lane_call(back_kernel, "back_states", [x, g, mid, enter, rate, a, beta, mix],
        [(x.shape, jnp.float32), states, states, states, (mid.shape, jnp.float32)],
        [pltpu.VMEM((g.shape[0], CTX, a.shape[0], 256), jnp.float32)], 256)

def state_ahead(begin, markers, carried, ends, decay):
    begins = []
    for j in range(carried.shape[0]):
        begin = jnp.where(markers[j] > 0, carried[j], begin)
        begins.append(begin)
        begin = decay * begin + ends[j]
    return jnp.stack(begins), begin

def adjoint_behind(enter, markers, locals_, decay):
    enters, starts = [], []
    for j in range(locals_.shape[0])[::-1]:
        enters.append(enter)
        start = decay * enter + locals_[j]
        starts.append(start)
        enter = jnp.where(markers[j] > 0, 0.0, start)
    return jnp.stack(enters[::-1]), jnp.stack(starts[::-1]), enter


def load_pieces(n, parts, rows, place_ref, refs, skip, target, sems):
    lists = [[] for _ in range(parts)]
    count = n // len(refs)
    for position in range(n):
        src = refs[position // count].at[position % count]
        first = pl.multiple_of(place_ref[position] * (target.shape[1] // n) + skip, rows)
        for part in range(parts):
            lists[part].append(
                pltpu.make_async_copy(
                    src.at[pl.ds(part * rows, rows)],
                    target.at[part, pl.ds(first, rows)],
                    sems.at[part * n + position],
                )
            )
    return lists


def pack_kernel(n, rows, span, core_ref, up_ref, down_ref, own_ref, other_ref):
    def write(core, ref):
        for chunk in range(2):
            for chip in range(n // 2):
                first = ((2 * chip + chunk) * 2 + core) * span
                ref[chunk * rows : (chunk + 1) * rows, chip * span : (chip + 1) * span] = up_ref[
                    :, first : first + span
                ].astype(ref.dtype)
        ref[2 * rows :, :] = down_ref[core * span : (core + 1) * span, :].astype(ref.dtype)

    for core in range(2):
        @pl.when(core_ref[0] == core)
        def _(core=core):
            write(core, own_ref)
            write(1 - core, other_ref)


def pack_halves(upper_core, up, down, n):
    rows, width = up.shape[0], down.shape[1]
    span = down.shape[0] // 2
    shape = jax.ShapeDtypeStruct((2 * rows + span, width), jnp.bfloat16)
    return pl.pallas_call(
        functools.partial(pack_kernel, n, rows, span),
        in_specs=[pl.BlockSpec(memory_space=pltpu.SMEM)] + [pl.BlockSpec(memory_space=pltpu.VMEM)] * 2,
        out_specs=[pl.BlockSpec(memory_space=pltpu.VMEM)] * 2,
        out_shape=[shape, shape],
        cost_estimate=LIGHT,
        name="pack_halves",
    )(upper_core.astype(jnp.int32)[None], up, down)


def load_halves(n, rows, place_ref, refs, skip, target, sems):
    count = n // len(refs)
    half = rows // 2
    lists = [[], []]
    for position in range(n):
        src = refs[position // count].at[position % count]
        rows_at = pl.ds(pl.multiple_of(place_ref[position] * rows + skip, half), half)
        lists[0].append(pltpu.make_async_copy(src.at[0], target.at[0, rows_at], sems.at[position]))
        rest = pl.ds(1, 2)
        lists[1].append(pltpu.make_async_copy(src.at[rest], target.at[rest, rows_at], sems.at[n + position]))
    return lists


def project_kernel(n, rows, sizes, place_ref, x_ref, *refs):
    parts = 3
    extras, refs = refs[: len(sizes)], refs[len(sizes) :]
    mine, theirs = refs[:4], refs[4:8]
    out_ref, extra_ref, weights_ref, held, extra_v, load_sems, store_sem = refs[8:]
    at = pl.program_id(0)
    store = pltpu.make_async_copy(held, weights_ref, store_sem.at[0])
    lists = load_halves(n, rows, place_ref, mine, place_ref[n], held, load_sems.at[pl.ds(0, 2 * n)])
    more = load_halves(n, rows, place_ref, theirs, place_ref[n + 1], held, load_sems.at[pl.ds(2 * n, 2 * n)])
    lists = [a + b for a, b in zip(lists, more)]
    first = 0
    for i, (ref, size) in enumerate(zip(extras, sizes)):
        lists[1].append(pltpu.make_async_copy(ref, extra_v.at[pl.ds(first, size)], load_sems.at[4 * n + i]))
        first += size

    @pl.when(at == 0)
    def _():
        for copy in lists[0] + lists[1]:
            copy.start()
        for copy in lists[0]:
            copy.wait()

    @pl.when(at == 1)
    def _():
        for copy in lists[1]:
            copy.wait()
        store.start()

    out_ref[0] = jnp.dot(x_ref[...], held[at], preferred_element_type=jnp.float32).astype(out_ref.dtype)

    @pl.when(at > 0)
    def _():
        extra_ref[0] = jnp.dot(extra_v[...], held[at], preferred_element_type=jnp.float32).astype(extra_ref.dtype)

    @pl.when(at == parts - 1)
    def _():
        store.wait()


def project(place, x, extras, mine, theirs):
    n = place.shape[0] - 2
    tokens, width = x.shape
    rows = width // n
    parts = 3
    sizes = [v.shape[0] for v in extras]
    anywhere = pl.BlockSpec(memory_space=pl.ANY)
    shape = lambda *dims: jax.ShapeDtypeStruct(dims, jnp.bfloat16)
    return pl.pallas_call(
        functools.partial(project_kernel, n, rows, sizes),
        grid_spec=pltpu.PrefetchScalarGridSpec(
            num_scalar_prefetch=1,
            grid=(parts,),
            in_specs=[pl.BlockSpec((tokens, width), lambda i, *_: (0, 0))] + [anywhere] * (8 + len(sizes)),
            out_specs=[
                pl.BlockSpec((1, tokens, width), lambda i, *_: (i, 0, 0)),
                pl.BlockSpec((1, sum(sizes), width), lambda i, *_: (jnp.maximum(i - 1, 0), 0, 0)),
                anywhere,
            ],
            scratch_shapes=[
                pltpu.VMEM((parts, width, width), jnp.bfloat16),
                pltpu.VMEM((sum(sizes), width), jnp.bfloat16),
                pltpu.SemaphoreType.DMA((4 * n + len(sizes),)),
                pltpu.SemaphoreType.DMA((1,)),
            ],
        ),
        out_shape=[shape(parts, tokens, width), shape(parts - 1, sum(sizes), width), shape(parts, width, width)],
        compiler_params=pltpu.CompilerParams(vmem_limit_bytes=VMEM_LIMIT),
        cost_estimate=LIGHT,
        name="project",
    )(place, x, *extras, *mine, *theirs)


def branch_kernel(n, rows, place_ref, x_ref, mixed_ref, gain_ref, *refs):
    middle_ref, normed_ref, weights_ref, held, load_sems, store_sem = refs[4:]
    at = pl.program_id(0)
    copies = load_pieces(n, 1, rows, place_ref, refs[:4], 0, held, load_sems)[0]
    store = pltpu.make_async_copy(held.at[0], weights_ref, store_sem.at[0])

    @pl.when(at == 0)
    def _():
        for copy in copies:
            copy.start()
        for copy in copies:
            copy.wait()
        store.start()

    middle = x_ref[...].astype(jnp.float32) + jnp.dot(mixed_ref[...], held[0], preferred_element_type=jnp.float32)
    middle_ref[...] = middle
    normed_ref[...] = layer_norm(middle, gain_ref[...]).astype(normed_ref.dtype)

    @pl.when(at == pl.num_programs(0) - 1)
    def _():
        store.wait()


def branch(place, x, mixed, gain, pieces):
    n = place.shape[0]
    tokens, width = x.shape
    rows = width // n
    tile = 256
    anywhere = pl.BlockSpec(memory_space=pl.ANY)
    strip = pl.BlockSpec((tile, width), lambda i, *_: (i, 0))
    return pl.pallas_call(
        functools.partial(branch_kernel, n, rows),
        grid_spec=pltpu.PrefetchScalarGridSpec(
            num_scalar_prefetch=1,
            grid=(tokens // tile,),
            in_specs=[strip, strip, pl.BlockSpec((1, width), lambda i, *_: (0, 0))] + [anywhere] * 4,
            out_specs=[strip, strip, anywhere],
            scratch_shapes=[
                pltpu.VMEM((1, width, width), jnp.bfloat16),
                pltpu.SemaphoreType.DMA((n,)),
                pltpu.SemaphoreType.DMA((1,)),
            ],
        ),
        out_shape=[
            jax.ShapeDtypeStruct((tokens, width), jnp.float32),
            jax.ShapeDtypeStruct((tokens, width), jnp.bfloat16),
            jax.ShapeDtypeStruct((width, width), jnp.bfloat16),
        ],
        compiler_params=pltpu.CompilerParams(vmem_limit_bytes=VMEM_LIMIT),
        cost_estimate=LIGHT,
        name="branch",
    )(place, x, mixed, gain, *pieces)


def weight_grad_kernel(n, rows, lefts, rights, place_ref, *refs):
    count = sum(map(len, lefts)) + sum(map(len, rights))
    sources = list(refs[:count])
    keep_ref, send_ref, x_v, g_v, turned, held, sems = refs[count:]
    at = pl.program_id(0)
    loads = []
    for sizes, target in [(s, x_v.at[i]) for i, s in enumerate(lefts)] + [(s, g_v.at[i]) for i, s in enumerate(rights)]:
        first, copies = 0, []
        for size in sizes:
            src = sources.pop(0).at[pl.ds(0, size)]
            copies.append(pltpu.make_async_copy(src, target.at[pl.ds(first, size)], sems.at[count - len(sources) - 1]))
            first += size
        loads.append(copies)

    @pl.when(at == 0)
    def _():
        for copies in loads:
            for copy in copies:
                copy.start()

    for i in range(len(rights)):
        @pl.when(at == i)
        def _(i=i):
            if i < len(lefts):
                for copy in loads[i]:
                    copy.wait()
                turned[...] = x_v[i].T
            for copy in loads[len(lefts) + i]:
                copy.wait()

    held[...] = jnp.dot(turned[...], g_v[at], preferred_element_type=jnp.float32).astype(held.dtype)
    for position in range(n):
        first = pl.multiple_of(place_ref[position] * rows, rows)
        target = keep_ref if position < n // 2 else send_ref
        target[position % (n // 2)] = held[pl.ds(first, rows), :]


def weight_grad(place, x, g):
    n = place.shape[0]
    width = g[0][0].shape[1]
    parts = len(g)
    rows = width // n
    rights = [[v.shape[0] for v in part] for part in g]
    lefts = [[v.shape[0] for v in part] for part in x]
    tokens = sum(rights[0])
    for sizes in lefts:
        sizes[-1] -= sum(sizes) - tokens
    half = pl.BlockSpec((n // 2, rows, width), lambda i, *_: (0, i, 0))
    anywhere = pl.BlockSpec(memory_space=pl.ANY)
    operands = [v for part in x + g for v in part]
    return pl.pallas_call(
        functools.partial(weight_grad_kernel, n, rows, lefts, rights),
        grid_spec=pltpu.PrefetchScalarGridSpec(
            num_scalar_prefetch=1,
            grid=(parts,),
            in_specs=[anywhere] * len(operands),
            out_specs=[half, half],
            scratch_shapes=[
                pltpu.VMEM((len(x), tokens, width), jnp.bfloat16),
                pltpu.VMEM((parts, tokens, width), jnp.bfloat16),
                pltpu.VMEM((width, tokens), jnp.bfloat16),
                pltpu.VMEM((width, width), jnp.bfloat16),
                pltpu.SemaphoreType.DMA((len(operands),)),
            ],
        ),
        out_shape=[jax.ShapeDtypeStruct((n // 2, parts * rows, width), jnp.bfloat16)] * 2,
        compiler_params=pltpu.CompilerParams(vmem_limit_bytes=VMEM_LIMIT),
        cost_estimate=LIGHT,
        name="weight_grad",
    )(place, *operands)


def norm_back(values, gain, grad):
    centered = values - jnp.mean(values, axis=-1, keepdims=True)
    scale = lax.rsqrt(jnp.mean(centered * centered, axis=-1, keepdims=True) + 1e-05)
    unit = centered * scale
    inner = grad * gain
    back = scale * (
        inner - jnp.mean(inner, axis=-1, keepdims=True) - unit * jnp.mean(inner * unit, axis=-1, keepdims=True)
    )
    return back, grad * unit


def middle_back_kernel(middle_ref, own0, own1, came0, came1, cot_ref, gain_ref, weights_ref, grad_ref, low_ref, mixed_ref, gain_out):
    f32, bf = jnp.float32, jnp.bfloat16
    grad = own0[...] + own1[...] + (came0[...].astype(f32) + came1[...].astype(f32))
    back, by_gain = norm_back(middle_ref[...], gain_ref[...], grad)
    back = back + cot_ref[...].astype(f32)
    low = back.astype(bf)
    grad_ref[...] = back
    low_ref[...] = low
    mixed_ref[...] = lax.dot_general(low, weights_ref[...], NT, preferred_element_type=f32).astype(bf)

    @pl.when(pl.program_id(0) == 0)
    def _():
        gain_out[...] = jnp.zeros_like(gain_out)

    gain_out[...] += jnp.sum(by_gain, axis=0, keepdims=True)


def middle_back(middle, own, came, cot, gain, weights):
    tokens, width = middle.shape
    tile = 256
    strip = pl.BlockSpec((tile, width), lambda i: (i, 0))
    line = pl.BlockSpec((1, width), lambda i: (0, 0))
    shape = lambda rows, kind: jax.ShapeDtypeStruct((rows, width), kind)
    return pl.pallas_call(
        middle_back_kernel,
        grid=(tokens // tile,),
        in_specs=[strip] * 6 + [line, pl.BlockSpec((width, width), lambda i: (0, 0))],
        out_specs=[strip, strip, strip, line],
        out_shape=[shape(tokens, jnp.float32), shape(tokens, jnp.bfloat16), shape(tokens, jnp.bfloat16), shape(1, jnp.float32)],
        compiler_params=pltpu.CompilerParams(vmem_limit_bytes=VMEM_LIMIT),
        cost_estimate=LIGHT,
        name="middle_back",
    )(middle, *own, *came, cot, gain, weights)


def input_back_kernel(counts, tile, came_tiles, x_ref, ssm_ref, middle_ref, came_ref, gain_ref, *refs):
    total = sum(map(len, counts))
    sources = list(refs[:total])
    weights_ref, grad_ref, gain_out, g_v, weights_v, sems = refs[total:]
    at = pl.program_id(0)
    f32 = jnp.float32

    @pl.when(at == 0)
    def _():
        copies = [pltpu.make_async_copy(weights_ref, weights_v, sems.at[total])]
        left = list(sources)
        for i, sizes in enumerate(counts):
            first = 0
            for size in sizes:
                copies.append(pltpu.make_async_copy(left.pop(0), g_v.at[i, pl.ds(first, size)], sems.at[total - len(left) - 1]))
                first += size
        for copy in copies:
            copy.start()
        gain_out[...] = jnp.zeros_like(gain_out)
        for copy in copies:
            copy.wait()

    rows = pl.ds(pl.multiple_of(at * tile, tile), tile)
    grad = ssm_ref[...]
    for i in range(len(counts)):
        grad += lax.dot_general(g_v[i, rows, :], weights_v[i], NT, preferred_element_type=f32)
    grad += jnp.where(at >= pl.num_programs(0) - came_tiles, 1.0, 0.0) * came_ref[...].astype(f32)
    back, by_gain = norm_back(x_ref[...].astype(f32), gain_ref[...], grad)
    grad_ref[...] = back + middle_ref[...]
    gain_out[...] += jnp.sum(by_gain, axis=0, keepdims=True)


def input_back(x, ssm, middle, came, gain, g, weights):
    tokens, width = x.shape
    tile = 256
    counts = [[v.shape[0] for v in part] for part in g]
    tiles = tokens // tile
    came_tiles = BLOCK // tile
    operands = [v for part in g for v in part]
    strip = pl.BlockSpec((tile, width), lambda i: (i, 0))
    line = pl.BlockSpec((1, width), lambda i: (0, 0))
    anywhere = pl.BlockSpec(memory_space=pl.ANY)
    came_strip = pl.BlockSpec((tile, width), lambda i: (jnp.maximum(i - (tiles - came_tiles), 0), 0))
    return pl.pallas_call(
        functools.partial(input_back_kernel, counts, tile, came_tiles),
        grid=(tiles,),
        in_specs=[strip, strip, strip, came_strip, line] + [anywhere] * (len(operands) + 1),
        out_specs=[strip, line],
        out_shape=[jax.ShapeDtypeStruct((tokens, width), jnp.float32), jax.ShapeDtypeStruct((1, width), jnp.float32)],
        scratch_shapes=[
            pltpu.VMEM((len(g), tokens, width), jnp.bfloat16),
            pltpu.VMEM(weights.shape, jnp.bfloat16),
            pltpu.SemaphoreType.DMA((len(operands) + 1,)),
        ],
        compiler_params=pltpu.CompilerParams(vmem_limit_bytes=VMEM_LIMIT),
        cost_estimate=LIGHT,
        name="input_back",
    )(x, ssm, middle, came, gain, *operands, weights)


def ff_kernel(n, tiles, table_ref, n2_ref, n2s_ref, cot_ref, cots_ref, *rest):
    (mine_low, mine_high, theirs_low, theirs_high, out_ref, gn2_ref, outs_ref, gn2s_ref, mine_ref, theirs_ref,
     n2_v, n2t_v, cot_v, weights_v, out_v, gn2_v, low_v, pack_v, sems, load_sems, store_sems) = rest
    f32, bf = jnp.float32, jnp.bfloat16
    t = pl.program_id(0)
    hidden = width = n2_ref.shape[1]
    rows, span = width // n, hidden // tiles
    half_rows = pack_v.shape[1] // 2
    side = table_ref[2 * n]
    kinds = (side, 1 - side)

    def pieces(refs, which):
        copies = []
        for position in range(n):
            src = refs[position // (n // 2)]
            skip = src.shape[1] - 2 * rows
            src = src.at[position % (n // 2) // 2, pl.ds(skip + position % 2 * rows, rows)]
            first = pl.multiple_of(table_ref[kinds[which] * n + position] * rows, rows)
            copies.append(pltpu.make_async_copy(
                src, weights_v.at[kinds[which], pl.ds(first, rows)], load_sems.at[which * n + position]))
        return copies

    @pl.when(t == 0)
    def _():
        weights = pieces((mine_low, mine_high), 0) + pieces((theirs_low, theirs_high), 1)
        first = [pltpu.make_async_copy(n2_ref, n2_v.at[0], sems.at[0]), pltpu.make_async_copy(n2s_ref, n2_v.at[1], sems.at[1])]
        second = [pltpu.make_async_copy(cot_ref, cot_v.at[0], sems.at[2]), pltpu.make_async_copy(cots_ref, cot_v.at[1], sems.at[3])]
        for copy in first + weights + second:
            copy.start()
        out_v[...] = jnp.zeros_like(out_v)
        gn2_v[...] = jnp.zeros_like(gn2_v)
        for copy in first:
            copy.wait()
        for at in range(2):
            n2t_v[at] = n2_v[at].T
        for copy in weights + second:
            copy.wait()

    cols = pl.ds(pl.multiple_of(t * span, span), span)
    up = weights_v[0, :, cols]
    down = weights_v[1, cols, :]
    gup = gdown = 0.0
    for at in range(2):
        cot = cot_v[at]
        hid = jnp.dot(n2_v[at], up, preferred_element_type=f32)
        gact = lax.dot_general(cot, down, NT, preferred_element_type=f32)
        sq = hid * hid
        th = jnp.tanh(GC * hid * (1.0 + GQ * sq))
        half = 0.5 * (1.0 + th)
        act = (hid * half).astype(bf)
        slope = half + (0.5 * GC) * hid * (1.0 - th * th) * (1.0 + (3.0 * GQ) * sq)
        gh = (gact * slope).astype(bf)
        out_v[at] += jnp.dot(act, down, preferred_element_type=f32)
        gn2_v[at] += lax.dot_general(gh, up, NT, preferred_element_type=f32)
        gdown += lax.dot_general(act, cot, TN, preferred_element_type=f32)
        gup += jnp.dot(n2t_v[at], gh, preferred_element_type=f32)
    gup = gup.astype(bf)
    gdown = gdown.astype(bf)
    groups = span // 128
    for d in range(n):
        for g in range(groups):
            first = pl.multiple_of((t * groups + g) * rows, rows)
            pack_v[d, pl.ds(first, rows), :] = gup[d * rows : (d + 1) * rows, g * 128 : (g + 1) * 128]
    slots = span // rows
    for o in range(slots):
        for g in range(width // 128):
            first = half_rows + g * rows
            pack_v[t * slots + o, first : first + rows, :] = gdown[o * rows : (o + 1) * rows, g * 128 : (g + 1) * 128]

    @pl.when(t == tiles - 1)
    def _():
        copies = []
        for which, ref in enumerate((mine_ref, theirs_ref)):
            for position in range(n):
                slot = table_ref[kinds[which] * n + position]
                src = pack_v.at[slot, pl.ds(pl.multiple_of(kinds[which] * half_rows, half_rows), half_rows)]
                copies.append(pltpu.make_async_copy(src, ref.at[position], store_sems.at[which * n + position]))
        copies.append(pltpu.make_async_copy(out_v.at[0], out_ref, sems.at[0]))
        copies.append(pltpu.make_async_copy(gn2_v.at[0], gn2_ref, sems.at[1]))
        for copy in copies:
            copy.start()
        low_v[0] = gn2_v[1].astype(bf)
        low_v[1] = out_v[1].astype(bf)
        for at, ref in enumerate((gn2s_ref, outs_ref)):
            copy = pltpu.make_async_copy(low_v.at[at], ref, sems.at[2 + at])
            copy.start()
            copies.append(copy)
        for copy in copies:
            copy.wait()


def feed_forward(table, n2, n2_other, cot, cot_other, mine, theirs, tiles):
    n = (table.shape[0] - 1) // 2
    tokens, width = n2.shape
    rows = width // n
    half_rows = width // 128 * rows
    bf, f32 = jnp.bfloat16, jnp.float32
    anywhere = pl.BlockSpec(memory_space=pl.ANY)
    shape = jax.ShapeDtypeStruct
    return pl.pallas_call(
        functools.partial(ff_kernel, n, tiles),
        grid_spec=pltpu.PrefetchScalarGridSpec(
            num_scalar_prefetch=1,
            grid=(tiles,),
            in_specs=[anywhere] * 8,
            out_specs=[anywhere] * 6,
            scratch_shapes=[
                pltpu.VMEM((2, tokens, width), bf),
                pltpu.VMEM((2, width, tokens), bf),
                pltpu.VMEM((2, tokens, width), bf),
                pltpu.VMEM((2, width, width), bf),
                pltpu.VMEM((2, tokens, width), f32),
                pltpu.VMEM((2, tokens, width), f32),
                pltpu.VMEM((2, tokens, width), bf),
                pltpu.VMEM((n, 2 * half_rows, 128), bf),
                pltpu.SemaphoreType.DMA((4,)),
                pltpu.SemaphoreType.DMA((2 * n,)),
                pltpu.SemaphoreType.DMA((2 * n,)),
            ],
        ),
        out_shape=[shape((tokens, width), f32)] * 2 + [shape((tokens, width), bf)] * 2 + [shape((n, half_rows, 128), bf)] * 2,
        compiler_params=pltpu.CompilerParams(vmem_limit_bytes=VMEM_LIMIT),
        cost_estimate=pl.CostEstimate(flops=24 * tokens * width * width, bytes_accessed=32 << 20, transcendentals=2 * tokens * width),
        name="feed_forward",
    )(table, n2, n2_other, cot, cot_other, *mine, *theirs)


def causal(rows, cols, first):
    r = lax.broadcasted_iota(jnp.int32, (rows, cols), 0) + first
    c = lax.broadcasted_iota(jnp.int32, (rows, cols), 1)
    return c <= r

def attend_forward_kernel(flag_ref, q_ref, kc_ref, kp_ref, ko_ref, vc_ref, vp_ref, vo_ref, mixed_ref, total_ref):
    scale = HEAD_DIM ** -0.5
    f32 = jnp.float32
    def tile(at, earlier):
        rows = pl.ds(at * TILE, TILE)
        own = (at + 1) * TILE
        q = q_ref[rows, :]
        so = lax.dot_general(q, ko_ref[:own, :], NT, preferred_element_type=f32)
        so = jnp.where(causal(TILE, own, at * TILE), so, -1e30)
        parts = [so]
        values = [vo_ref[:own, :]]
        if earlier:
            parts = [lax.dot_general(q, kc_ref[...], NT, preferred_element_type=f32), lax.dot_general(q, kp_ref[...], NT, preferred_element_type=f32)] + parts
            values = [vc_ref[...], vp_ref[...]] + values
        top = functools.reduce(jnp.maximum, [jnp.max(s, axis=-1, keepdims=True) for s in parts])
        shift = top * (scale * LOG2E)
        soft = [jnp.exp2(s * (scale * LOG2E) - shift) for s in parts]
        total = sum(jnp.sum(s, axis=-1, keepdims=True) for s in soft)
        mixed = sum(jnp.dot(s.astype(jnp.bfloat16), v, preferred_element_type=f32) for s, v in zip(soft, values))
        mixed_ref[rows, :] = (mixed * (1.0 / total)).astype(mixed_ref.dtype)
        total_ref[0, rows, :] = shift + jnp.log2(total)
    flagged = flag_ref[0] > 0
    for at in range(BLOCK // TILE):
        pl.when(flagged)(functools.partial(tile, at, False))
        pl.when(jnp.logical_not(flagged))(functools.partial(tile, at, True))

def head_spec(rows, row_at=0, lead=None):
    if lead is None:
        return pl.BlockSpec((rows, HEAD_DIM), lambda h, *_: (row_at, h))
    return pl.BlockSpec((None, rows, HEAD_DIM), lambda h, *_: (lead, row_at, h))

def attend_forward(flag, query, key_ctx, key_prev, key_own, value_ctx, value_prev, value_own):
    ops=[query,key_ctx,key_prev,key_own,value_ctx,value_prev,value_own]
    sizes=[BLOCK,CTX,BLOCK,BLOCK,CTX,BLOCK,BLOCK]
    return pl.pallas_call(
        attend_forward_kernel,
        grid_spec=pltpu.PrefetchScalarGridSpec(num_scalar_prefetch=1, grid=(HEADS,),
            in_specs=[head_spec(s, o[1], o[2] if len(o) > 2 else None) for o, s in zip(ops, sizes)],
            out_specs=[head_spec(BLOCK), pl.BlockSpec((1, BLOCK, 1), lambda h, *_: (h, 0, 0))]),
        out_shape=[jax.ShapeDtypeStruct((BLOCK, HEADS * HEAD_DIM), jnp.bfloat16), jax.ShapeDtypeStruct((HEADS, BLOCK, 1), jnp.float32)],
        compiler_params=pltpu.CompilerParams(vmem_limit_bytes=VMEM_LIMIT),
        cost_estimate=LIGHT,
        name="attend_forward",
    )(flag, *[o[0] for o in ops])

def attend_backward_kernel(merge, flag_ref, q_ref, kc_ref, kp_ref, ko_ref, vc_ref, vp_ref, vo_ref, total_ref, g_ref, *rest):
    scale = HEAD_DIM ** -0.5
    f32, bf = jnp.float32, jnp.bfloat16
    if merge:
        kadd_ref, vadd_ref, dq_ref, dkc_ref, dkp_ref, dko_ref, dvc_ref, dvp_ref, dvo_ref, acc_k, acc_v = rest
    else:
        dq_ref, dkc_ref, dkp_ref, dko_ref, dvc_ref, dvp_ref, dvo_ref, acc_k, acc_v = rest
    lead = CTX + BLOCK
    acc_k[...] = jnp.zeros_like(acc_k)
    acc_v[...] = jnp.zeros_like(acc_v)
    def tile(at, earlier):
        rows = pl.ds(at * TILE, TILE)
        own = (at + 1) * TILE
        q = q_ref[rows, :]
        g = g_ref[rows, :]
        total = total_ref[0, rows, :]
        keys = [(ko_ref[:own, :], vo_ref[:own, :], lead, own)]
        if earlier:
            keys = [(kc_ref[...], vc_ref[...], 0, CTX), (kp_ref[...], vp_ref[...], CTX, BLOCK)] + keys
        softs, grads = [], []
        for k, v, first, size in keys:
            s = lax.dot_general(q, k, NT, preferred_element_type=f32)
            s = s * (scale * LOG2E) - total
            if first == lead:
                s = jnp.where(causal(TILE, own, at * TILE), s, -1e30)
            softs.append(jnp.exp2(s))
            grads.append(lax.dot_general(g, v, NT, preferred_element_type=f32))
        products = [p * d for p, d in zip(softs, grads)]
        rowsum = sum(jnp.sum(x, axis=-1, keepdims=True) for x in products)
        dq = 0.0
        for (k, v, first, size), p, x in zip(keys, softs, products):
            ds = (x - p * rowsum).astype(bf)
            dq += jnp.dot(ds, k, preferred_element_type=f32)
            at_rows = pl.ds(first, size)
            acc_k[at_rows, :] += lax.dot_general(ds, q, TN, preferred_element_type=f32)
            acc_v[at_rows, :] += lax.dot_general(p.astype(bf), g, TN, preferred_element_type=f32)
        dq_ref[rows, :] = (dq * scale).astype(dq_ref.dtype)
    flagged = flag_ref[0] > 0
    for at in range(BLOCK // TILE):
        pl.when(flagged)(functools.partial(tile, at, False))
        pl.when(jnp.logical_not(flagged))(functools.partial(tile, at, True))
    more_k = kadd_ref[...] if merge else 0.0
    more_v = vadd_ref[...] if merge else 0.0
    dkc_ref[...] = (acc_k[:CTX, :] * scale).astype(dkc_ref.dtype)
    dvc_ref[...] = acc_v[:CTX, :].astype(dvc_ref.dtype)
    dkp_ref[...] = (acc_k[CTX:lead, :] * scale + more_k).astype(dkp_ref.dtype)
    dvp_ref[...] = (acc_v[CTX:lead, :] + more_v).astype(dvp_ref.dtype)
    dko_ref[...] = (acc_k[lead:, :] * scale).astype(dko_ref.dtype)
    dvo_ref[...] = acc_v[lead:, :].astype(dvo_ref.dtype)

def attend_backward(flag, query, key_ctx, key_prev, key_own, value_ctx, value_prev, value_own, total, grad, add=None, final=False):
    ops=[query,key_ctx,key_prev,key_own,value_ctx,value_prev,value_own]
    sizes=[BLOCK,CTX,BLOCK,BLOCK,CTX,BLOCK,BLOCK]
    specs=[head_spec(s, o[1], o[2] if len(o) > 2 else None) for o, s in zip(ops, sizes)]
    specs+=[pl.BlockSpec((1, BLOCK, 1), lambda h, *_: (h, 0, 0)), head_spec(BLOCK, grad[1])]
    args=[o[0] for o in ops]+[total, grad[0]]
    if add is not None:
        specs+=[head_spec(BLOCK)]*2
        args+=list(add)
    width=HEADS*HEAD_DIM
    bf,f32=jnp.bfloat16,jnp.float32
    own = bf if final else f32
    out=lambda r,t: jax.ShapeDtypeStruct((r,width),t)
    return pl.pallas_call(
        functools.partial(attend_backward_kernel, add is not None),
        grid_spec=pltpu.PrefetchScalarGridSpec(num_scalar_prefetch=1, grid=(HEADS,),
            in_specs=specs,
            out_specs=[head_spec(BLOCK), head_spec(CTX), head_spec(BLOCK), head_spec(BLOCK), head_spec(CTX), head_spec(BLOCK), head_spec(BLOCK)],
            scratch_shapes=[pltpu.VMEM((CTX+2*BLOCK,HEAD_DIM),f32)]*2),
        out_shape=[out(BLOCK,bf), out(CTX,bf), out(BLOCK,bf), out(BLOCK,own), out(CTX,bf), out(BLOCK,bf), out(BLOCK,own)],
        compiler_params=pltpu.CompilerParams(vmem_limit_bytes=VMEM_LIMIT),
        cost_estimate=LIGHT,
        name="attend_backward",
    )(flag, *args)


def adamw_step(weight, first, second, gradient, step_rate, shrink):
    new_first = 0.9 * first + 0.1 * gradient
    new_second = 0.95 * second + 0.05 * gradient * gradient
    scaled_first = new_first / (1.0 - 0.9**STEP)
    scaled_second = new_second / (1.0 - 0.95**STEP)
    update = scaled_first / (jnp.sqrt(scaled_second) + 1e-08) + shrink * weight
    return (new_first, new_second, weight - step_rate * update)


def body(
    tokens,
    cotangent,
    carry_in,
    block_flags,
    qkv_w,
    qkv_m,
    qkv_v,
    out_w,
    out_m,
    out_v,
    up_w,
    up_m,
    up_v,
    down_w,
    down_m,
    down_v,
    gain_w,
    gain_m,
    gain_v,
    ssm_w,
    ssm_m,
    ssm_v,
):
    low_type = jnp.bfloat16
    n = lax.axis_size("blk")
    width = tokens.shape[-1]
    rows = width // n
    span = FF // n // 2
    far = far_masks(n)
    place = places(far + [2, 1])
    ff_place = places([1] + far + [2])
    side = lax.axis_index("win") & 1
    slots = 2 * (ff_place // 2) + jnp.arange(n, dtype=jnp.int32) % 2
    ff_table = jnp.concatenate([ff_place, slots, side[None].astype(jnp.int32)])
    upper_core = (lax.axis_index("blk") & 1) != 0


    small = jnp.concatenate([gain_w, ssm_w.reshape(-1, ssm_w.shape[-1])], axis=0)
    small = gather_round(small, n // 2)
    qkv_half = qkv_w.astype(low_type).reshape(3, 2, rows // 2, width)
    held = jnp.where(side == 1, qkv_half[:, 1], qkv_half[:, 0])[None]
    for mask in far[:-1]:
        held = widen(held, mask)
    mask = n // 4
    while mask > 2:
        small = gather_round(small, mask)
        mask //= 2
    own_half, other_half = pack_halves(upper_core, *tie((up_w, down_w), small), n)
    small = gather_round(tie(small, held), 2)
    small = gather_round(small, 1)
    small = joined_columns(small)
    near = widen(held, far[-1])
    across = swap(near, "blk", 2)
    near_y = swap(near, "win", 1)
    near_c = swap(near, "blk", 1)

    gain_all, ssm_all = small[:2], small[2:].reshape(ssm_w.shape[:2] + (width,))
    inputs = tokens[0].astype(jnp.float32)
    flags = block_flags[0]
    markers = flags.astype(jnp.float32)
    carried = carry_in[0]
    block_count = markers.shape[0]
    last = block_count - 1
    forward_pairs = [(at, at + 1) for at in range(n - 1)]
    normed = layer_norm(inputs, gain_all[0])
    normed_low = normed.astype(low_type)
    rate = jnp.exp(ssm_all[0])
    decay = jnp.exp(-rate)
    root = jnp.sqrt(-jnp.expm1(-2.0 * rate))
    beta = root * ssm_all[1]
    over_block = jnp.exp(-rate * BLOCK)
    through = jnp.prod(1.0 - markers) * jnp.exp(-rate * (block_count * BLOCK))
    came_half = swap(other_half, "blk", 1)
    cot = cotangent[0]
    cot_other = swap(cot, "blk", 1)

    def chunk(c):
        ups = [own_half[c * rows : (c + 1) * rows], came_half[c * rows : (c + 1) * rows]]
        is_own = upper_core == (c == 1)
        down = jnp.where(is_own, own_half[2 * rows :], came_half[2 * rows :])
        return jnp.where(side == 1, down, jnp.concatenate(ups, axis=0))

    first = jnp.concatenate([out_w.astype(low_type), chunk(0)], axis=0)[None]
    second = chunk(1)[None]
    first_came = swap(tie(first, near), "blk", far[0])
    base_ctx, middles, slopes, ends = scan_states(tie(normed, near, first), decay, ssm_all[2] * beta)
    nothing = jnp.zeros_like(rate)
    _, local_end = state_ahead(nothing, markers, carried, beta * tie(ends, first_came, near_y), over_block)
    across = tie(across, ends)
    across_y = swap(across, "win", 1)
    across_c = swap(across, "blk", 1)
    near_yc = swap(near_y, "blk", 1)
    entering, hooks = carried_in(through, tie(local_end, across), False)
    first = jnp.concatenate([first, tie(first_came, entering)], axis=0)
    for mask in far[1:-1]:
        first = widen(first, mask)
    sent = tie(normed_low[-BLOCK:], hooks[1])
    came_normed = lax.ppermute(sent, "blk", forward_pairs)
    begins, _ = state_ahead(tie(entering, across_y, came_normed), markers, carried, beta * ends, over_block)
    contexts_low = finish_contexts(base_ctx, rate, ssm_all[2] * begins).reshape(-1, width)
    came_ctx = lax.ppermute(contexts_low[-CTX:], "blk", forward_pairs)
    across_yc = swap(tie(across_y, contexts_low), "blk", 1)
    first = tie(first, came_ctx)
    first_came = swap(first, "blk", far[-1])
    second = tie(second, first)
    second_came = swap(second, "blk", far[0])
    table = jnp.concatenate([place, jnp.stack([side, 1 - side]).astype(jnp.int32) * (rows // 2)])
    projected, extra_pair, qkv_all = project(
        table,
        tie(normed_low, contexts_low, first),
        [came_normed, contexts_low, came_ctx],
        [near, across, near_c, across_c],
        [near_y, across_y, near_yc, across_yc],
    )
    first_came = tie(first_came, projected)
    first = jnp.concatenate([first, first_came], axis=0)

    first_x = swap(first, "blk", 2)
    out_near_c = swap(first[:, :rows], "blk", 1)
    near_half = first[:, rows:]
    theirs0 = [swap(near_half, "win", 1)]
    context_rows = BLOCK // CTX

    def lists(at):
        own = [(projected, at, 1), (projected, at, 2)]
        ctx_at = context_rows + (at - 1 if at else block_count)
        if at:
            earlier = [(extra_pair, ctx_at, 0), (projected, at - 1, 1), (extra_pair, ctx_at, 1), (projected, at - 1, 2)]
        else:
            earlier = [(extra_pair, ctx_at, 0), (extra_pair, 0, 0), (extra_pair, ctx_at, 1), (extra_pair, 0, 1)]
        return [(projected, at, 0), earlier[0], earlier[1], own[0], earlier[2], earlier[3], own[1]]

    attended = {}
    place_flags = tie(flags, first, near_half)
    for at in range(block_count)[::-1]:
        attended[at] = attend_forward(place_flags[at : at + 1], *lists(at))
        if at == last:
            second = jnp.concatenate([second, tie(second_came, attended[at][0])], axis=0)
            for mask in far[1:-1]:
                second = widen(second, mask)
            second_came = swap(second, "blk", far[-1])
            place_flags = tie(flags, second)
    mixed_low = jnp.concatenate([attended[at][0] for at in range(block_count)], axis=0)
    totals = [attended[at][1] for at in range(block_count)]
    first_x = tie(first_x, mixed_low)
    out_across_c = swap(first_x[:, :rows], "blk", 1)
    theirs0.append(swap(first_x[:, rows:], "win", 1))
    second = jnp.concatenate([second, tie(second_came, mixed_low)], axis=0)
    second_x = swap(second, "blk", 2)
    theirs1 = [swap(tie(second, theirs0[1]), "win", 1)]
    middle, normed_two_low, out_all = branch(
        place, tokens[0], tie(mixed_low, second, theirs0[0]), gain_all[1:], [first, first_x, out_near_c, out_across_c]
    )
    normed_two_low = tie(normed_two_low, theirs0[1], second_x)
    n2_other = swap(normed_two_low, "blk", 1)
    theirs1.append(swap(second_x, "win", 1))
    ff = [feed_forward(ff_table, normed_two_low, n2_other, cot, cot_other, [first, first_x], theirs0, TILES)]
    keep0, send0 = ff[0][4:]
    came0 = swap(send0, "win", 1)
    backs = [swap(ff[0][3], "blk", 1), swap(ff[0][2], "blk", 1)]
    ff.append(feed_forward(ff_table, tie(normed_two_low, send0, ff[0][3]), n2_other, cot, cot_other, [second, second_x], theirs1, TILES))
    keep1, send1 = ff[1][4:]
    came1 = swap(tie(send1, came0), "win", 1)
    keep0, came0 = tie((keep0, came0), keep1)
    keep0, send0 = fold(keep0, came0)
    came0 = swap(send0, "blk", 2)
    own_grad, other_grad, other_out = tie((ff[1][1], ff[1][3], ff[1][2]), send0)
    backs += [swap(other_grad, "blk", 1), swap(other_out, "blk", 1)]
    f32 = jnp.float32
    grad_middle, grad_branch, grad_mixed, grad_gain_two = middle_back(
        middle, [ff[0][1], own_grad], [backs[0], backs[2]], cot, gain_all[1:], out_all
    )
    back_dot = lambda a, b: lax.dot_general(a, b, NT, preferred_element_type=jnp.float32)
    grads = []
    for at in range(block_count):
        add = (grads[-1][3], grads[-1][6]) if at else None
        query, *others = lists(at)
        if at:
            grad_mixed = tie(grad_mixed, grads[-1][0])
        grads.append(attend_backward(flags[at : at + 1], query, *others, totals[at], (grad_mixed, at), add, at == last))
        if not at:
            earlier_k = jnp.concatenate([grads[0][2], grads[0][1]], axis=0)
            earlier_v = jnp.concatenate([grads[0][5], grads[0][4]], axis=0)
            sent_back = (back_dot(earlier_k, qkv_all[1]) + back_dot(earlier_v, qkv_all[2])).astype(low_type)
            came_back = lax.ppermute(sent_back, "blk", [(at + 1, at) for at in range(n - 1)])
            keep1, came1 = tie((keep1, came1), grads[0][0])
            keep1, send1 = fold(keep1, came1)
            came1 = swap(send1, "blk", 2)
            keep0, came0 = tie((keep0, came0), send1)
            for mask in far[1:][::-1]:
                keep0, send0 = fold(keep0, came0)
                came0 = swap(send0, "blk", mask)
            grad_mixed = tie(grad_mixed, send0, send1, sent_back)
    later = range(1, block_count)
    own_contexts = jnp.concatenate(
        [back_dot(grads[at][1], qkv_all[1]) + back_dot(grads[at][4], qkv_all[2]) for at in later], axis=0
    )
    grad_contexts = jnp.concatenate([own_contexts, came_back[BLOCK:].astype(f32)], axis=0).reshape(block_count, CTX, width)
    sums = adjoint_sums(grad_contexts, decay)
    local_starts = jnp.exp(-rate * (BEFORE + 1)) * ssm_all[2] * sums
    _, _, leaving_own = adjoint_behind(nothing, markers, local_starts, over_block)
    leaving, hooks = carried_in(through, leaving_own, True)
    q_grads = [part[0] for part in grads]
    kv_grads = [
        [grads[at][own - 1] for at in later] + [grads[last][own], grads[0][own - 1]]
        + [grads[at][own - 2] for at in range(block_count)]
        for own in (3, 6)
    ]
    keep0, came0, keep1, came1 = tie((keep0, came0, keep1, came1), sums)
    for mask in far[:1]:
        keep0, send0 = fold(keep0, came0)
        came0 = swap(send0, "blk", mask)
    keep1, send1 = fold(keep1, came1)
    came1 = swap(tie(send1, send0), "blk", far[-1])
    keep2, send2 = weight_grad(place, [[tie(mixed_low, hooks[0], send0, send1)], [normed_low]], [[grad_branch], q_grads])
    came2 = swap(send2, "blk", 1)
    keep1, came1, came0 = tie((keep1, came1, came0), keep2)
    sum0 = sum_over_win(add_low(keep0, came0), 2)
    for mask in far[:-1][::-1]:
        keep1, send1 = fold(keep1, came1)
        came1 = swap(send1, "blk", mask)
    kv_left = tie(normed_low, hooks[1], send1, send2, sum0)
    keep3, send3 = weight_grad(place, [[kv_left, came_normed, came_ctx, contexts_low]], kv_grads)
    came3 = swap(send3, "blk", 1)
    whole2 = add_low(keep2, tie(came2, keep3, hooks[2]))
    keep2 = jnp.where(side == 1, whole2[:, rows:], whole2[:, :rows])
    send2 = jnp.where(side == 1, whole2[:, :rows], whole2[:, rows:])
    came2 = swap(send2, "win", 1)
    keep3, send3 = fold(keep3, tie(came3, send2))
    came3 = swap(send3, "blk", 2)
    leaving = tie(leaving, send2, send3)
    enters, starts, _ = adjoint_behind(leaving, markers, local_starts, over_block)
    grad_carried = markers[:, None, None] * starts
    at_context = beta * middles + jnp.exp(-rate * BEFORE) * begins
    grad_normed_ssm, grad_mix, grad_beta, grad_decay, passed = back_states(
        normed, grad_contexts, at_context, enters, rate, decay, beta, ssm_all[2]
    )
    came1, came2, came3, grad_normed_ssm = tie((came1, came2, came3, grad_normed_ssm))
    keep2, send2 = fold(keep2, came2)
    came2 = swap(send2, "blk", 2)
    keep3, send3 = fold(keep3, tie(came3, send2))
    came3 = swap(send3, "blk", far[-1])
    sum1 = sum_over_win(add_low(keep1, tie(came1, send3)), 2)
    mine_ff = jnp.stack([sum0, sum1])
    theirs_ff = swap(mine_ff, "win", 1)
    grad_tokens, grad_gain_one = input_back(
        tokens[0],
        tie(grad_normed_ssm, send2, send3, mine_ff),
        grad_middle,
        came_back,
        gain_all[:1],
        [q_grads] + [part[:block_count] for part in kv_grads],
        qkv_all,
    )
    keep2, send2 = fold(keep2, tie(came2, grad_tokens))
    came2 = swap(send2, "blk", far[-1])
    for mask in far[:-1][::-1]:
        keep3, send3 = fold(keep3, tie(came3, send2))
        came3 = swap(send3, "blk", mask)
    grad_gain_one = tie(grad_gain_one, send2, send3)
    grad_beta = grad_beta + jnp.sum(passed * middles, axis=0)
    grad_decay = grad_decay + jnp.sum(
        passed * (BEFORE * jnp.exp(-rate * (BEFORE - 1)) * begins + beta * slopes), axis=0
    )
    grad_rate = grad_beta * ssm_all[1] * jnp.exp(-2.0 * rate) / root - decay * grad_decay
    grad_ssm = jnp.stack([grad_rate * rate, grad_beta * root, grad_mix])
    result = middle + ff[0][0] + tie(ff[1][0], grad_tokens) + (backs[1].astype(f32) + backs[3].astype(f32))
    result = result.astype(low_type)
    sum_small = jnp.concatenate([grad_gain_one, grad_gain_two, grad_ssm.reshape(-1, width)], axis=0)
    mask = n // 2
    while mask > 2:
        sum_small = reduce_round(sum_small, mask)
        mask //= 2
    ups, downs = both_sides(side, mine_ff, tie(theirs_ff, sum_small))
    chunk_at = upper_core.astype(jnp.int32)
    own_down = jnp.where(upper_core, downs[1], downs[0])
    other_down = jnp.where(upper_core, downs[0], downs[1])
    sent_ff = jnp.concatenate([ups[:, 1], other_down], axis=0)
    came_ff = swap(sent_ff, "blk", 1)
    came2, came3 = tie((came2, came3), sum_small)
    for mask in far[:-1][::-1]:
        keep2, send2 = fold(keep2, came2)
        came2 = swap(send2, "blk", mask)
    mine3 = add_low(keep3, came3)
    sum3 = sum_over_win(mine3, 1)[0].astype(f32)
    sum_small = tie(sum_small, send2, mine3)
    for mask in (2, 1):
        sum_small = reduce_round(sum_small, mask)
    came2 = tie(came2, sum_small)
    mine2 = sum_over_win(add_low(keep2, came2), 2)[0]
    sum2 = both_sides(side, mine2, swap(mine2, "win", 1)).reshape(-1, width).astype(f32)
    sum_small = tie(sum_small, mine2)
    mask = 1
    while mask < lax.axis_size("win"):
        sum_small = sum_small + swap(sum_small, "win", mask)
        mask *= 2
    sum_gain, sum_ssm = sum_small[:2], sum_small[2:].reshape(ssm_w.shape)

    up_halves = both_sides(chunk_at, ups[:, 0], came_ff[:2])
    down_halves = both_sides(chunk_at, own_down, came_ff[2:])
    columns = lambda v: v.reshape(v.shape[:-2] + (-1, rows, 128)).swapaxes(-3, -2).reshape(v.shape[:-2] + (rows, width))
    sum_up = columns(up_halves).reshape(2, 2, rows, n // 2, span).transpose(2, 3, 1, 0, 4).reshape(rows, FF).astype(f32)
    sum_down = columns(down_halves).reshape(-1, width).astype(f32)
    sum_out = sum2[:rows]
    sum_qkv = jnp.concatenate([sum2[rows:], sum3], axis=0).reshape(3, rows, width)
    qkv_first, qkv_second, qkv_new = adamw_step(
        qkv_w, qkv_m, qkv_v, sum_qkv, 2.0 * D ** (-0.5), 0.1
    )
    out_first, out_second, out_new = adamw_step(out_w, out_m, out_v, sum_out, 1.0, 0.1)
    up_first, up_second, up_new = adamw_step(up_w, up_m, up_v, sum_up, 2.0 * D ** (-0.5), 0.1)
    down_first, down_second, down_new = adamw_step(
        down_w, down_m, down_v, sum_down, 2.0 * FF ** (-0.5), 0.1
    )
    gain_first, gain_second, gain_new = adamw_step(gain_w, gain_m, gain_v, sum_gain, 1.0, 0.0)
    ssm_first, ssm_second, ssm_new = adamw_step(ssm_w, ssm_m, ssm_v, sum_ssm, 4.0, 0.0)
    return (
        result[None],
        grad_tokens[None],
        grad_carried[None],
        qkv_first,
        qkv_second,
        qkv_new,
        out_first,
        out_second,
        out_new,
        up_first,
        up_second,
        up_new,
        down_first,
        down_second,
        down_new,
        gain_first,
        gain_second,
        gain_new,
        ssm_first,
        ssm_second[1:],
        ssm_second[0],
        ssm_new,
    )


def solution(mesh):
    in_specs = (
        P("win", "blk", None),
        P("win", "blk", None),
        P("win", "blk", None, None),
        P("win", "blk"),
        P(None, "blk", None),
        P(None, "blk", None),
        P(None, "blk", None),
        P("blk", None),
        P("blk", None),
        P("blk", None),
        P("blk", None),
        P("blk", None),
        P("blk", None),
        P("blk", None),
        P("blk", None),
        P("blk", None),
        P(None, "blk"),
        P(None, "blk"),
        P(None, "blk"),
        P(None, None, "blk"),
        P(None, None, "blk"),
        P(None, None, "blk"),
    )
    out_specs = (
        P("win", "blk", None),
        P("win", "blk", None),
        P("win", "blk", None, None),
        P(None, "blk", None),
        P(None, "blk", None),
        P(None, "blk", None),
        P("blk", None),
        P("blk", None),
        P("blk", None),
        P("blk", None),
        P("blk", None),
        P("blk", None),
        P("blk", None),
        P("blk", None),
        P("blk", None),
        P(None, "blk"),
        P(None, "blk"),
        P(None, "blk"),
        P(None, None, "blk"),
        P(None, None, "blk"),
        P(None, "blk"),
        P(None, None, "blk"),
    )
    return jax.shard_map(body, mesh=mesh, in_specs=in_specs, out_specs=out_specs, check_vma=False)
```

```python
import functools

import jax
import jax.numpy as jnp
from jax import lax
from jax.experimental import pallas as pl
from jax.experimental.pallas import tpu as pltpu
from jax.sharding import PartitionSpec as P

D = 1024
FF = 4096
HEADS = 8
HEAD_DIM = 128
CTX = 128
BLOCK = 512
STEP = 10
CHUNKS = 2
TILES = 2
TILE = 256
BEFORE = BLOCK - CTX
LANES = 512
VMEM_LIMIT = 60 * 1024 * 1024
LOG2E = 1.4426950408889634
GC = 0.79788456
GQ = 0.044715
LIGHT = pl.CostEstimate(flops=1000, bytes_accessed=1000, transcendentals=0)
NT = (((1,), (1,)), ((), ()))
TN = (((0,), (0,)), ((), ()))

def swap(value, axis, mask):
    count = lax.axis_size(axis)
    return lax.ppermute(value, axis, [(at, at ^ mask) for at in range(count)])


def tie(value, *after):
    return lax.optimization_barrier((value, after))[0]


def far_masks(n):
    masks = [1 << at for at in range(2, n.bit_length() - 1)][::-1]
    if len(masks) >= 2:
        masks[0] |= masks[1]
    return masks


def shift_of(position, masks):
    total = 0
    for at, mask in enumerate(masks):
        if position >> at & 1:
            total ^= mask
    return total


def places(masks):
    mine = lax.axis_index("blk")
    return jnp.stack([mine ^ shift_of(position, masks) for position in range(1 << len(masks))]).astype(jnp.int32)


def widen(held, mask, *after):
    return jnp.concatenate([held, swap(tie(held, *after), "blk", mask)], axis=0)


def add_low(a, b):
    return (a.astype(jnp.float32) + b.astype(jnp.float32)).astype(jnp.bfloat16)


def fold(keep, came):
    half = keep.shape[0] // 2
    return add_low(keep[:half], came[:half]), add_low(keep[half:], came[half:])


def sum_over_win(value, mask):
    while mask < lax.axis_size("win"):
        value = add_low(value, swap(value, "win", mask))
        mask *= 2
    return value


def both_sides(side, mine, other):
    return jnp.stack([jnp.where(side == 1, other, mine), jnp.where(side == 1, mine, other)])


def gather_round(value, mask):
    came = swap(value, "blk", mask)
    upper = (lax.axis_index("blk") & mask) != 0
    return jnp.stack([jnp.where(upper, came, value), jnp.where(upper, value, came)])


def joined_columns(value):
    bits = value.ndim - 2
    value = value.transpose((bits,) + tuple(range(bits))[::-1] + (bits + 1,))
    return value.reshape(value.shape[0], -1)


def reduce_round(value, mask):
    half = value.shape[-1] // 2
    upper = (lax.axis_index("blk") & mask) != 0
    low, high = value[:, :half], value[:, half:]
    return jnp.where(upper, high, low) + swap(jnp.where(upper, low, high), "blk", mask)


class CarriedIn:
    def __init__(self, through, value, backward):
        self.total = jnp.stack([through, value])
        self.ahead = jnp.stack([jnp.ones_like(through), jnp.zeros_like(value)])
        self.backward = backward
        self.mask = 1

    def step(self, *hold):
        compose = lambda earlier, later: jnp.stack([earlier[0] * later[0], later[0] * earlier[1] + later[1]])
        other = tie(swap(self.total, "blk", self.mask), *hold)
        before = ((lax.axis_index("blk") & self.mask) != 0) != self.backward
        self.ahead = jnp.where(before, compose(other, self.ahead), self.ahead)
        self.total = jnp.where(before, compose(other, self.total), compose(self.total, other))
        self.mask *= 2


def layer_norm(values, gain):
    centered = values - jnp.mean(values, axis=-1, keepdims=True)
    variance = jnp.mean(centered * centered, axis=-1, keepdims=True)
    return centered * lax.rsqrt(variance + 1e-05) * gain


def lane_spec(shape, lanes):
    lead = len(shape) - 1
    return pl.BlockSpec(tuple(shape[:-1]) + (lanes,), lambda i: (0,) * lead + (i,))

def lane_call(kernel, name, inputs, outputs, scratch, lanes):
    width = inputs[0].shape[-1]
    return pl.pallas_call(
        kernel,
        grid=(width // lanes,),
        in_specs=[lane_spec(v.shape, lanes) for v in inputs],
        out_specs=[lane_spec(s, lanes) for s, _ in outputs],
        out_shape=[jax.ShapeDtypeStruct(s, t) for s, t in outputs],
        scratch_shapes=scratch,
        compiler_params=pltpu.CompilerParams(vmem_limit_bytes=VMEM_LIMIT),
        cost_estimate=LIGHT,
        name=name,
    )(*inputs)

def scan_kernel(x_ref, a_ref, mix_ref, ctx_ref, mid_ref, slope_ref, end_ref):
    blocks = ctx_ref.shape[0]
    a = a_ref[...]
    mix = mix_ref[...]
    zero = jnp.zeros_like(a)
    def before(group, state):
        state = list(state)
        for j in range(blocks):
            u, d = state[j]
            first = pl.multiple_of(j * BLOCK + group * 8, 8)
            rows = x_ref[pl.ds(first, 8), :]
            for k in range(8):
                d = a * d + u
                u = a * u + rows[k:k + 1, :]
            state[j] = (u, d)
        return tuple(state)
    state = lax.fori_loop(0, BEFORE // 8, before, tuple((zero, zero) for _ in range(blocks)))
    for j in range(blocks):
        mid_ref[j] = state[j][0]
        slope_ref[j] = state[j][1]
    def inside(group, state):
        state = list(state)
        for j in range(blocks):
            u = state[j]
            first = pl.multiple_of(j * BLOCK + BEFORE + group * 8, 8)
            rows = x_ref[pl.ds(first, 8), :]
            made = []
            for k in range(8):
                u = a * u + rows[k:k + 1, :]
                made.append(jnp.sum(mix * u, axis=0, keepdims=True))
            ctx_ref[j, pl.ds(pl.multiple_of(group * 8, 8), 8), :] = jnp.concatenate(made, axis=0)
            state[j] = u
        return tuple(state)
    state = lax.fori_loop(0, CTX // 8, inside, tuple(s[0] for s in state))
    for j in range(blocks):
        end_ref[j] = state[j]

def scan_states(x, a, mix):
    width = x.shape[-1]
    blocks = x.shape[0] // BLOCK
    states = ((blocks,) + a.shape, jnp.float32)
    return lane_call(scan_kernel, "scan_states", [x, a, mix], [((blocks, CTX, width), jnp.float32), states, states, states], [], 512)

def fan(rate, weight, lag, rows, store):
    count = rate.shape[0]
    for c in range(rate.shape[1] // 128):
        lanes = slice(c * 128, (c + 1) * 128)
        row = lax.broadcasted_iota(jnp.int32, (8, 128), 0).astype(jnp.float32)
        values = tuple(weight[s:s + 1, lanes] * jnp.exp(-rate[s:s + 1, lanes] * (lag(row))) for s in range(count))
        steps = [jnp.broadcast_to(jnp.exp(-8.0 * rate[s:s + 1, lanes]), (8, 128)) for s in range(count)]
        def group_of(group, values):
            total = values[0]
            for v in values[1:]:
                total = total + v
            store(group, lanes, total)
            return tuple(v * s for v, s in zip(values, steps))
        lax.fori_loop(0, rows // 8, group_of, values)

def context_kernel(base_ref, rate_ref, weight_ref, out_ref, held):
    for j in range(base_ref.shape[0]):
        def store(group, lanes, total, j=j):
            rows = pl.ds(pl.multiple_of(group * 8, 8), 8)
            held[rows, lanes] = base_ref[j, rows, lanes] + total
        fan(rate_ref[...], weight_ref[j], lambda row: row + (BEFORE + 1.0), CTX, store)
        out_ref[j] = held[...].astype(out_ref.dtype)

def finish_contexts(base, rate, weight):
    return lane_call(context_kernel, "finish_contexts", [base, rate, weight], [(base.shape, jnp.bfloat16)], [pltpu.VMEM((CTX, 512), jnp.float32)], 512)[0]

def adjoint_kernel(g_ref, a_ref, out_ref):
    blocks = g_ref.shape[0]
    a = a_ref[...]
    def step(group, state):
        state = list(state)
        for j in range(blocks):
            first = pl.multiple_of(CTX - 8 - group * 8, 8)
            rows = g_ref[j, pl.ds(first, 8), :]
            for k in range(7, -1, -1):
                state[j] = a * state[j] + rows[k:k + 1, :]
        return tuple(state)
    state = lax.fori_loop(0, CTX // 8, step, tuple(jnp.zeros_like(a) for _ in range(blocks)))
    for j in range(blocks):
        out_ref[j] = state[j]

def adjoint_sums(g, a):
    return lane_call(adjoint_kernel, "adjoint_sums", [g, a], [((g.shape[0],) + a.shape, jnp.float32)], [], 512)[0]

def back_kernel(x_ref, g_ref, mid_ref, enter_ref, rate_ref, a_ref, beta_ref, mix_ref, gx_ref, gmix_ref, gbeta_ref, ga_ref, leave_ref, held):
    blocks = g_ref.shape[0]
    a = a_ref[...]
    beta = beta_ref[...]
    mix = mix_ref[...]
    zero = jnp.zeros_like(a)

    def ahead(group, states):
        states = list(states)
        for j in range(blocks):
            rows = x_ref[pl.ds(pl.multiple_of(j * BLOCK + BEFORE + group * 8, 8), 8), :]
            for k in range(8):
                held[j, group * 8 + k] = states[j]
                states[j] = a * states[j] + beta * rows[k:k + 1, :]
        return tuple(states)

    lasts = lax.fori_loop(0, CTX // 8, ahead, tuple(mid_ref[j] for j in range(blocks)))

    def back(at, state):
        carries, curs, gmix, gbeta, ga = state
        carries, curs = list(carries), list(curs)
        group = CTX // 8 - 1 - at
        first = pl.multiple_of(group * 8, 8)
        for j in range(blocks):
            here = pl.ds(pl.multiple_of(j * BLOCK + BEFORE + group * 8, 8), 8)
            xs = x_ref[here, :]
            gs = g_ref[j, pl.ds(first, 8), :]
            made = [None] * 8
            for k in range(7, -1, -1):
                g = gs[k:k + 1, :]
                lam = carries[j] + mix * g
                prev = held[j, group * 8 + k]
                gmix = gmix + g * curs[j]
                gbeta = gbeta + lam * xs[k:k + 1, :]
                ga = ga + lam * prev
                made[k] = jnp.sum(beta * lam, axis=0, keepdims=True)
                carries[j] = a * lam
                curs[j] = prev
            gx_ref[here, :] = jnp.concatenate(made, axis=0)
        return tuple(carries), tuple(curs), gmix, gbeta, ga

    carries, _, gmix, gbeta, ga = lax.fori_loop(
        0, CTX // 8, back, (tuple(enter_ref[j] for j in range(blocks)), lasts, zero, zero, zero))
    gmix_ref[...] = gmix
    gbeta_ref[...] = gbeta
    ga_ref[...] = ga
    for j in range(blocks):
        leave_ref[j] = carries[j]

        def store(group, lanes, total, j=j):
            rows = pl.ds(pl.multiple_of(j * BLOCK + BEFORE - 8 - group * 8, 8), 8)
            gx_ref[rows, lanes] = total

        fan(rate_ref[...], beta * carries[j], lambda row: 7.0 - row, BEFORE, store)


def back_states(x, g, mid, enter, rate, a, beta, mix):
    states = (a.shape, jnp.float32)
    return lane_call(back_kernel, "back_states", [x, g, mid, enter, rate, a, beta, mix],
        [(x.shape, jnp.float32), states, states, states, (mid.shape, jnp.float32)],
        [pltpu.VMEM((g.shape[0], CTX, a.shape[0], 256), jnp.float32)], 256)

def state_ahead(begin, markers, carried, ends, decay):
    begins = []
    for j in range(carried.shape[0]):
        begin = jnp.where(markers[j] > 0, carried[j], begin)
        begins.append(begin)
        begin = decay * begin + ends[j]
    return jnp.stack(begins), begin

def adjoint_behind(enter, markers, locals_, decay):
    enters, starts = [], []
    for j in range(locals_.shape[0])[::-1]:
        enters.append(enter)
        start = decay * enter + locals_[j]
        starts.append(start)
        enter = jnp.where(markers[j] > 0, 0.0, start)
    return jnp.stack(enters[::-1]), jnp.stack(starts[::-1]), enter


def load_pieces(n, parts, rows, place_ref, refs, skip, target, sems):
    lists = [[] for _ in range(parts)]
    count = n // len(refs)
    for position in range(n):
        src = refs[position // count].at[position % count]
        first = pl.multiple_of(place_ref[position] * (target.shape[1] // n) + skip, rows)
        for part in range(parts):
            lists[part].append(
                pltpu.make_async_copy(
                    src.at[pl.ds(part * rows, rows)],
                    target.at[part, pl.ds(first, rows)],
                    sems.at[part * n + position],
                )
            )
    return lists


def pack_kernel(n, rows, span, core_ref, up_ref, down_ref, own_ref, other_ref):
    def write(core, ref):
        for chunk in range(2):
            for chip in range(n // 2):
                first = ((2 * chip + chunk) * 2 + core) * span
                ref[chunk * rows : (chunk + 1) * rows, chip * span : (chip + 1) * span] = up_ref[
                    :, first : first + span
                ].astype(ref.dtype)
        ref[2 * rows :, :] = down_ref[core * span : (core + 1) * span, :].astype(ref.dtype)

    for core in range(2):
        @pl.when(core_ref[0] == core)
        def _(core=core):
            write(core, own_ref)
            write(1 - core, other_ref)


def pack_halves(upper_core, up, down, n):
    rows, width = up.shape[0], down.shape[1]
    span = down.shape[0] // 2
    shape = jax.ShapeDtypeStruct((2 * rows + span, width), jnp.bfloat16)
    return pl.pallas_call(
        functools.partial(pack_kernel, n, rows, span),
        in_specs=[pl.BlockSpec(memory_space=pltpu.SMEM)] + [pl.BlockSpec(memory_space=pltpu.VMEM)] * 2,
        out_specs=[pl.BlockSpec(memory_space=pltpu.VMEM)] * 2,
        out_shape=[shape, shape],
        cost_estimate=LIGHT,
        name="pack_halves",
    )(upper_core.astype(jnp.int32)[None], up, down)


def load_halves(n, rows, place_ref, refs, skip, target, sems):
    count = n // len(refs)
    half = rows // 2
    lists = [[], []]
    for position in range(n):
        src = refs[position // count].at[position % count]
        rows_at = pl.ds(pl.multiple_of(place_ref[position] * rows + skip, half), half)
        lists[0].append(pltpu.make_async_copy(src.at[0], target.at[0, rows_at], sems.at[position]))
        rest = pl.ds(1, 2)
        lists[1].append(pltpu.make_async_copy(src.at[rest], target.at[rest, rows_at], sems.at[n + position]))
    return lists


def project_kernel(n, rows, sizes, place_ref, x_ref, *refs):
    parts = 3
    extras, refs = refs[: len(sizes)], refs[len(sizes) :]
    mine, theirs = refs[:4], refs[4:8]
    out_ref, extra_ref, weights_ref, held, extra_v, load_sems, store_sem = refs[8:]
    at = pl.program_id(0)
    store = pltpu.make_async_copy(held, weights_ref, store_sem.at[0])
    lists = load_halves(n, rows, place_ref, mine, place_ref[n], held, load_sems.at[pl.ds(0, 2 * n)])
    more = load_halves(n, rows, place_ref, theirs, place_ref[n + 1], held, load_sems.at[pl.ds(2 * n, 2 * n)])
    lists = [a + b for a, b in zip(lists, more)]
    first = 0
    for i, (ref, size) in enumerate(zip(extras, sizes)):
        lists[1].append(pltpu.make_async_copy(ref, extra_v.at[pl.ds(first, size)], load_sems.at[4 * n + i]))
        first += size

    @pl.when(at == 0)
    def _():
        for copy in lists[0] + lists[1]:
            copy.start()
        for copy in lists[0]:
            copy.wait()

    @pl.when(at == 1)
    def _():
        for copy in lists[1]:
            copy.wait()
        store.start()

    out_ref[0] = jnp.dot(x_ref[...], held[at], preferred_element_type=jnp.float32).astype(out_ref.dtype)

    @pl.when(at > 0)
    def _():
        extra_ref[0] = jnp.dot(extra_v[...], held[at], preferred_element_type=jnp.float32).astype(extra_ref.dtype)

    @pl.when(at == parts - 1)
    def _():
        store.wait()


def project(place, x, extras, mine, theirs):
    n = place.shape[0] - 2
    tokens, width = x.shape
    rows = width // n
    parts = 3
    sizes = [v.shape[0] for v in extras]
    anywhere = pl.BlockSpec(memory_space=pl.ANY)
    shape = lambda *dims: jax.ShapeDtypeStruct(dims, jnp.bfloat16)
    return pl.pallas_call(
        functools.partial(project_kernel, n, rows, sizes),
        grid_spec=pltpu.PrefetchScalarGridSpec(
            num_scalar_prefetch=1,
            grid=(parts,),
            in_specs=[pl.BlockSpec((tokens, width), lambda i, *_: (0, 0))] + [anywhere] * (8 + len(sizes)),
            out_specs=[
                pl.BlockSpec((1, tokens, width), lambda i, *_: (i, 0, 0)),
                pl.BlockSpec((1, sum(sizes), width), lambda i, *_: (jnp.maximum(i - 1, 0), 0, 0)),
                anywhere,
            ],
            scratch_shapes=[
                pltpu.VMEM((parts, width, width), jnp.bfloat16),
                pltpu.VMEM((sum(sizes), width), jnp.bfloat16),
                pltpu.SemaphoreType.DMA((4 * n + len(sizes),)),
                pltpu.SemaphoreType.DMA((1,)),
            ],
        ),
        out_shape=[shape(parts, tokens, width), shape(parts - 1, sum(sizes), width), shape(parts, width, width)],
        compiler_params=pltpu.CompilerParams(vmem_limit_bytes=VMEM_LIMIT),
        cost_estimate=LIGHT,
        name="project",
    )(place, x, *extras, *mine, *theirs)


def branch_kernel(n, rows, place_ref, x_ref, mixed_ref, gain_ref, *refs):
    middle_ref, normed_ref, weights_ref, held, load_sems, store_sem = refs[4:]
    at = pl.program_id(0)
    copies = load_pieces(n, 1, rows, place_ref, refs[:4], 0, held, load_sems)[0]
    store = pltpu.make_async_copy(held.at[0], weights_ref, store_sem.at[0])

    @pl.when(at == 0)
    def _():
        for copy in copies:
            copy.start()
        for copy in copies:
            copy.wait()
        store.start()

    middle = x_ref[...].astype(jnp.float32) + jnp.dot(mixed_ref[...], held[0], preferred_element_type=jnp.float32)
    middle_ref[...] = middle
    normed_ref[...] = layer_norm(middle, gain_ref[...]).astype(normed_ref.dtype)

    @pl.when(at == pl.num_programs(0) - 1)
    def _():
        store.wait()


def branch(place, x, mixed, gain, pieces):
    n = place.shape[0]
    tokens, width = x.shape
    rows = width // n
    tile = 256
    anywhere = pl.BlockSpec(memory_space=pl.ANY)
    strip = pl.BlockSpec((tile, width), lambda i, *_: (i, 0))
    return pl.pallas_call(
        functools.partial(branch_kernel, n, rows),
        grid_spec=pltpu.PrefetchScalarGridSpec(
            num_scalar_prefetch=1,
            grid=(tokens // tile,),
            in_specs=[strip, strip, pl.BlockSpec((1, width), lambda i, *_: (0, 0))] + [anywhere] * 4,
            out_specs=[strip, strip, anywhere],
            scratch_shapes=[
                pltpu.VMEM((1, width, width), jnp.bfloat16),
                pltpu.SemaphoreType.DMA((n,)),
                pltpu.SemaphoreType.DMA((1,)),
            ],
        ),
        out_shape=[
            jax.ShapeDtypeStruct((tokens, width), jnp.float32),
            jax.ShapeDtypeStruct((tokens, width), jnp.bfloat16),
            jax.ShapeDtypeStruct((width, width), jnp.bfloat16),
        ],
        compiler_params=pltpu.CompilerParams(vmem_limit_bytes=VMEM_LIMIT),
        cost_estimate=LIGHT,
        name="branch",
    )(place, x, mixed, gain, *pieces)


def weight_grad_kernel(n, rows, lefts, rights, place_ref, *refs):
    count = sum(map(len, lefts)) + sum(map(len, rights))
    sources = list(refs[:count])
    keep_ref, send_ref, x_v, g_v, turned, held, sems = refs[count:]
    at = pl.program_id(0)
    loads = []
    for sizes, target in [(s, x_v.at[i]) for i, s in enumerate(lefts)] + [(s, g_v.at[i]) for i, s in enumerate(rights)]:
        first, copies = 0, []
        for size in sizes:
            src = sources.pop(0).at[pl.ds(0, size)]
            copies.append(pltpu.make_async_copy(src, target.at[pl.ds(first, size)], sems.at[count - len(sources) - 1]))
            first += size
        loads.append(copies)

    @pl.when(at == 0)
    def _():
        for copies in loads:
            for copy in copies:
                copy.start()

    for i in range(len(rights)):
        @pl.when(at == i)
        def _(i=i):
            if i < len(lefts):
                for copy in loads[i]:
                    copy.wait()
                turned[...] = x_v[i].T
            for copy in loads[len(lefts) + i]:
                copy.wait()

    held[...] = jnp.dot(turned[...], g_v[at], preferred_element_type=jnp.float32).astype(held.dtype)
    for position in range(n):
        first = pl.multiple_of(place_ref[position] * rows, rows)
        target = keep_ref if position < n // 2 else send_ref
        target[position % (n // 2)] = held[pl.ds(first, rows), :]


def weight_grad(place, x, g):
    n = place.shape[0]
    width = g[0][0].shape[1]
    parts = len(g)
    rows = width // n
    rights = [[v.shape[0] for v in part] for part in g]
    lefts = [[v.shape[0] for v in part] for part in x]
    tokens = sum(rights[0])
    for sizes in lefts:
        sizes[-1] -= sum(sizes) - tokens
    half = pl.BlockSpec((n // 2, rows, width), lambda i, *_: (0, i, 0))
    anywhere = pl.BlockSpec(memory_space=pl.ANY)
    operands = [v for part in x + g for v in part]
    return pl.pallas_call(
        functools.partial(weight_grad_kernel, n, rows, lefts, rights),
        grid_spec=pltpu.PrefetchScalarGridSpec(
            num_scalar_prefetch=1,
            grid=(parts,),
            in_specs=[anywhere] * len(operands),
            out_specs=[half, half],
            scratch_shapes=[
                pltpu.VMEM((len(x), tokens, width), jnp.bfloat16),
                pltpu.VMEM((parts, tokens, width), jnp.bfloat16),
                pltpu.VMEM((width, tokens), jnp.bfloat16),
                pltpu.VMEM((width, width), jnp.bfloat16),
                pltpu.SemaphoreType.DMA((len(operands),)),
            ],
        ),
        out_shape=[jax.ShapeDtypeStruct((n // 2, parts * rows, width), jnp.bfloat16)] * 2,
        compiler_params=pltpu.CompilerParams(vmem_limit_bytes=VMEM_LIMIT),
        cost_estimate=LIGHT,
        name="weight_grad",
    )(place, *operands)


def norm_back(values, gain, grad):
    centered = values - jnp.mean(values, axis=-1, keepdims=True)
    scale = lax.rsqrt(jnp.mean(centered * centered, axis=-1, keepdims=True) + 1e-05)
    unit = centered * scale
    inner = grad * gain
    back = scale * (
        inner - jnp.mean(inner, axis=-1, keepdims=True) - unit * jnp.mean(inner * unit, axis=-1, keepdims=True)
    )
    return back, grad * unit


def middle_back_kernel(middle_ref, own0, own1, came0, came1, cot_ref, gain_ref, weights_ref, grad_ref, low_ref, mixed_ref, gain_out):
    f32, bf = jnp.float32, jnp.bfloat16
    grad = own0[...] + own1[...] + (came0[...].astype(f32) + came1[...].astype(f32))
    back, by_gain = norm_back(middle_ref[...], gain_ref[...], grad)
    back = back + cot_ref[...].astype(f32)
    low = back.astype(bf)
    grad_ref[...] = back
    low_ref[...] = low
    mixed_ref[...] = lax.dot_general(low, weights_ref[...], NT, preferred_element_type=f32).astype(bf)

    @pl.when(pl.program_id(0) == 0)
    def _():
        gain_out[...] = jnp.zeros_like(gain_out)

    gain_out[...] += jnp.sum(by_gain, axis=0, keepdims=True)


def middle_back(middle, own, came, cot, gain, weights):
    tokens, width = middle.shape
    tile = 256
    strip = pl.BlockSpec((tile, width), lambda i: (i, 0))
    line = pl.BlockSpec((1, width), lambda i: (0, 0))
    shape = lambda rows, kind: jax.ShapeDtypeStruct((rows, width), kind)
    return pl.pallas_call(
        middle_back_kernel,
        grid=(tokens // tile,),
        in_specs=[strip] * 6 + [line, pl.BlockSpec((width, width), lambda i: (0, 0))],
        out_specs=[strip, strip, strip, line],
        out_shape=[shape(tokens, jnp.float32), shape(tokens, jnp.bfloat16), shape(tokens, jnp.bfloat16), shape(1, jnp.float32)],
        compiler_params=pltpu.CompilerParams(vmem_limit_bytes=VMEM_LIMIT),
        cost_estimate=LIGHT,
        name="middle_back",
    )(middle, *own, *came, cot, gain, weights)


def input_back_kernel(counts, tile, came_tiles, x_ref, ssm_ref, middle_ref, came_ref, gain_ref, *refs):
    total = sum(map(len, counts))
    sources = list(refs[:total])
    weights_ref, grad_ref, gain_out, g_v, weights_v, sems = refs[total:]
    at = pl.program_id(0)
    f32 = jnp.float32

    @pl.when(at == 0)
    def _():
        copies = [pltpu.make_async_copy(weights_ref, weights_v, sems.at[total])]
        left = list(sources)
        for i, sizes in enumerate(counts):
            first = 0
            for size in sizes:
                copies.append(pltpu.make_async_copy(left.pop(0), g_v.at[i, pl.ds(first, size)], sems.at[total - len(left) - 1]))
                first += size
        for copy in copies:
            copy.start()
        gain_out[...] = jnp.zeros_like(gain_out)
        for copy in copies:
            copy.wait()

    rows = pl.ds(pl.multiple_of(at * tile, tile), tile)
    grad = ssm_ref[...]
    for i in range(len(counts)):
        grad += lax.dot_general(g_v[i, rows, :], weights_v[i], NT, preferred_element_type=f32)
    grad += jnp.where(at >= pl.num_programs(0) - came_tiles, 1.0, 0.0) * came_ref[...].astype(f32)
    back, by_gain = norm_back(x_ref[...].astype(f32), gain_ref[...], grad)
    grad_ref[...] = back + middle_ref[...]
    gain_out[...] += jnp.sum(by_gain, axis=0, keepdims=True)


def input_back(x, ssm, middle, came, gain, g, weights):
    tokens, width = x.shape
    tile = 256
    counts = [[v.shape[0] for v in part] for part in g]
    tiles = tokens // tile
    came_tiles = BLOCK // tile
    operands = [v for part in g for v in part]
    strip = pl.BlockSpec((tile, width), lambda i: (i, 0))
    line = pl.BlockSpec((1, width), lambda i: (0, 0))
    anywhere = pl.BlockSpec(memory_space=pl.ANY)
    came_strip = pl.BlockSpec((tile, width), lambda i: (jnp.maximum(i - (tiles - came_tiles), 0), 0))
    return pl.pallas_call(
        functools.partial(input_back_kernel, counts, tile, came_tiles),
        grid=(tiles,),
        in_specs=[strip, strip, strip, came_strip, line] + [anywhere] * (len(operands) + 1),
        out_specs=[strip, line],
        out_shape=[jax.ShapeDtypeStruct((tokens, width), jnp.float32), jax.ShapeDtypeStruct((1, width), jnp.float32)],
        scratch_shapes=[
            pltpu.VMEM((len(g), tokens, width), jnp.bfloat16),
            pltpu.VMEM(weights.shape, jnp.bfloat16),
            pltpu.SemaphoreType.DMA((len(operands) + 1,)),
        ],
        compiler_params=pltpu.CompilerParams(vmem_limit_bytes=VMEM_LIMIT),
        cost_estimate=LIGHT,
        name="input_back",
    )(x, ssm, middle, came, gain, *operands, weights)


def ff_kernel(n, tiles, table_ref, n2_ref, n2s_ref, cot_ref, cots_ref, *rest):
    (mine_low, mine_high, theirs_low, theirs_high, out_ref, gn2_ref, outs_ref, gn2s_ref, mine_ref, theirs_ref,
     n2_v, n2t_v, cot_v, weights_v, out_v, gn2_v, low_v, pack_v, sems, load_sems, store_sems) = rest
    f32, bf = jnp.float32, jnp.bfloat16
    t = pl.program_id(0)
    hidden = width = n2_ref.shape[1]
    rows, span = width // n, hidden // tiles
    half_rows = pack_v.shape[1] // 2
    side = table_ref[2 * n]
    kinds = (side, 1 - side)

    def pieces(refs, which):
        copies = []
        for position in range(n):
            src = refs[position // (n // 2)]
            skip = src.shape[1] - 2 * rows
            src = src.at[position % (n // 2) // 2, pl.ds(skip + position % 2 * rows, rows)]
            first = pl.multiple_of(table_ref[kinds[which] * n + position] * rows, rows)
            copies.append(pltpu.make_async_copy(
                src, weights_v.at[kinds[which], pl.ds(first, rows)], load_sems.at[which * n + position]))
        return copies

    @pl.when(t == 0)
    def _():
        weights = pieces((mine_low, mine_high), 0) + pieces((theirs_low, theirs_high), 1)
        first = [pltpu.make_async_copy(n2_ref, n2_v.at[0], sems.at[0]), pltpu.make_async_copy(n2s_ref, n2_v.at[1], sems.at[1])]
        second = [pltpu.make_async_copy(cot_ref, cot_v.at[0], sems.at[2]), pltpu.make_async_copy(cots_ref, cot_v.at[1], sems.at[3])]
        for copy in first + weights + second:
            copy.start()
        out_v[...] = jnp.zeros_like(out_v)
        gn2_v[...] = jnp.zeros_like(gn2_v)
        for copy in first:
            copy.wait()
        for at in range(2):
            n2t_v[at] = n2_v[at].T
        for copy in weights + second:
            copy.wait()

    cols = pl.ds(pl.multiple_of(t * span, span), span)
    up = weights_v[0, :, cols]
    down = weights_v[1, cols, :]
    gup = gdown = 0.0
    for at in range(2):
        cot = cot_v[at]
        hid = jnp.dot(n2_v[at], up, preferred_element_type=f32)
        gact = lax.dot_general(cot, down, NT, preferred_element_type=f32)
        sq = hid * hid
        th = jnp.tanh(GC * hid * (1.0 + GQ * sq))
        half = 0.5 * (1.0 + th)
        act = (hid * half).astype(bf)
        slope = half + (0.5 * GC) * hid * (1.0 - th * th) * (1.0 + (3.0 * GQ) * sq)
        gh = (gact * slope).astype(bf)
        out_v[at] += jnp.dot(act, down, preferred_element_type=f32)
        gn2_v[at] += lax.dot_general(gh, up, NT, preferred_element_type=f32)
        gdown += lax.dot_general(act, cot, TN, preferred_element_type=f32)
        gup += jnp.dot(n2t_v[at], gh, preferred_element_type=f32)
    gup = gup.astype(bf)
    gdown = gdown.astype(bf)
    groups = span // 128
    for d in range(n):
        for g in range(groups):
            first = pl.multiple_of((t * groups + g) * rows, rows)
            pack_v[d, pl.ds(first, rows), :] = gup[d * rows : (d + 1) * rows, g * 128 : (g + 1) * 128]
    slots = span // rows
    for o in range(slots):
        for g in range(width // 128):
            first = half_rows + g * rows
            pack_v[t * slots + o, first : first + rows, :] = gdown[o * rows : (o + 1) * rows, g * 128 : (g + 1) * 128]

    @pl.when(t == tiles - 1)
    def _():
        copies = []
        for which, ref in enumerate((mine_ref, theirs_ref)):
            for position in range(n):
                slot = table_ref[kinds[which] * n + position]
                src = pack_v.at[slot, pl.ds(pl.multiple_of(kinds[which] * half_rows, half_rows), half_rows)]
                copies.append(pltpu.make_async_copy(src, ref.at[position], store_sems.at[which * n + position]))
        copies.append(pltpu.make_async_copy(out_v.at[0], out_ref, sems.at[0]))
        copies.append(pltpu.make_async_copy(gn2_v.at[0], gn2_ref, sems.at[1]))
        for copy in copies:
            copy.start()
        low_v[0] = gn2_v[1].astype(bf)
        low_v[1] = out_v[1].astype(bf)
        for at, ref in enumerate((gn2s_ref, outs_ref)):
            copy = pltpu.make_async_copy(low_v.at[at], ref, sems.at[2 + at])
            copy.start()
            copies.append(copy)
        for copy in copies:
            copy.wait()


def feed_forward(table, n2, n2_other, cot, cot_other, mine, theirs, tiles):
    n = (table.shape[0] - 1) // 2
    tokens, width = n2.shape
    rows = width // n
    half_rows = width // 128 * rows
    bf, f32 = jnp.bfloat16, jnp.float32
    anywhere = pl.BlockSpec(memory_space=pl.ANY)
    shape = jax.ShapeDtypeStruct
    return pl.pallas_call(
        functools.partial(ff_kernel, n, tiles),
        grid_spec=pltpu.PrefetchScalarGridSpec(
            num_scalar_prefetch=1,
            grid=(tiles,),
            in_specs=[anywhere] * 8,
            out_specs=[anywhere] * 6,
            scratch_shapes=[
                pltpu.VMEM((2, tokens, width), bf),
                pltpu.VMEM((2, width, tokens), bf),
                pltpu.VMEM((2, tokens, width), bf),
                pltpu.VMEM((2, width, width), bf),
                pltpu.VMEM((2, tokens, width), f32),
                pltpu.VMEM((2, tokens, width), f32),
                pltpu.VMEM((2, tokens, width), bf),
                pltpu.VMEM((n, 2 * half_rows, 128), bf),
                pltpu.SemaphoreType.DMA((4,)),
                pltpu.SemaphoreType.DMA((2 * n,)),
                pltpu.SemaphoreType.DMA((2 * n,)),
            ],
        ),
        out_shape=[shape((tokens, width), f32)] * 2 + [shape((tokens, width), bf)] * 2 + [shape((n, half_rows, 128), bf)] * 2,
        compiler_params=pltpu.CompilerParams(vmem_limit_bytes=VMEM_LIMIT),
        cost_estimate=pl.CostEstimate(flops=24 * tokens * width * width, bytes_accessed=32 << 20, transcendentals=2 * tokens * width),
        name="feed_forward",
    )(table, n2, n2_other, cot, cot_other, *mine, *theirs)


def causal(rows, cols, first):
    r = lax.broadcasted_iota(jnp.int32, (rows, cols), 0) + first
    c = lax.broadcasted_iota(jnp.int32, (rows, cols), 1)
    return c <= r

def attend_forward_kernel(flag_ref, q_ref, kc_ref, kp_ref, ko_ref, vc_ref, vp_ref, vo_ref, mixed_ref, total_ref):
    scale = HEAD_DIM ** -0.5
    f32 = jnp.float32
    def tile(at, earlier):
        rows = pl.ds(at * TILE, TILE)
        own = (at + 1) * TILE
        q = q_ref[rows, :]
        so = lax.dot_general(q, ko_ref[:own, :], NT, preferred_element_type=f32)
        so = jnp.where(causal(TILE, own, at * TILE), so, -1e30)
        parts = [so]
        values = [vo_ref[:own, :]]
        if earlier:
            parts = [lax.dot_general(q, kc_ref[...], NT, preferred_element_type=f32), lax.dot_general(q, kp_ref[...], NT, preferred_element_type=f32)] + parts
            values = [vc_ref[...], vp_ref[...]] + values
        top = functools.reduce(jnp.maximum, [jnp.max(s, axis=-1, keepdims=True) for s in parts])
        shift = top * (scale * LOG2E)
        soft = [jnp.exp2(s * (scale * LOG2E) - shift) for s in parts]
        total = sum(jnp.sum(s, axis=-1, keepdims=True) for s in soft)
        mixed = sum(jnp.dot(s.astype(jnp.bfloat16), v, preferred_element_type=f32) for s, v in zip(soft, values))
        mixed_ref[rows, :] = (mixed * (1.0 / total)).astype(mixed_ref.dtype)
        total_ref[0, rows, :] = shift + jnp.log2(total)
    flagged = flag_ref[0] > 0
    for at in range(BLOCK // TILE):
        pl.when(flagged)(functools.partial(tile, at, False))
        pl.when(jnp.logical_not(flagged))(functools.partial(tile, at, True))

def head_spec(rows, row_at=0, lead=None):
    if lead is None:
        return pl.BlockSpec((rows, HEAD_DIM), lambda h, *_: (row_at, h))
    return pl.BlockSpec((None, rows, HEAD_DIM), lambda h, *_: (lead, row_at, h))

def attend_forward(flag, query, key_ctx, key_prev, key_own, value_ctx, value_prev, value_own):
    ops=[query,key_ctx,key_prev,key_own,value_ctx,value_prev,value_own]
    sizes=[BLOCK,CTX,BLOCK,BLOCK,CTX,BLOCK,BLOCK]
    return pl.pallas_call(
        attend_forward_kernel,
        grid_spec=pltpu.PrefetchScalarGridSpec(num_scalar_prefetch=1, grid=(HEADS,),
            in_specs=[head_spec(s, o[1], o[2] if len(o) > 2 else None) for o, s in zip(ops, sizes)],
            out_specs=[head_spec(BLOCK), pl.BlockSpec((1, BLOCK, 1), lambda h, *_: (h, 0, 0))]),
        out_shape=[jax.ShapeDtypeStruct((BLOCK, HEADS * HEAD_DIM), jnp.bfloat16), jax.ShapeDtypeStruct((HEADS, BLOCK, 1), jnp.float32)],
        compiler_params=pltpu.CompilerParams(vmem_limit_bytes=VMEM_LIMIT),
        cost_estimate=LIGHT,
        name="attend_forward",
    )(flag, *[o[0] for o in ops])

def attend_backward_kernel(merge, flag_ref, q_ref, kc_ref, kp_ref, ko_ref, vc_ref, vp_ref, vo_ref, total_ref, g_ref, mixed_ref, *rest):
    scale = HEAD_DIM ** -0.5
    f32, bf = jnp.float32, jnp.bfloat16
    if merge:
        kadd_ref, vadd_ref, dq_ref, dkc_ref, dkp_ref, dko_ref, dvc_ref, dvp_ref, dvo_ref, acc_k, acc_v = rest
    else:
        dq_ref, dkc_ref, dkp_ref, dko_ref, dvc_ref, dvp_ref, dvo_ref, acc_k, acc_v = rest
    lead = CTX + BLOCK
    acc_k[...] = jnp.zeros_like(acc_k)
    acc_v[...] = jnp.zeros_like(acc_v)
    def tile(at, earlier):
        rows = pl.ds(at * TILE, TILE)
        own = (at + 1) * TILE
        q = q_ref[rows, :]
        g = g_ref[rows, :]
        total = total_ref[0, rows, :]
        keys = [(ko_ref[:own, :], vo_ref[:own, :], lead, own)]
        if earlier:
            keys = [(kc_ref[...], vc_ref[...], 0, CTX), (kp_ref[...], vp_ref[...], CTX, BLOCK)] + keys
        softs, grads = [], []
        for k, v, first, size in keys:
            s = lax.dot_general(q, k, NT, preferred_element_type=f32)
            s = s * (scale * LOG2E) - total
            if first == lead:
                s = jnp.where(causal(TILE, own, at * TILE), s, -1e30)
            softs.append(jnp.exp2(s))
            grads.append(lax.dot_general(g, v, NT, preferred_element_type=f32))
        rowsum = jnp.sum(mixed_ref[rows, :].astype(f32) * g.astype(f32), axis=-1, keepdims=True)
        dq = 0.0
        for (k, v, first, size), p, d in zip(keys, softs, grads):
            ds = (p * (d - rowsum)).astype(bf)
            dq += jnp.dot(ds, k, preferred_element_type=f32)
            at_rows = pl.ds(first, size)
            acc_k[at_rows, :] += lax.dot_general(ds, q, TN, preferred_element_type=f32)
            acc_v[at_rows, :] += lax.dot_general(p.astype(bf), g, TN, preferred_element_type=f32)
        dq_ref[rows, :] = (dq * scale).astype(dq_ref.dtype)
    flagged = flag_ref[0] > 0
    for at in range(BLOCK // TILE):
        pl.when(flagged)(functools.partial(tile, at, False))
        pl.when(jnp.logical_not(flagged))(functools.partial(tile, at, True))
    more_k = kadd_ref[...] if merge else 0.0
    more_v = vadd_ref[...] if merge else 0.0
    dkc_ref[...] = (acc_k[:CTX, :] * scale).astype(dkc_ref.dtype)
    dvc_ref[...] = acc_v[:CTX, :].astype(dvc_ref.dtype)
    dkp_ref[...] = (acc_k[CTX:lead, :] * scale + more_k).astype(dkp_ref.dtype)
    dvp_ref[...] = (acc_v[CTX:lead, :] + more_v).astype(dvp_ref.dtype)
    dko_ref[...] = (acc_k[lead:, :] * scale).astype(dko_ref.dtype)
    dvo_ref[...] = acc_v[lead:, :].astype(dvo_ref.dtype)

def attend_backward(flag, query, key_ctx, key_prev, key_own, value_ctx, value_prev, value_own, total, grad, mixed, add=None, final=False):
    ops=[query,key_ctx,key_prev,key_own,value_ctx,value_prev,value_own]
    sizes=[BLOCK,CTX,BLOCK,BLOCK,CTX,BLOCK,BLOCK]
    specs=[head_spec(s, o[1], o[2] if len(o) > 2 else None) for o, s in zip(ops, sizes)]
    specs+=[pl.BlockSpec((1, BLOCK, 1), lambda h, *_: (h, 0, 0)), head_spec(BLOCK, grad[1]), head_spec(BLOCK, mixed[1])]
    args=[o[0] for o in ops]+[total, grad[0], mixed[0]]
    if add is not None:
        specs+=[head_spec(BLOCK)]*2
        args+=list(add)
    width=HEADS*HEAD_DIM
    bf,f32=jnp.bfloat16,jnp.float32
    own = bf if final else f32
    out=lambda r,t: jax.ShapeDtypeStruct((r,width),t)
    return pl.pallas_call(
        functools.partial(attend_backward_kernel, add is not None),
        grid_spec=pltpu.PrefetchScalarGridSpec(num_scalar_prefetch=1, grid=(HEADS,),
            in_specs=specs,
            out_specs=[head_spec(BLOCK), head_spec(CTX), head_spec(BLOCK), head_spec(BLOCK), head_spec(CTX), head_spec(BLOCK), head_spec(BLOCK)],
            scratch_shapes=[pltpu.VMEM((CTX+2*BLOCK,HEAD_DIM),f32)]*2),
        out_shape=[out(BLOCK,bf), out(CTX,bf), out(BLOCK,bf), out(BLOCK,own), out(CTX,bf), out(BLOCK,bf), out(BLOCK,own)],
        compiler_params=pltpu.CompilerParams(vmem_limit_bytes=VMEM_LIMIT),
        cost_estimate=LIGHT,
        name="attend_backward",
    )(flag, *args)


def adamw_step(weight, first, second, gradient, step_rate, shrink):
    new_first = 0.9 * first + 0.1 * gradient
    new_second = 0.95 * second + 0.05 * gradient * gradient
    scaled_first = new_first / (1.0 - 0.9**STEP)
    scaled_second = new_second / (1.0 - 0.95**STEP)
    update = scaled_first / (jnp.sqrt(scaled_second) + 1e-08) + shrink * weight
    return (new_first, new_second, weight - step_rate * update)


def body(
    tokens,
    cotangent,
    carry_in,
    block_flags,
    qkv_w,
    qkv_m,
    qkv_v,
    out_w,
    out_m,
    out_v,
    up_w,
    up_m,
    up_v,
    down_w,
    down_m,
    down_v,
    gain_w,
    gain_m,
    gain_v,
    ssm_w,
    ssm_m,
    ssm_v,
):
    low_type = jnp.bfloat16
    n = lax.axis_size("blk")
    width = tokens.shape[-1]
    rows = width // n
    span = FF // n // 2
    far = far_masks(n)
    place = places(far + [2, 1])
    ff_place = places([1] + far + [2])
    side = lax.axis_index("win") & 1
    slots = 2 * (ff_place // 2) + jnp.arange(n, dtype=jnp.int32) % 2
    ff_table = jnp.concatenate([ff_place, slots, side[None].astype(jnp.int32)])
    upper_core = (lax.axis_index("blk") & 1) != 0


    small = jnp.concatenate([gain_w, ssm_w.reshape(-1, ssm_w.shape[-1])], axis=0)
    small = gather_round(small, n // 2)
    qkv_half = qkv_w.astype(low_type).reshape(3, 2, rows // 2, width)
    held = jnp.where(side == 1, qkv_half[:, 1], qkv_half[:, 0])[None]
    for mask in far[:-1]:
        held = widen(held, mask)
    mask = n // 4
    while mask > 2:
        small = gather_round(small, mask)
        mask //= 2
    own_half, other_half = pack_halves(upper_core, *tie((up_w, down_w), small), n)
    small = gather_round(tie(small, held), 2)
    small = gather_round(small, 1)
    small = joined_columns(small)
    near = widen(held, far[-1])
    across = swap(near, "blk", 2)
    near_y = swap(near, "win", 1)
    near_c = swap(near, "blk", 1)

    small = tie(small, near)
    gain_all, ssm_all = small[:2], small[2:].reshape(ssm_w.shape[:2] + (width,))
    inputs = tokens[0].astype(jnp.float32)
    flags = block_flags[0]
    markers = flags.astype(jnp.float32)
    carried = carry_in[0]
    block_count = markers.shape[0]
    last = block_count - 1
    forward_pairs = [(at, at + 1) for at in range(n - 1)]
    normed = layer_norm(inputs, gain_all[0])
    normed_low = normed.astype(low_type)
    rate = jnp.exp(ssm_all[0])
    decay = jnp.exp(-rate)
    root = jnp.sqrt(-jnp.expm1(-2.0 * rate))
    beta = root * ssm_all[1]
    over_block = jnp.exp(-rate * BLOCK)
    through = jnp.prod(1.0 - markers) * jnp.exp(-rate * (block_count * BLOCK))
    came_half = swap(other_half, "blk", 1)
    cot = cotangent[0]
    cot_other = swap(cot, "blk", 1)

    def chunk(c):
        ups = [own_half[c * rows : (c + 1) * rows], came_half[c * rows : (c + 1) * rows]]
        is_own = upper_core == (c == 1)
        down = jnp.where(is_own, own_half[2 * rows :], came_half[2 * rows :])
        return jnp.where(side == 1, down, jnp.concatenate(ups, axis=0))

    first = jnp.concatenate([out_w.astype(low_type), chunk(0)], axis=0)[None]
    second = chunk(1)[None]
    first_came = swap(tie(first, near), "blk", far[0])
    base_ctx, middles, slopes, ends = scan_states(tie(normed, near, first), decay, ssm_all[2] * beta)
    nothing = jnp.zeros_like(rate)
    _, local_end = state_ahead(nothing, markers, carried, beta * tie(ends, first_came, near_y), over_block)
    across = tie(across, ends)
    across_y = swap(across, "win", 1)
    across_c = swap(across, "blk", 1)
    near_yc = swap(near_y, "blk", 1)
    scan = CarriedIn(through, tie(local_end, across), False)
    scan.step()
    scan.step()
    sent = tie(normed_low[-BLOCK:], scan.total)
    came_normed = lax.ppermute(sent, "blk", forward_pairs)
    while scan.mask < n:
        scan.step()
    entering = scan.ahead[1]
    first = jnp.concatenate([first, tie(first_came, entering)], axis=0)
    for mask in far[1:-1]:
        first = widen(first, mask)
    first_came = swap(first, "blk", far[-1])
    begins, _ = state_ahead(tie(entering, across_y, came_normed), markers, carried, beta * ends, over_block)
    contexts_low = finish_contexts(base_ctx, rate, ssm_all[2] * begins).reshape(-1, width)
    came_ctx = lax.ppermute(contexts_low[-CTX:], "blk", forward_pairs)
    across_yc = swap(tie(across_y, contexts_low), "blk", 1)
    table = jnp.concatenate([place, jnp.stack([side, 1 - side]).astype(jnp.int32) * (rows // 2)])
    projected, extra_pair, qkv_all = project(
        table,
        tie(normed_low, contexts_low),
        [came_normed, contexts_low],
        [near, across, near_c, across_c],
        [near_y, across_y, near_yc, across_yc],
    )
    to_pair = lambda v: jnp.einsum("td,kde->kte", v, qkv_all[1:], preferred_element_type=jnp.float32).astype(low_type)
    first_came = tie(first_came, projected, came_ctx)
    first = jnp.concatenate([first, first_came], axis=0)

    first_x = swap(first, "blk", 2)
    out_near_c = swap(first[:, :rows], "blk", 1)
    near_half = first[:, rows:]
    theirs0 = [swap(near_half, "win", 1)]
    second = tie(second, first)
    second_came = swap(second, "blk", far[0])
    context_rows = BLOCK // CTX

    def lists(at):
        own = [(projected, at, 1), (projected, at, 2)]
        if at:
            ctx_at = context_rows + at - 1
            earlier = [(extra_pair, ctx_at, 0), (projected, at - 1, 1), (extra_pair, ctx_at, 1), (projected, at - 1, 2)]
        else:
            earlier = [(came_pair, 0, 0), (extra_pair, 0, 0), (came_pair, 0, 1), (extra_pair, 0, 1)]
        return [(projected, at, 0), earlier[0], earlier[1], own[0], earlier[2], earlier[3], own[1]]

    attended = {}
    came_pair = None
    place_flags = tie(flags, first, near_half)
    for at in range(block_count)[::-1]:
        attended[at] = attend_forward(place_flags[at : at + 1], *lists(at))
        if at == last:
            second = jnp.concatenate([second, tie(second_came, attended[at][0])], axis=0)
            for mask in far[1:-1]:
                second = widen(second, mask)
            second_came = swap(second, "blk", far[-1])
            place_flags = tie(flags, second)
            came_pair = to_pair(tie(came_ctx, attended[at][0]))
    mixed_low = jnp.concatenate([attended[at][0] for at in range(block_count)], axis=0)
    totals = [attended[at][1] for at in range(block_count)]
    first_x = tie(first_x, mixed_low)
    out_across_c = swap(first_x[:, :rows], "blk", 1)
    theirs0.append(swap(first_x[:, rows:], "win", 1))
    second = jnp.concatenate([second, tie(second_came, mixed_low)], axis=0)
    second_x = swap(second, "blk", 2)
    theirs1 = [swap(tie(second, theirs0[1]), "win", 1)]
    middle, normed_two_low, out_all = branch(
        place, tokens[0], tie(mixed_low, second, theirs0[0]), gain_all[1:], [first, first_x, out_near_c, out_across_c]
    )
    normed_two_low = tie(normed_two_low, theirs0[1], second_x)
    n2_other = swap(normed_two_low, "blk", 1)
    theirs1.append(swap(second_x, "win", 1))
    ff = [feed_forward(ff_table, normed_two_low, n2_other, cot, cot_other, [first, first_x], theirs0, TILES)]
    keep0, send0 = ff[0][4:]
    came0 = swap(send0, "win", 1)
    backs = [swap(ff[0][3], "blk", 1), swap(ff[0][2], "blk", 1)]
    ff.append(feed_forward(ff_table, tie(normed_two_low, send0, ff[0][3]), n2_other, cot, cot_other, [second, second_x], theirs1, TILES))
    keep1, send1 = ff[1][4:]
    came1 = swap(tie(send1, came0), "win", 1)
    keep0, came0 = tie((keep0, came0), keep1)
    keep0, send0 = fold(keep0, came0)
    came0 = swap(send0, "blk", 2)
    own_grad, other_grad, other_out = tie((ff[1][1], ff[1][3], ff[1][2]), send0)
    backs += [swap(other_grad, "blk", 1), swap(other_out, "blk", 1)]
    f32 = jnp.float32
    grad_middle, grad_branch, grad_mixed, grad_gain_two = middle_back(
        middle, [ff[0][1], own_grad], [backs[0], backs[2]], cot, gain_all[1:], out_all
    )
    back_dot = lambda a, b: lax.dot_general(a, b, NT, preferred_element_type=jnp.float32)
    grads = []
    for at in range(block_count):
        add = (grads[-1][3], grads[-1][6]) if at else None
        query, *others = lists(at)
        if at:
            grad_mixed = tie(grad_mixed, grads[-1][0])
        grads.append(attend_backward(flags[at : at + 1], query, *others, totals[at], (grad_mixed, at), (mixed_low, at), add, at == last))
        if not at:
            earlier_k = jnp.concatenate([grads[0][2], grads[0][1]], axis=0)
            earlier_v = jnp.concatenate([grads[0][5], grads[0][4]], axis=0)
            sent_back = (back_dot(earlier_k, qkv_all[1]) + back_dot(earlier_v, qkv_all[2])).astype(low_type)
            came_back = lax.ppermute(sent_back, "blk", [(at + 1, at) for at in range(n - 1)])
            keep1, came1 = tie((keep1, came1), grads[0][0])
            keep1, send1 = fold(keep1, came1)
            came1 = swap(send1, "blk", 2)
            keep0, came0 = tie((keep0, came0), send1)
            for mask in far[1:][::-1]:
                keep0, send0 = fold(keep0, came0)
                came0 = swap(send0, "blk", mask)
            grad_mixed = tie(grad_mixed, send0, send1, sent_back)
    later = range(1, block_count)
    own_contexts = jnp.concatenate(
        [back_dot(grads[at][1], qkv_all[1]) + back_dot(grads[at][4], qkv_all[2]) for at in later], axis=0
    )
    grad_contexts = jnp.concatenate([own_contexts, came_back[BLOCK:].astype(f32)], axis=0).reshape(block_count, CTX, width)
    sums = adjoint_sums(grad_contexts, decay)
    local_starts = jnp.exp(-rate * (BEFORE + 1)) * ssm_all[2] * sums
    _, _, leaving_own = adjoint_behind(nothing, markers, local_starts, over_block)
    scan = CarriedIn(through, leaving_own, True)
    scan.step()
    started = scan.total
    q_grads = [part[0] for part in grads]
    kv_grads = [
        [grads[at][own - 1] for at in later] + [grads[last][own], grads[0][own - 1]]
        + [grads[at][own - 2] for at in range(block_count)]
        for own in (3, 6)
    ]
    keep0, came0, keep1, came1 = tie((keep0, came0, keep1, came1), sums)
    for mask in far[:1]:
        keep0, send0 = fold(keep0, came0)
        came0 = swap(send0, "blk", mask)
    keep1, send1 = fold(keep1, came1)
    came1 = swap(tie(send1, send0), "blk", far[-1])
    keep2, send2 = weight_grad(place, [[tie(mixed_low, started, send0, send1)], [normed_low]], [[grad_branch], q_grads])
    came2 = swap(send2, "blk", 1)
    scan.step(keep2)
    keep1, came1, came0 = tie((keep1, came1, came0), keep2)
    sum0 = sum_over_win(add_low(keep0, came0), 2)
    for mask in far[:-1][::-1]:
        keep1, send1 = fold(keep1, came1)
        came1 = swap(send1, "blk", mask)
    kv_left = tie(normed_low, scan.total, send1, send2, sum0)
    keep3, send3 = weight_grad(place, [[kv_left, came_normed, came_ctx, contexts_low]], kv_grads)
    came3 = swap(send3, "blk", 1)
    scan.step(keep3)
    whole2 = add_low(keep2, tie(came2, keep3, scan.total))
    keep2 = jnp.where(side == 1, whole2[:, rows:], whole2[:, :rows])
    send2 = jnp.where(side == 1, whole2[:, :rows], whole2[:, rows:])
    came2 = swap(send2, "win", 1)
    keep3, send3 = fold(keep3, tie(came3, send2))
    came3 = swap(send3, "blk", 2)
    while scan.mask < n:
        scan.step(send3)
    leaving = tie(scan.ahead[1], send2, send3)
    enters, starts, _ = adjoint_behind(leaving, markers, local_starts, over_block)
    grad_carried = markers[:, None, None] * starts
    at_context = beta * middles + jnp.exp(-rate * BEFORE) * begins
    grad_normed_ssm, grad_mix, grad_beta, grad_decay, passed = back_states(
        normed, grad_contexts, at_context, enters, rate, decay, beta, ssm_all[2]
    )
    came1, came2, came3, grad_normed_ssm = tie((came1, came2, came3, grad_normed_ssm))
    keep2, send2 = fold(keep2, came2)
    came2 = swap(send2, "blk", 2)
    keep3, send3 = fold(keep3, tie(came3, send2))
    came3 = swap(send3, "blk", far[-1])
    sum1 = sum_over_win(add_low(keep1, tie(came1, send3)), 2)
    mine_ff = jnp.stack([sum0, sum1])
    theirs_ff = swap(mine_ff, "win", 1)
    grad_tokens, grad_gain_one = input_back(
        tokens[0],
        tie(grad_normed_ssm, send2, send3, mine_ff),
        grad_middle,
        came_back,
        gain_all[:1],
        [q_grads] + [part[:block_count] for part in kv_grads],
        qkv_all,
    )
    keep2, send2 = fold(keep2, tie(came2, grad_tokens))
    came2 = swap(send2, "blk", far[-1])
    for mask in far[:-1][::-1]:
        keep3, send3 = fold(keep3, tie(came3, send2))
        came3 = swap(send3, "blk", mask)
    grad_gain_one = tie(grad_gain_one, send2, send3)
    grad_beta = grad_beta + jnp.sum(passed * middles, axis=0)
    grad_decay = grad_decay + jnp.sum(
        passed * (BEFORE * jnp.exp(-rate * (BEFORE - 1)) * begins + beta * slopes), axis=0
    )
    grad_rate = grad_beta * ssm_all[1] * jnp.exp(-2.0 * rate) / root - decay * grad_decay
    grad_ssm = jnp.stack([grad_rate * rate, grad_beta * root, grad_mix])
    ups, downs = both_sides(side, mine_ff, tie(theirs_ff, grad_tokens))
    chunk_at = upper_core.astype(jnp.int32)
    own_down = jnp.where(upper_core, downs[1], downs[0])
    other_down = jnp.where(upper_core, downs[0], downs[1])
    sent_ff = jnp.concatenate([ups[:, 1], other_down], axis=0)
    came_ff = swap(sent_ff, "blk", 1)
    up_halves = both_sides(chunk_at, ups[:, 0], came_ff[:2])
    down_halves = both_sides(chunk_at, own_down, came_ff[2:])
    columns = lambda v: v.reshape(v.shape[:-2] + (-1, rows, 128)).swapaxes(-3, -2).reshape(v.shape[:-2] + (rows, width))
    sum_up = columns(up_halves).reshape(2, 2, rows, n // 2, span).transpose(2, 3, 1, 0, 4).reshape(rows, FF).astype(f32)
    sum_down = columns(down_halves).reshape(-1, width).astype(f32)
    up_first, up_second, up_new = adamw_step(up_w, up_m, up_v, sum_up, 2.0 * D ** (-0.5), 0.1)
    down_first, down_second, down_new = adamw_step(
        down_w, down_m, down_v, sum_down, 2.0 * FF ** (-0.5), 0.1
    )
    result = middle + ff[0][0] + tie(ff[1][0], grad_tokens) + (backs[1].astype(f32) + backs[3].astype(f32))
    result = result.astype(low_type)
    sum_small = jnp.concatenate([grad_gain_one, grad_gain_two, grad_ssm.reshape(-1, width)], axis=0)
    mask = n // 2
    while mask > 2:
        sum_small = reduce_round(sum_small, mask)
        mask //= 2
    came2, came3 = tie((came2, came3), sum_small)
    for mask in far[:-1][::-1]:
        keep2, send2 = fold(keep2, came2)
        came2 = swap(send2, "blk", mask)
    mine3 = add_low(keep3, came3)
    sum3 = sum_over_win(mine3, 1)[0].astype(f32)
    sum_small = tie(sum_small, send2, mine3)
    for mask in (2, 1):
        sum_small = reduce_round(sum_small, mask)
    came2 = tie(came2, sum_small, up_new, down_new)
    mine2 = sum_over_win(add_low(keep2, came2), 2)[0]
    sum2 = both_sides(side, mine2, swap(mine2, "win", 1)).reshape(-1, width).astype(f32)
    sum_small = tie(sum_small, mine2)
    mask = 1
    while mask < lax.axis_size("win"):
        sum_small = sum_small + swap(sum_small, "win", mask)
        mask *= 2
    sum_gain, sum_ssm = sum_small[:2], sum_small[2:].reshape(ssm_w.shape)

    sum_out = sum2[:rows]
    sum_qkv = jnp.concatenate([sum2[rows:], sum3], axis=0).reshape(3, rows, width)
    qkv_first, qkv_second, qkv_new = adamw_step(
        qkv_w, qkv_m, qkv_v, sum_qkv, 2.0 * D ** (-0.5), 0.1
    )
    out_first, out_second, out_new = adamw_step(out_w, out_m, out_v, sum_out, 1.0, 0.1)
    gain_first, gain_second, gain_new = adamw_step(gain_w, gain_m, gain_v, sum_gain, 1.0, 0.0)
    ssm_first, ssm_second, ssm_new = adamw_step(ssm_w, ssm_m, ssm_v, sum_ssm, 4.0, 0.0)
    return (
        result[None],
        grad_tokens[None],
        grad_carried[None],
        qkv_first,
        qkv_second,
        qkv_new,
        out_first,
        out_second,
        out_new,
        up_first,
        up_second,
        up_new,
        down_first,
        down_second,
        down_new,
        gain_first,
        gain_second,
        gain_new,
        ssm_first,
        ssm_second[1:],
        ssm_second[0],
        ssm_new,
    )


def solution(mesh):
    in_specs = (
        P("win", "blk", None),
        P("win", "blk", None),
        P("win", "blk", None, None),
        P("win", "blk"),
        P(None, "blk", None),
        P(None, "blk", None),
        P(None, "blk", None),
        P("blk", None),
        P("blk", None),
        P("blk", None),
        P("blk", None),
        P("blk", None),
        P("blk", None),
        P("blk", None),
        P("blk", None),
        P("blk", None),
        P(None, "blk"),
        P(None, "blk"),
        P(None, "blk"),
        P(None, None, "blk"),
        P(None, None, "blk"),
        P(None, None, "blk"),
    )
    out_specs = (
        P("win", "blk", None),
        P("win", "blk", None),
        P("win", "blk", None, None),
        P(None, "blk", None),
        P(None, "blk", None),
        P(None, "blk", None),
        P("blk", None),
        P("blk", None),
        P("blk", None),
        P("blk", None),
        P("blk", None),
        P("blk", None),
        P("blk", None),
        P("blk", None),
        P("blk", None),
        P(None, "blk"),
        P(None, "blk"),
        P(None, "blk"),
        P(None, None, "blk"),
        P(None, None, "blk"),
        P(None, "blk"),
        P(None, None, "blk"),
    )
    return jax.shard_map(body, mesh=mesh, in_specs=in_specs, out_specs=out_specs, check_vma=False)
```

```python
import functools

import jax
import jax.numpy as jnp
from jax import lax
from jax.experimental import pallas as pl
from jax.experimental.pallas import tpu as pltpu
from jax.sharding import PartitionSpec as P

D = 1024
FF = 4096
HEADS = 8
HEAD_DIM = 128
CTX = 128
BLOCK = 512
STEP = 10
CHUNKS = 2
TILES = 2
TILE = 256
BEFORE = BLOCK - CTX
LANES = 512
VMEM_LIMIT = 60 * 1024 * 1024
LOG2E = 1.4426950408889634
GC = 0.79788456
GQ = 0.044715
LIGHT = pl.CostEstimate(flops=1000, bytes_accessed=1000, transcendentals=0)
NT = (((1,), (1,)), ((), ()))
TN = (((0,), (0,)), ((), ()))

def swap(value, axis, mask):
    count = lax.axis_size(axis)
    return lax.ppermute(value, axis, [(at, at ^ mask) for at in range(count)])


def tie(value, *after):
    return lax.optimization_barrier((value, after))[0]


def far_masks(n):
    masks = [1 << at for at in range(2, n.bit_length() - 1)][::-1]
    if len(masks) >= 2:
        masks[0] |= masks[1]
    return masks


def shift_of(position, masks):
    total = 0
    for at, mask in enumerate(masks):
        if position >> at & 1:
            total ^= mask
    return total


def places(masks):
    mine = lax.axis_index("blk")
    return jnp.stack([mine ^ shift_of(position, masks) for position in range(1 << len(masks))]).astype(jnp.int32)


def widen(held, mask, *after):
    return jnp.concatenate([held, swap(tie(held, *after), "blk", mask)], axis=0)


def add_low(a, b):
    return (a.astype(jnp.float32) + b.astype(jnp.float32)).astype(jnp.bfloat16)


def fold(keep, came):
    half = keep.shape[0] // 2
    return add_low(keep[:half], came[:half]), add_low(keep[half:], came[half:])


def sum_over_win(value, mask):
    while mask < lax.axis_size("win"):
        value = add_low(value, swap(value, "win", mask))
        mask *= 2
    return value


def both_sides(side, mine, other):
    return jnp.stack([jnp.where(side == 1, other, mine), jnp.where(side == 1, mine, other)])


def gather_round(value, mask):
    came = swap(value, "blk", mask)
    upper = (lax.axis_index("blk") & mask) != 0
    return jnp.stack([jnp.where(upper, came, value), jnp.where(upper, value, came)])


def joined_columns(value):
    bits = value.ndim - 2
    value = value.transpose((bits,) + tuple(range(bits))[::-1] + (bits + 1,))
    return value.reshape(value.shape[0], -1)


def reduce_round(value, mask):
    half = value.shape[-1] // 2
    upper = (lax.axis_index("blk") & mask) != 0
    low, high = value[:, :half], value[:, half:]
    return jnp.where(upper, high, low) + swap(jnp.where(upper, low, high), "blk", mask)


class CarriedIn:
    def __init__(self, through, value, backward):
        self.total = jnp.stack([through, value])
        self.ahead = jnp.stack([jnp.ones_like(through), jnp.zeros_like(value)])
        self.backward = backward
        self.mask = 1

    def step(self, *hold):
        compose = lambda earlier, later: jnp.stack([earlier[0] * later[0], later[0] * earlier[1] + later[1]])
        other = tie(swap(self.total, "blk", self.mask), *hold)
        before = ((lax.axis_index("blk") & self.mask) != 0) != self.backward
        self.ahead = jnp.where(before, compose(other, self.ahead), self.ahead)
        self.total = jnp.where(before, compose(other, self.total), compose(self.total, other))
        self.mask *= 2


def layer_norm(values, gain):
    centered = values - jnp.mean(values, axis=-1, keepdims=True)
    variance = jnp.mean(centered * centered, axis=-1, keepdims=True)
    return centered * lax.rsqrt(variance + 1e-05) * gain


def lane_spec(shape, lanes):
    lead = len(shape) - 1
    return pl.BlockSpec(tuple(shape[:-1]) + (lanes,), lambda i: (0,) * lead + (i,))

def lane_call(kernel, name, inputs, outputs, scratch, lanes):
    width = inputs[0].shape[-1]
    return pl.pallas_call(
        kernel,
        grid=(width // lanes,),
        in_specs=[lane_spec(v.shape, lanes) for v in inputs],
        out_specs=[lane_spec(s, lanes) for s, _ in outputs],
        out_shape=[jax.ShapeDtypeStruct(s, t) for s, t in outputs],
        scratch_shapes=scratch,
        compiler_params=pltpu.CompilerParams(vmem_limit_bytes=VMEM_LIMIT),
        cost_estimate=LIGHT,
        name=name,
    )(*inputs)

def scan_kernel(x_ref, a_ref, mix_ref, ctx_ref, mid_ref, slope_ref, end_ref):
    blocks = ctx_ref.shape[0]
    a = a_ref[...]
    mix = mix_ref[...]
    zero = jnp.zeros_like(a)
    def before(group, state):
        state = list(state)
        for j in range(blocks):
            u, d = state[j]
            first = pl.multiple_of(j * BLOCK + group * 8, 8)
            rows = x_ref[pl.ds(first, 8), :]
            for k in range(8):
                d = a * d + u
                u = a * u + rows[k:k + 1, :]
            state[j] = (u, d)
        return tuple(state)
    state = lax.fori_loop(0, BEFORE // 8, before, tuple((zero, zero) for _ in range(blocks)))
    for j in range(blocks):
        mid_ref[j] = state[j][0]
        slope_ref[j] = state[j][1]
    def inside(group, state):
        state = list(state)
        for j in range(blocks):
            u = state[j]
            first = pl.multiple_of(j * BLOCK + BEFORE + group * 8, 8)
            rows = x_ref[pl.ds(first, 8), :]
            made = []
            for k in range(8):
                u = a * u + rows[k:k + 1, :]
                made.append(jnp.sum(mix * u, axis=0, keepdims=True))
            ctx_ref[j, pl.ds(pl.multiple_of(group * 8, 8), 8), :] = jnp.concatenate(made, axis=0)
            state[j] = u
        return tuple(state)
    state = lax.fori_loop(0, CTX // 8, inside, tuple(s[0] for s in state))
    for j in range(blocks):
        end_ref[j] = state[j]

def scan_states(x, a, mix):
    width = x.shape[-1]
    blocks = x.shape[0] // BLOCK
    states = ((blocks,) + a.shape, jnp.float32)
    return lane_call(scan_kernel, "scan_states", [x, a, mix], [((blocks, CTX, width), jnp.float32), states, states, states], [], 512)

def fan(rate, weight, lag, rows, store):
    count = rate.shape[0]
    for c in range(rate.shape[1] // 128):
        lanes = slice(c * 128, (c + 1) * 128)
        row = lax.broadcasted_iota(jnp.int32, (8, 128), 0).astype(jnp.float32)
        values = tuple(weight[s:s + 1, lanes] * jnp.exp(-rate[s:s + 1, lanes] * (lag(row))) for s in range(count))
        steps = [jnp.broadcast_to(jnp.exp(-8.0 * rate[s:s + 1, lanes]), (8, 128)) for s in range(count)]
        def group_of(group, values):
            total = values[0]
            for v in values[1:]:
                total = total + v
            store(group, lanes, total)
            return tuple(v * s for v, s in zip(values, steps))
        lax.fori_loop(0, rows // 8, group_of, values)

def context_kernel(base_ref, rate_ref, weight_ref, out_ref, held):
    for j in range(base_ref.shape[0]):
        def store(group, lanes, total, j=j):
            rows = pl.ds(pl.multiple_of(group * 8, 8), 8)
            held[rows, lanes] = base_ref[j, rows, lanes] + total
        fan(rate_ref[...], weight_ref[j], lambda row: row + (BEFORE + 1.0), CTX, store)
        out_ref[j] = held[...].astype(out_ref.dtype)

def finish_contexts(base, rate, weight):
    return lane_call(context_kernel, "finish_contexts", [base, rate, weight], [(base.shape, jnp.bfloat16)], [pltpu.VMEM((CTX, 512), jnp.float32)], 512)[0]

def adjoint_kernel(g_ref, a_ref, out_ref):
    blocks = g_ref.shape[0]
    a = a_ref[...]
    def step(group, state):
        state = list(state)
        for j in range(blocks):
            first = pl.multiple_of(CTX - 8 - group * 8, 8)
            rows = g_ref[j, pl.ds(first, 8), :]
            for k in range(7, -1, -1):
                state[j] = a * state[j] + rows[k:k + 1, :]
        return tuple(state)
    state = lax.fori_loop(0, CTX // 8, step, tuple(jnp.zeros_like(a) for _ in range(blocks)))
    for j in range(blocks):
        out_ref[j] = state[j]

def adjoint_sums(g, a):
    return lane_call(adjoint_kernel, "adjoint_sums", [g, a], [((g.shape[0],) + a.shape, jnp.float32)], [], 512)[0]

def back_kernel(x_ref, g_ref, mid_ref, enter_ref, rate_ref, a_ref, beta_ref, mix_ref, gx_ref, gmix_ref, gbeta_ref, ga_ref, leave_ref, held):
    blocks = g_ref.shape[0]
    a = a_ref[...]
    beta = beta_ref[...]
    mix = mix_ref[...]
    zero = jnp.zeros_like(a)

    def ahead(group, states):
        states = list(states)
        for j in range(blocks):
            rows = x_ref[pl.ds(pl.multiple_of(j * BLOCK + BEFORE + group * 8, 8), 8), :]
            for k in range(8):
                held[j, group * 8 + k] = states[j]
                states[j] = a * states[j] + beta * rows[k:k + 1, :]
        return tuple(states)

    lasts = lax.fori_loop(0, CTX // 8, ahead, tuple(mid_ref[j] for j in range(blocks)))

    def back(at, state):
        carries, curs, gmix, gbeta, ga = state
        carries, curs = list(carries), list(curs)
        group = CTX // 8 - 1 - at
        first = pl.multiple_of(group * 8, 8)
        for j in range(blocks):
            here = pl.ds(pl.multiple_of(j * BLOCK + BEFORE + group * 8, 8), 8)
            xs = x_ref[here, :]
            gs = g_ref[j, pl.ds(first, 8), :]
            made = [None] * 8
            for k in range(7, -1, -1):
                g = gs[k:k + 1, :]
                lam = carries[j] + mix * g
                prev = held[j, group * 8 + k]
                gmix = gmix + g * curs[j]
                gbeta = gbeta + lam * xs[k:k + 1, :]
                ga = ga + lam * prev
                made[k] = jnp.sum(beta * lam, axis=0, keepdims=True)
                carries[j] = a * lam
                curs[j] = prev
            gx_ref[here, :] = jnp.concatenate(made, axis=0)
        return tuple(carries), tuple(curs), gmix, gbeta, ga

    carries, _, gmix, gbeta, ga = lax.fori_loop(
        0, CTX // 8, back, (tuple(enter_ref[j] for j in range(blocks)), lasts, zero, zero, zero))
    gmix_ref[...] = gmix
    gbeta_ref[...] = gbeta
    ga_ref[...] = ga
    for j in range(blocks):
        leave_ref[j] = carries[j]

        def store(group, lanes, total, j=j):
            rows = pl.ds(pl.multiple_of(j * BLOCK + BEFORE - 8 - group * 8, 8), 8)
            gx_ref[rows, lanes] = total

        fan(rate_ref[...], beta * carries[j], lambda row: 7.0 - row, BEFORE, store)


def back_states(x, g, mid, enter, rate, a, beta, mix):
    states = (a.shape, jnp.float32)
    return lane_call(back_kernel, "back_states", [x, g, mid, enter, rate, a, beta, mix],
        [(x.shape, jnp.float32), states, states, states, (mid.shape, jnp.float32)],
        [pltpu.VMEM((g.shape[0], CTX, a.shape[0], 256), jnp.float32)], 256)

def state_ahead(begin, markers, carried, ends, decay):
    begins = []
    for j in range(carried.shape[0]):
        begin = jnp.where(markers[j] > 0, carried[j], begin)
        begins.append(begin)
        begin = decay * begin + ends[j]
    return jnp.stack(begins), begin

def adjoint_behind(enter, markers, locals_, decay):
    enters, starts = [], []
    for j in range(locals_.shape[0])[::-1]:
        enters.append(enter)
        start = decay * enter + locals_[j]
        starts.append(start)
        enter = jnp.where(markers[j] > 0, 0.0, start)
    return jnp.stack(enters[::-1]), jnp.stack(starts[::-1]), enter


def load_pieces(n, parts, rows, place_ref, refs, skip, target, sems):
    lists = [[] for _ in range(parts)]
    count = n // len(refs)
    for position in range(n):
        src = refs[position // count].at[position % count]
        first = pl.multiple_of(place_ref[position] * (target.shape[1] // n) + skip, rows)
        for part in range(parts):
            lists[part].append(
                pltpu.make_async_copy(
                    src.at[pl.ds(part * rows, rows)],
                    target.at[part, pl.ds(first, rows)],
                    sems.at[part * n + position],
                )
            )
    return lists


def pack_kernel(n, rows, span, core_ref, up_ref, down_ref, own_ref, other_ref):
    def write(core, ref):
        for chunk in range(2):
            for chip in range(n // 2):
                first = ((2 * chip + chunk) * 2 + core) * span
                ref[chunk * rows : (chunk + 1) * rows, chip * span : (chip + 1) * span] = up_ref[
                    :, first : first + span
                ].astype(ref.dtype)
        ref[2 * rows :, :] = down_ref[core * span : (core + 1) * span, :].astype(ref.dtype)

    for core in range(2):
        @pl.when(core_ref[0] == core)
        def _(core=core):
            write(core, own_ref)
            write(1 - core, other_ref)


def pack_halves(upper_core, up, down, n):
    rows, width = up.shape[0], down.shape[1]
    span = down.shape[0] // 2
    shape = jax.ShapeDtypeStruct((2 * rows + span, width), jnp.bfloat16)
    return pl.pallas_call(
        functools.partial(pack_kernel, n, rows, span),
        in_specs=[pl.BlockSpec(memory_space=pltpu.SMEM)] + [pl.BlockSpec(memory_space=pltpu.VMEM)] * 2,
        out_specs=[pl.BlockSpec(memory_space=pltpu.VMEM)] * 2,
        out_shape=[shape, shape],
        cost_estimate=LIGHT,
        name="pack_halves",
    )(upper_core.astype(jnp.int32)[None], up, down)


def load_halves(n, rows, place_ref, refs, skip, target, sems):
    count = n // len(refs)
    half = rows // 2
    lists = [[], []]
    for position in range(n):
        src = refs[position // count].at[position % count]
        rows_at = pl.ds(pl.multiple_of(place_ref[position] * rows + skip, half), half)
        lists[0].append(pltpu.make_async_copy(src.at[0], target.at[0, rows_at], sems.at[position]))
        rest = pl.ds(1, 2)
        lists[1].append(pltpu.make_async_copy(src.at[rest], target.at[rest, rows_at], sems.at[n + position]))
    return lists


def project_kernel(n, rows, sizes, place_ref, x_ref, *refs):
    parts = 3
    extras, refs = refs[: len(sizes)], refs[len(sizes) :]
    mine, theirs = refs[:4], refs[4:8]
    out_ref, extra_ref, weights_ref, held, extra_v, load_sems, store_sem = refs[8:]
    at = pl.program_id(0)
    store = pltpu.make_async_copy(held, weights_ref, store_sem.at[0])
    lists = load_halves(n, rows, place_ref, mine, place_ref[n], held, load_sems.at[pl.ds(0, 2 * n)])
    more = load_halves(n, rows, place_ref, theirs, place_ref[n + 1], held, load_sems.at[pl.ds(2 * n, 2 * n)])
    lists = [a + b for a, b in zip(lists, more)]
    first = 0
    for i, (ref, size) in enumerate(zip(extras, sizes)):
        lists[1].append(pltpu.make_async_copy(ref, extra_v.at[pl.ds(first, size)], load_sems.at[4 * n + i]))
        first += size

    @pl.when(at == 0)
    def _():
        for copy in lists[0] + lists[1]:
            copy.start()
        for copy in lists[0]:
            copy.wait()

    @pl.when(at == 1)
    def _():
        for copy in lists[1]:
            copy.wait()
        store.start()

    out_ref[0] = jnp.dot(x_ref[...], held[at], preferred_element_type=jnp.float32).astype(out_ref.dtype)

    @pl.when(at > 0)
    def _():
        extra_ref[0] = jnp.dot(extra_v[...], held[at], preferred_element_type=jnp.float32).astype(extra_ref.dtype)

    @pl.when(at == parts - 1)
    def _():
        store.wait()


def project(place, x, extras, mine, theirs):
    n = place.shape[0] - 2
    tokens, width = x.shape
    rows = width // n
    parts = 3
    sizes = [v.shape[0] for v in extras]
    anywhere = pl.BlockSpec(memory_space=pl.ANY)
    shape = lambda *dims: jax.ShapeDtypeStruct(dims, jnp.bfloat16)
    return pl.pallas_call(
        functools.partial(project_kernel, n, rows, sizes),
        grid_spec=pltpu.PrefetchScalarGridSpec(
            num_scalar_prefetch=1,
            grid=(parts,),
            in_specs=[pl.BlockSpec((tokens, width), lambda i, *_: (0, 0))] + [anywhere] * (8 + len(sizes)),
            out_specs=[
                pl.BlockSpec((1, tokens, width), lambda i, *_: (i, 0, 0)),
                pl.BlockSpec((1, sum(sizes), width), lambda i, *_: (jnp.maximum(i - 1, 0), 0, 0)),
                anywhere,
            ],
            scratch_shapes=[
                pltpu.VMEM((parts, width, width), jnp.bfloat16),
                pltpu.VMEM((sum(sizes), width), jnp.bfloat16),
                pltpu.SemaphoreType.DMA((4 * n + len(sizes),)),
                pltpu.SemaphoreType.DMA((1,)),
            ],
        ),
        out_shape=[shape(parts, tokens, width), shape(parts - 1, sum(sizes), width), shape(parts, width, width)],
        compiler_params=pltpu.CompilerParams(vmem_limit_bytes=VMEM_LIMIT),
        cost_estimate=LIGHT,
        name="project",
    )(place, x, *extras, *mine, *theirs)


def branch_kernel(n, rows, place_ref, x_ref, mixed_ref, gain_ref, *refs):
    middle_ref, normed_ref, weights_ref, held, load_sems, store_sem = refs[4:]
    at = pl.program_id(0)
    copies = load_pieces(n, 1, rows, place_ref, refs[:4], 0, held, load_sems)[0]
    store = pltpu.make_async_copy(held.at[0], weights_ref, store_sem.at[0])

    @pl.when(at == 0)
    def _():
        for copy in copies:
            copy.start()
        for copy in copies:
            copy.wait()
        store.start()

    middle = x_ref[...].astype(jnp.float32) + jnp.dot(mixed_ref[...], held[0], preferred_element_type=jnp.float32)
    middle_ref[...] = middle
    normed_ref[...] = layer_norm(middle, gain_ref[...]).astype(normed_ref.dtype)

    @pl.when(at == pl.num_programs(0) - 1)
    def _():
        store.wait()


def branch(place, x, mixed, gain, pieces):
    n = place.shape[0]
    tokens, width = x.shape
    rows = width // n
    tile = 256
    anywhere = pl.BlockSpec(memory_space=pl.ANY)
    strip = pl.BlockSpec((tile, width), lambda i, *_: (i, 0))
    return pl.pallas_call(
        functools.partial(branch_kernel, n, rows),
        grid_spec=pltpu.PrefetchScalarGridSpec(
            num_scalar_prefetch=1,
            grid=(tokens // tile,),
            in_specs=[strip, strip, pl.BlockSpec((1, width), lambda i, *_: (0, 0))] + [anywhere] * 4,
            out_specs=[strip, strip, anywhere],
            scratch_shapes=[
                pltpu.VMEM((1, width, width), jnp.bfloat16),
                pltpu.SemaphoreType.DMA((n,)),
                pltpu.SemaphoreType.DMA((1,)),
            ],
        ),
        out_shape=[
            jax.ShapeDtypeStruct((tokens, width), jnp.float32),
            jax.ShapeDtypeStruct((tokens, width), jnp.bfloat16),
            jax.ShapeDtypeStruct((width, width), jnp.bfloat16),
        ],
        compiler_params=pltpu.CompilerParams(vmem_limit_bytes=VMEM_LIMIT),
        cost_estimate=LIGHT,
        name="branch",
    )(place, x, mixed, gain, *pieces)


def weight_grad_kernel(n, rows, lefts, rights, place_ref, *refs):
    count = sum(map(len, lefts)) + sum(map(len, rights))
    sources = list(refs[:count])
    keep_ref, send_ref, x_v, g_v, turned, held, sems = refs[count:]
    at = pl.program_id(0)
    loads = []
    for sizes, target in [(s, x_v.at[i]) for i, s in enumerate(lefts)] + [(s, g_v.at[i]) for i, s in enumerate(rights)]:
        first, copies = 0, []
        for size in sizes:
            src = sources.pop(0).at[pl.ds(0, size)]
            copies.append(pltpu.make_async_copy(src, target.at[pl.ds(first, size)], sems.at[count - len(sources) - 1]))
            first += size
        loads.append(copies)

    @pl.when(at == 0)
    def _():
        for copies in loads:
            for copy in copies:
                copy.start()

    for i in range(len(rights)):
        @pl.when(at == i)
        def _(i=i):
            if i < len(lefts):
                for copy in loads[i]:
                    copy.wait()
                turned[...] = x_v[i].T
            for copy in loads[len(lefts) + i]:
                copy.wait()

    held[...] = jnp.dot(turned[...], g_v[at], preferred_element_type=jnp.float32).astype(held.dtype)
    for position in range(n):
        first = pl.multiple_of(place_ref[position] * rows, rows)
        target = keep_ref if position < n // 2 else send_ref
        target[position % (n // 2)] = held[pl.ds(first, rows), :]


def weight_grad(place, x, g):
    n = place.shape[0]
    width = g[0][0].shape[1]
    parts = len(g)
    rows = width // n
    rights = [[v.shape[0] for v in part] for part in g]
    lefts = [[v.shape[0] for v in part] for part in x]
    tokens = sum(rights[0])
    for sizes in lefts:
        sizes[-1] -= sum(sizes) - tokens
    half = pl.BlockSpec((n // 2, rows, width), lambda i, *_: (0, i, 0))
    anywhere = pl.BlockSpec(memory_space=pl.ANY)
    operands = [v for part in x + g for v in part]
    return pl.pallas_call(
        functools.partial(weight_grad_kernel, n, rows, lefts, rights),
        grid_spec=pltpu.PrefetchScalarGridSpec(
            num_scalar_prefetch=1,
            grid=(parts,),
            in_specs=[anywhere] * len(operands),
            out_specs=[half, half],
            scratch_shapes=[
                pltpu.VMEM((len(x), tokens, width), jnp.bfloat16),
                pltpu.VMEM((parts, tokens, width), jnp.bfloat16),
                pltpu.VMEM((width, tokens), jnp.bfloat16),
                pltpu.VMEM((width, width), jnp.bfloat16),
                pltpu.SemaphoreType.DMA((len(operands),)),
            ],
        ),
        out_shape=[jax.ShapeDtypeStruct((n // 2, parts * rows, width), jnp.bfloat16)] * 2,
        compiler_params=pltpu.CompilerParams(vmem_limit_bytes=VMEM_LIMIT),
        cost_estimate=LIGHT,
        name="weight_grad",
    )(place, *operands)


def norm_back(values, gain, grad):
    centered = values - jnp.mean(values, axis=-1, keepdims=True)
    scale = lax.rsqrt(jnp.mean(centered * centered, axis=-1, keepdims=True) + 1e-05)
    unit = centered * scale
    inner = grad * gain
    back = scale * (
        inner - jnp.mean(inner, axis=-1, keepdims=True) - unit * jnp.mean(inner * unit, axis=-1, keepdims=True)
    )
    return back, grad * unit


def middle_back_kernel(middle_ref, own0, own1, came0, came1, cot_ref, gain_ref, weights_ref, grad_ref, low_ref, mixed_ref, gain_out):
    f32, bf = jnp.float32, jnp.bfloat16
    grad = own0[...] + own1[...] + (came0[...].astype(f32) + came1[...].astype(f32))
    back, by_gain = norm_back(middle_ref[...], gain_ref[...], grad)
    back = back + cot_ref[...].astype(f32)
    low = back.astype(bf)
    grad_ref[...] = back
    low_ref[...] = low
    mixed_ref[...] = lax.dot_general(low, weights_ref[...], NT, preferred_element_type=f32).astype(bf)

    @pl.when(pl.program_id(0) == 0)
    def _():
        gain_out[...] = jnp.zeros_like(gain_out)

    gain_out[...] += jnp.sum(by_gain, axis=0, keepdims=True)


def middle_back(middle, own, came, cot, gain, weights):
    tokens, width = middle.shape
    tile = 256
    strip = pl.BlockSpec((tile, width), lambda i: (i, 0))
    line = pl.BlockSpec((1, width), lambda i: (0, 0))
    shape = lambda rows, kind: jax.ShapeDtypeStruct((rows, width), kind)
    return pl.pallas_call(
        middle_back_kernel,
        grid=(tokens // tile,),
        in_specs=[strip] * 6 + [line, pl.BlockSpec((width, width), lambda i: (0, 0))],
        out_specs=[strip, strip, strip, line],
        out_shape=[shape(tokens, jnp.float32), shape(tokens, jnp.bfloat16), shape(tokens, jnp.bfloat16), shape(1, jnp.float32)],
        compiler_params=pltpu.CompilerParams(vmem_limit_bytes=VMEM_LIMIT),
        cost_estimate=LIGHT,
        name="middle_back",
    )(middle, *own, *came, cot, gain, weights)


def input_back_kernel(counts, tile, came_tiles, x_ref, ssm_ref, middle_ref, came_ref, gain_ref, *refs):
    total = sum(map(len, counts))
    sources = list(refs[:total])
    weights_ref, grad_ref, gain_out, g_v, weights_v, sems = refs[total:]
    at = pl.program_id(0)
    f32 = jnp.float32

    @pl.when(at == 0)
    def _():
        copies = [pltpu.make_async_copy(weights_ref, weights_v, sems.at[total])]
        left = list(sources)
        for i, sizes in enumerate(counts):
            first = 0
            for size in sizes:
                copies.append(pltpu.make_async_copy(left.pop(0), g_v.at[i, pl.ds(first, size)], sems.at[total - len(left) - 1]))
                first += size
        for copy in copies:
            copy.start()
        gain_out[...] = jnp.zeros_like(gain_out)
        for copy in copies:
            copy.wait()

    rows = pl.ds(pl.multiple_of(at * tile, tile), tile)
    grad = ssm_ref[...]
    for i in range(len(counts)):
        grad += lax.dot_general(g_v[i, rows, :], weights_v[i], NT, preferred_element_type=f32)
    grad += jnp.where(at >= pl.num_programs(0) - came_tiles, 1.0, 0.0) * came_ref[...].astype(f32)
    back, by_gain = norm_back(x_ref[...].astype(f32), gain_ref[...], grad)
    grad_ref[...] = back + middle_ref[...]
    gain_out[...] += jnp.sum(by_gain, axis=0, keepdims=True)


def input_back(x, ssm, middle, came, gain, g, weights):
    tokens, width = x.shape
    tile = 256
    counts = [[v.shape[0] for v in part] for part in g]
    tiles = tokens // tile
    came_tiles = BLOCK // tile
    operands = [v for part in g for v in part]
    strip = pl.BlockSpec((tile, width), lambda i: (i, 0))
    line = pl.BlockSpec((1, width), lambda i: (0, 0))
    anywhere = pl.BlockSpec(memory_space=pl.ANY)
    came_strip = pl.BlockSpec((tile, width), lambda i: (jnp.maximum(i - (tiles - came_tiles), 0), 0))
    return pl.pallas_call(
        functools.partial(input_back_kernel, counts, tile, came_tiles),
        grid=(tiles,),
        in_specs=[strip, strip, strip, came_strip, line] + [anywhere] * (len(operands) + 1),
        out_specs=[strip, line],
        out_shape=[jax.ShapeDtypeStruct((tokens, width), jnp.float32), jax.ShapeDtypeStruct((1, width), jnp.float32)],
        scratch_shapes=[
            pltpu.VMEM((len(g), tokens, width), jnp.bfloat16),
            pltpu.VMEM(weights.shape, jnp.bfloat16),
            pltpu.SemaphoreType.DMA((len(operands) + 1,)),
        ],
        compiler_params=pltpu.CompilerParams(vmem_limit_bytes=VMEM_LIMIT),
        cost_estimate=LIGHT,
        name="input_back",
    )(x, ssm, middle, came, gain, *operands, weights)


def ff_kernel(n, tiles, table_ref, n2_ref, n2s_ref, cot_ref, cots_ref, *rest):
    (mine_low, mine_high, theirs_low, theirs_high, out_ref, gn2_ref, outs_ref, gn2s_ref, mine_ref, theirs_ref,
     n2_v, n2t_v, cot_v, weights_v, out_v, gn2_v, low_v, pack_v, sems, load_sems, store_sems) = rest
    f32, bf = jnp.float32, jnp.bfloat16
    t = pl.program_id(0)
    hidden = width = n2_ref.shape[1]
    rows, span = width // n, hidden // tiles
    half_rows = pack_v.shape[1] // 2
    side = table_ref[2 * n]
    kinds = (side, 1 - side)

    def pieces(refs, which):
        copies = []
        for position in range(n):
            src = refs[position // (n // 2)]
            skip = src.shape[1] - 2 * rows
            src = src.at[position % (n // 2) // 2, pl.ds(skip + position % 2 * rows, rows)]
            first = pl.multiple_of(table_ref[kinds[which] * n + position] * rows, rows)
            copies.append(pltpu.make_async_copy(
                src, weights_v.at[kinds[which], pl.ds(first, rows)], load_sems.at[which * n + position]))
        return copies

    @pl.when(t == 0)
    def _():
        weights = pieces((mine_low, mine_high), 0) + pieces((theirs_low, theirs_high), 1)
        first = [pltpu.make_async_copy(n2_ref, n2_v.at[0], sems.at[0]), pltpu.make_async_copy(n2s_ref, n2_v.at[1], sems.at[1])]
        second = [pltpu.make_async_copy(cot_ref, cot_v.at[0], sems.at[2]), pltpu.make_async_copy(cots_ref, cot_v.at[1], sems.at[3])]
        for copy in first + weights + second:
            copy.start()
        out_v[...] = jnp.zeros_like(out_v)
        gn2_v[...] = jnp.zeros_like(gn2_v)
        for copy in first:
            copy.wait()
        for at in range(2):
            n2t_v[at] = n2_v[at].T
        for copy in weights + second:
            copy.wait()

    cols = pl.ds(pl.multiple_of(t * span, span), span)
    up = weights_v[0, :, cols]
    down = weights_v[1, cols, :]
    gup = gdown = 0.0
    for at in range(2):
        cot = cot_v[at]
        hid = jnp.dot(n2_v[at], up, preferred_element_type=f32)
        gact = lax.dot_general(cot, down, NT, preferred_element_type=f32)
        sq = hid * hid
        th = jnp.tanh(GC * hid * (1.0 + GQ * sq))
        half = 0.5 * (1.0 + th)
        act = (hid * half).astype(bf)
        slope = half + (0.5 * GC) * hid * (1.0 - th * th) * (1.0 + (3.0 * GQ) * sq)
        gh = (gact * slope).astype(bf)
        out_v[at] += jnp.dot(act, down, preferred_element_type=f32)
        gn2_v[at] += lax.dot_general(gh, up, NT, preferred_element_type=f32)
        gdown += lax.dot_general(act, cot, TN, preferred_element_type=f32)
        gup += jnp.dot(n2t_v[at], gh, preferred_element_type=f32)
    results = [
        pltpu.make_async_copy(out_v.at[0], out_ref, sems.at[0]),
        pltpu.make_async_copy(gn2_v.at[0], gn2_ref, sems.at[1]),
        pltpu.make_async_copy(low_v.at[0], gn2s_ref, sems.at[2]),
        pltpu.make_async_copy(low_v.at[1], outs_ref, sems.at[3]),
    ]

    @pl.when(t == tiles - 1)
    def _():
        for copy in results[:2]:
            copy.start()
        low_v[0] = gn2_v[1].astype(bf)
        low_v[1] = out_v[1].astype(bf)
        for copy in results[2:]:
            copy.start()

    gup = gup.astype(bf)
    gdown = gdown.astype(bf)
    groups = span // 128
    for d in range(n):
        for g in range(groups):
            first = pl.multiple_of((t * groups + g) * rows, rows)
            pack_v[d, pl.ds(first, rows), :] = gup[d * rows : (d + 1) * rows, g * 128 : (g + 1) * 128]
    slots = span // rows
    for o in range(slots):
        for g in range(width // 128):
            first = half_rows + g * rows
            pack_v[t * slots + o, first : first + rows, :] = gdown[o * rows : (o + 1) * rows, g * 128 : (g + 1) * 128]

    @pl.when(t == tiles - 1)
    def _():
        copies = []
        for which, ref in enumerate((mine_ref, theirs_ref)):
            for position in range(n):
                slot = table_ref[kinds[which] * n + position]
                src = pack_v.at[slot, pl.ds(pl.multiple_of(kinds[which] * half_rows, half_rows), half_rows)]
                copies.append(pltpu.make_async_copy(src, ref.at[position], store_sems.at[which * n + position]))
        for copy in copies:
            copy.start()
        for copy in copies + results:
            copy.wait()


def feed_forward(table, n2, n2_other, cot, cot_other, mine, theirs, tiles):
    n = (table.shape[0] - 1) // 2
    tokens, width = n2.shape
    rows = width // n
    half_rows = width // 128 * rows
    bf, f32 = jnp.bfloat16, jnp.float32
    anywhere = pl.BlockSpec(memory_space=pl.ANY)
    shape = jax.ShapeDtypeStruct
    return pl.pallas_call(
        functools.partial(ff_kernel, n, tiles),
        grid_spec=pltpu.PrefetchScalarGridSpec(
            num_scalar_prefetch=1,
            grid=(tiles,),
            in_specs=[anywhere] * 8,
            out_specs=[anywhere] * 6,
            scratch_shapes=[
                pltpu.VMEM((2, tokens, width), bf),
                pltpu.VMEM((2, width, tokens), bf),
                pltpu.VMEM((2, tokens, width), bf),
                pltpu.VMEM((2, width, width), bf),
                pltpu.VMEM((2, tokens, width), f32),
                pltpu.VMEM((2, tokens, width), f32),
                pltpu.VMEM((2, tokens, width), bf),
                pltpu.VMEM((n, 2 * half_rows, 128), bf),
                pltpu.SemaphoreType.DMA((4,)),
                pltpu.SemaphoreType.DMA((2 * n,)),
                pltpu.SemaphoreType.DMA((2 * n,)),
            ],
        ),
        out_shape=[shape((tokens, width), f32)] * 2 + [shape((tokens, width), bf)] * 2 + [shape((n, half_rows, 128), bf)] * 2,
        compiler_params=pltpu.CompilerParams(vmem_limit_bytes=VMEM_LIMIT),
        cost_estimate=pl.CostEstimate(flops=24 * tokens * width * width, bytes_accessed=32 << 20, transcendentals=2 * tokens * width),
        name="feed_forward",
    )(table, n2, n2_other, cot, cot_other, *mine, *theirs)


def causal(rows, cols, first):
    r = lax.broadcasted_iota(jnp.int32, (rows, cols), 0) + first
    c = lax.broadcasted_iota(jnp.int32, (rows, cols), 1)
    return c <= r

def attend_forward_kernel(flag_ref, q_ref, kc_ref, kp_ref, ko_ref, vc_ref, vp_ref, vo_ref, mixed_ref, total_ref):
    scale = HEAD_DIM ** -0.5
    f32 = jnp.float32
    def tile(at, earlier):
        rows = pl.ds(at * TILE, TILE)
        own = (at + 1) * TILE
        q = q_ref[rows, :]
        so = lax.dot_general(q, ko_ref[:own, :], NT, preferred_element_type=f32)
        so = jnp.where(causal(TILE, own, at * TILE), so, -1e30)
        parts = [so]
        values = [vo_ref[:own, :]]
        if earlier:
            parts = [lax.dot_general(q, kc_ref[...], NT, preferred_element_type=f32), lax.dot_general(q, kp_ref[...], NT, preferred_element_type=f32)] + parts
            values = [vc_ref[...], vp_ref[...]] + values
        top = functools.reduce(jnp.maximum, [jnp.max(s, axis=-1, keepdims=True) for s in parts])
        shift = top * (scale * LOG2E)
        soft = [jnp.exp2(s * (scale * LOG2E) - shift) for s in parts]
        total = sum(jnp.sum(s, axis=-1, keepdims=True) for s in soft)
        mixed = sum(jnp.dot(s.astype(jnp.bfloat16), v, preferred_element_type=f32) for s, v in zip(soft, values))
        mixed_ref[rows, :] = (mixed * (1.0 / total)).astype(mixed_ref.dtype)
        total_ref[0, rows, :] = shift + jnp.log2(total)
    flagged = flag_ref[0] > 0
    for at in range(BLOCK // TILE):
        pl.when(flagged)(functools.partial(tile, at, False))
        pl.when(jnp.logical_not(flagged))(functools.partial(tile, at, True))

def head_spec(rows, row_at=0, lead=None):
    if lead is None:
        return pl.BlockSpec((rows, HEAD_DIM), lambda h, *_: (row_at, h))
    return pl.BlockSpec((None, rows, HEAD_DIM), lambda h, *_: (lead, row_at, h))

def attend_forward(flag, query, key_ctx, key_prev, key_own, value_ctx, value_prev, value_own):
    ops=[query,key_ctx,key_prev,key_own,value_ctx,value_prev,value_own]
    sizes=[BLOCK,CTX,BLOCK,BLOCK,CTX,BLOCK,BLOCK]
    return pl.pallas_call(
        attend_forward_kernel,
        grid_spec=pltpu.PrefetchScalarGridSpec(num_scalar_prefetch=1, grid=(HEADS,),
            in_specs=[head_spec(s, o[1], o[2] if len(o) > 2 else None) for o, s in zip(ops, sizes)],
            out_specs=[head_spec(BLOCK), pl.BlockSpec((1, BLOCK, 1), lambda h, *_: (h, 0, 0))]),
        out_shape=[jax.ShapeDtypeStruct((BLOCK, HEADS * HEAD_DIM), jnp.bfloat16), jax.ShapeDtypeStruct((HEADS, BLOCK, 1), jnp.float32)],
        compiler_params=pltpu.CompilerParams(vmem_limit_bytes=VMEM_LIMIT),
        cost_estimate=LIGHT,
        name="attend_forward",
    )(flag, *[o[0] for o in ops])

def attend_backward_kernel(merge, flag_ref, q_ref, kc_ref, kp_ref, ko_ref, vc_ref, vp_ref, vo_ref, total_ref, g_ref, mixed_ref, *rest):
    scale = HEAD_DIM ** -0.5
    f32, bf = jnp.float32, jnp.bfloat16
    if merge:
        kadd_ref, vadd_ref, dq_ref, dkc_ref, dkp_ref, dko_ref, dvc_ref, dvp_ref, dvo_ref, acc_k, acc_v = rest
    else:
        dq_ref, dkc_ref, dkp_ref, dko_ref, dvc_ref, dvp_ref, dvo_ref, acc_k, acc_v = rest
    lead = CTX + BLOCK
    acc_k[...] = jnp.zeros_like(acc_k)
    acc_v[...] = jnp.zeros_like(acc_v)
    def tile(at, earlier):
        rows = pl.ds(at * TILE, TILE)
        own = (at + 1) * TILE
        q = q_ref[rows, :]
        g = g_ref[rows, :]
        total = total_ref[0, rows, :]
        keys = [(ko_ref[:own, :], vo_ref[:own, :], lead, own)]
        if earlier:
            keys = [(kc_ref[...], vc_ref[...], 0, CTX), (kp_ref[...], vp_ref[...], CTX, BLOCK)] + keys
        softs, grads = [], []
        for k, v, first, size in keys:
            s = lax.dot_general(q, k, NT, preferred_element_type=f32)
            s = s * (scale * LOG2E) - total
            if first == lead:
                s = jnp.where(causal(TILE, own, at * TILE), s, -1e30)
            softs.append(jnp.exp2(s))
            grads.append(lax.dot_general(g, v, NT, preferred_element_type=f32))
        rowsum = jnp.sum(mixed_ref[rows, :].astype(f32) * g.astype(f32), axis=-1, keepdims=True)
        dq = 0.0
        for (k, v, first, size), p, d in zip(keys, softs, grads):
            ds = (p * (d - rowsum)).astype(bf)
            dq += jnp.dot(ds, k, preferred_element_type=f32)
            at_rows = pl.ds(first, size)
            acc_k[at_rows, :] += lax.dot_general(ds, q, TN, preferred_element_type=f32)
            acc_v[at_rows, :] += lax.dot_general(p.astype(bf), g, TN, preferred_element_type=f32)
        dq_ref[rows, :] = (dq * scale).astype(dq_ref.dtype)
    flagged = flag_ref[0] > 0
    for at in range(BLOCK // TILE):
        pl.when(flagged)(functools.partial(tile, at, False))
        pl.when(jnp.logical_not(flagged))(functools.partial(tile, at, True))
    more_k = kadd_ref[...] if merge else 0.0
    more_v = vadd_ref[...] if merge else 0.0
    dkc_ref[...] = (acc_k[:CTX, :] * scale).astype(dkc_ref.dtype)
    dvc_ref[...] = acc_v[:CTX, :].astype(dvc_ref.dtype)
    dkp_ref[...] = (acc_k[CTX:lead, :] * scale + more_k).astype(dkp_ref.dtype)
    dvp_ref[...] = (acc_v[CTX:lead, :] + more_v).astype(dvp_ref.dtype)
    dko_ref[...] = (acc_k[lead:, :] * scale).astype(dko_ref.dtype)
    dvo_ref[...] = acc_v[lead:, :].astype(dvo_ref.dtype)

def attend_backward(flag, query, key_ctx, key_prev, key_own, value_ctx, value_prev, value_own, total, grad, mixed, add=None, final=False):
    ops=[query,key_ctx,key_prev,key_own,value_ctx,value_prev,value_own]
    sizes=[BLOCK,CTX,BLOCK,BLOCK,CTX,BLOCK,BLOCK]
    specs=[head_spec(s, o[1], o[2] if len(o) > 2 else None) for o, s in zip(ops, sizes)]
    specs+=[pl.BlockSpec((1, BLOCK, 1), lambda h, *_: (h, 0, 0)), head_spec(BLOCK, grad[1]), head_spec(BLOCK, mixed[1])]
    args=[o[0] for o in ops]+[total, grad[0], mixed[0]]
    if add is not None:
        specs+=[head_spec(BLOCK)]*2
        args+=list(add)
    width=HEADS*HEAD_DIM
    bf,f32=jnp.bfloat16,jnp.float32
    own = bf if final else f32
    out=lambda r,t: jax.ShapeDtypeStruct((r,width),t)
    return pl.pallas_call(
        functools.partial(attend_backward_kernel, add is not None),
        grid_spec=pltpu.PrefetchScalarGridSpec(num_scalar_prefetch=1, grid=(HEADS,),
            in_specs=specs,
            out_specs=[head_spec(BLOCK), head_spec(CTX), head_spec(BLOCK), head_spec(BLOCK), head_spec(CTX), head_spec(BLOCK), head_spec(BLOCK)],
            scratch_shapes=[pltpu.VMEM((CTX+2*BLOCK,HEAD_DIM),f32)]*2),
        out_shape=[out(BLOCK,bf), out(CTX,bf), out(BLOCK,bf), out(BLOCK,own), out(CTX,bf), out(BLOCK,bf), out(BLOCK,own)],
        compiler_params=pltpu.CompilerParams(vmem_limit_bytes=VMEM_LIMIT),
        cost_estimate=LIGHT,
        name="attend_backward",
    )(flag, *args)


def adamw_step(weight, first, second, gradient, step_rate, shrink):
    new_first = 0.9 * first + 0.1 * gradient
    new_second = 0.95 * second + 0.05 * gradient * gradient
    scaled_first = new_first / (1.0 - 0.9**STEP)
    scaled_second = new_second / (1.0 - 0.95**STEP)
    update = scaled_first / (jnp.sqrt(scaled_second) + 1e-08) + shrink * weight
    return (new_first, new_second, weight - step_rate * update)


def body(
    tokens,
    cotangent,
    carry_in,
    block_flags,
    qkv_w,
    qkv_m,
    qkv_v,
    out_w,
    out_m,
    out_v,
    up_w,
    up_m,
    up_v,
    down_w,
    down_m,
    down_v,
    gain_w,
    gain_m,
    gain_v,
    ssm_w,
    ssm_m,
    ssm_v,
):
    low_type = jnp.bfloat16
    n = lax.axis_size("blk")
    width = tokens.shape[-1]
    rows = width // n
    span = FF // n // 2
    far = far_masks(n)
    place = places(far + [2, 1])
    ff_place = places([1] + far + [2])
    side = lax.axis_index("win") & 1
    slots = 2 * (ff_place // 2) + jnp.arange(n, dtype=jnp.int32) % 2
    ff_table = jnp.concatenate([ff_place, slots, side[None].astype(jnp.int32)])
    upper_core = (lax.axis_index("blk") & 1) != 0


    small = jnp.concatenate([gain_w, ssm_w.reshape(-1, ssm_w.shape[-1])], axis=0)
    small = gather_round(small, n // 2)
    qkv_half = qkv_w.astype(low_type).reshape(3, 2, rows // 2, width)
    held = jnp.where(side == 1, qkv_half[:, 1], qkv_half[:, 0])[None]
    for mask in far[:-1]:
        held = widen(held, mask)
    mask = n // 4
    while mask > 2:
        small = gather_round(small, mask)
        mask //= 2
    own_half, other_half = pack_halves(upper_core, *tie((up_w, down_w), small), n)
    small = gather_round(tie(small, held), 2)
    small = gather_round(small, 1)
    small = joined_columns(small)
    near = widen(held, far[-1])
    across = swap(near, "blk", 2)
    near_y = swap(near, "win", 1)
    near_c = swap(near, "blk", 1)

    small = tie(small, near)
    gain_all, ssm_all = small[:2], small[2:].reshape(ssm_w.shape[:2] + (width,))
    inputs = tokens[0].astype(jnp.float32)
    flags = block_flags[0]
    markers = flags.astype(jnp.float32)
    carried = carry_in[0]
    block_count = markers.shape[0]
    last = block_count - 1
    forward_pairs = [(at, at + 1) for at in range(n - 1)]
    normed = layer_norm(inputs, gain_all[0])
    normed_low = normed.astype(low_type)
    rate = jnp.exp(ssm_all[0])
    decay = jnp.exp(-rate)
    root = jnp.sqrt(-jnp.expm1(-2.0 * rate))
    beta = root * ssm_all[1]
    over_block = jnp.exp(-rate * BLOCK)
    through = jnp.prod(1.0 - markers) * jnp.exp(-rate * (block_count * BLOCK))
    came_half = swap(other_half, "blk", 1)
    cot = cotangent[0]
    cot_other = swap(cot, "blk", 1)

    def chunk(c):
        ups = [own_half[c * rows : (c + 1) * rows], came_half[c * rows : (c + 1) * rows]]
        is_own = upper_core == (c == 1)
        down = jnp.where(is_own, own_half[2 * rows :], came_half[2 * rows :])
        return jnp.where(side == 1, down, jnp.concatenate(ups, axis=0))

    first = jnp.concatenate([out_w.astype(low_type), chunk(0)], axis=0)[None]
    second = chunk(1)[None]
    first_came = swap(tie(first, near), "blk", far[0])
    base_ctx, middles, slopes, ends = scan_states(tie(normed, near, first), decay, ssm_all[2] * beta)
    nothing = jnp.zeros_like(rate)
    _, local_end = state_ahead(nothing, markers, carried, beta * tie(ends, first_came, near_y), over_block)
    across = tie(across, ends)
    across_y = swap(across, "win", 1)
    across_c = swap(across, "blk", 1)
    near_yc = swap(near_y, "blk", 1)
    scan = CarriedIn(through, tie(local_end, across), False)
    scan.step()
    scan.step()
    sent = tie(normed_low[-BLOCK:], scan.total)
    came_normed = lax.ppermute(sent, "blk", forward_pairs)
    while scan.mask < n:
        scan.step()
    entering = scan.ahead[1]
    first = jnp.concatenate([first, tie(first_came, entering)], axis=0)
    for mask in far[1:-1]:
        first = widen(first, mask)
    first_came = swap(first, "blk", far[-1])
    begins, _ = state_ahead(tie(entering, across_y, came_normed), markers, carried, beta * ends, over_block)
    contexts_low = finish_contexts(base_ctx, rate, ssm_all[2] * begins).reshape(-1, width)
    came_ctx = lax.ppermute(contexts_low[-CTX:], "blk", forward_pairs)
    across_yc = swap(tie(across_y, contexts_low), "blk", 1)
    table = jnp.concatenate([place, jnp.stack([side, 1 - side]).astype(jnp.int32) * (rows // 2)])
    projected, extra_pair, qkv_all = project(
        table,
        tie(normed_low, contexts_low),
        [came_normed, contexts_low],
        [near, across, near_c, across_c],
        [near_y, across_y, near_yc, across_yc],
    )
    to_pair = lambda v: jnp.einsum("td,kde->kte", v, qkv_all[1:], preferred_element_type=jnp.float32).astype(low_type)
    first_came = tie(first_came, projected, came_ctx)
    first = jnp.concatenate([first, first_came], axis=0)

    first_x = swap(first, "blk", 2)
    out_near_c = swap(first[:, :rows], "blk", 1)
    near_half = first[:, rows:]
    theirs0 = [swap(near_half, "win", 1)]
    second = tie(second, first)
    second_came = swap(second, "blk", far[0])
    context_rows = BLOCK // CTX

    def lists(at):
        own = [(projected, at, 1), (projected, at, 2)]
        if at:
            ctx_at = context_rows + at - 1
            earlier = [(extra_pair, ctx_at, 0), (projected, at - 1, 1), (extra_pair, ctx_at, 1), (projected, at - 1, 2)]
        else:
            earlier = [(came_pair, 0, 0), (extra_pair, 0, 0), (came_pair, 0, 1), (extra_pair, 0, 1)]
        return [(projected, at, 0), earlier[0], earlier[1], own[0], earlier[2], earlier[3], own[1]]

    attended = {}
    came_pair = None
    place_flags = tie(flags, first, near_half)
    for at in range(block_count)[::-1]:
        attended[at] = attend_forward(place_flags[at : at + 1], *lists(at))
        if at == last:
            second = jnp.concatenate([second, tie(second_came, attended[at][0])], axis=0)
            for mask in far[1:-1]:
                second = widen(second, mask)
            second_came = swap(second, "blk", far[-1])
            place_flags = tie(flags, second)
            came_pair = to_pair(tie(came_ctx, attended[at][0]))
    mixed_low = jnp.concatenate([attended[at][0] for at in range(block_count)], axis=0)
    totals = [attended[at][1] for at in range(block_count)]
    first_x = tie(first_x, mixed_low)
    out_across_c = swap(first_x[:, :rows], "blk", 1)
    theirs0.append(swap(first_x[:, rows:], "win", 1))
    second = jnp.concatenate([second, tie(second_came, mixed_low)], axis=0)
    second_x = swap(second, "blk", 2)
    theirs1 = [swap(tie(second, theirs0[1]), "win", 1)]
    middle, normed_two_low, out_all = branch(
        place, tokens[0], tie(mixed_low, second, theirs0[0]), gain_all[1:], [first, first_x, out_near_c, out_across_c]
    )
    normed_two_low = tie(normed_two_low, theirs0[1], second_x)
    n2_other = swap(normed_two_low, "blk", 1)
    theirs1.append(swap(second_x, "win", 1))
    ff = [feed_forward(ff_table, normed_two_low, n2_other, cot, cot_other, [first, first_x], theirs0, TILES)]
    keep0, send0 = ff[0][4:]
    came0 = swap(send0, "win", 1)
    backs = [swap(ff[0][3], "blk", 1), swap(ff[0][2], "blk", 1)]
    ff.append(feed_forward(ff_table, tie(normed_two_low, send0, ff[0][3]), n2_other, cot, cot_other, [second, second_x], theirs1, TILES))
    keep1, send1 = ff[1][4:]
    came1 = swap(tie(send1, came0), "win", 1)
    keep0, came0 = tie((keep0, came0), keep1)
    keep0, send0 = fold(keep0, came0)
    came0 = swap(send0, "blk", 2)
    own_grad, other_grad, other_out = tie((ff[1][1], ff[1][3], ff[1][2]), send0)
    backs += [swap(other_grad, "blk", 1), swap(other_out, "blk", 1)]
    f32 = jnp.float32
    grad_middle, grad_branch, grad_mixed, grad_gain_two = middle_back(
        middle, [ff[0][1], own_grad], [backs[0], backs[2]], cot, gain_all[1:], out_all
    )
    back_dot = lambda a, b: lax.dot_general(a, b, NT, preferred_element_type=jnp.float32)
    grads = []
    for at in range(block_count):
        add = (grads[-1][3], grads[-1][6]) if at else None
        query, *others = lists(at)
        if at:
            grad_mixed = tie(grad_mixed, grads[-1][0])
        grads.append(attend_backward(flags[at : at + 1], query, *others, totals[at], (grad_mixed, at), (mixed_low, at), add, at == last))
        if not at:
            earlier_k = jnp.concatenate([grads[0][2], grads[0][1]], axis=0)
            earlier_v = jnp.concatenate([grads[0][5], grads[0][4]], axis=0)
            sent_back = (back_dot(earlier_k, qkv_all[1]) + back_dot(earlier_v, qkv_all[2])).astype(low_type)
            came_back = lax.ppermute(sent_back, "blk", [(at + 1, at) for at in range(n - 1)])
            keep1, came1 = tie((keep1, came1), grads[0][0])
            keep1, send1 = fold(keep1, came1)
            came1 = swap(send1, "blk", 2)
            keep0, came0 = tie((keep0, came0), send1)
            for mask in far[1:][::-1]:
                keep0, send0 = fold(keep0, came0)
                came0 = swap(send0, "blk", mask)
            grad_mixed = tie(grad_mixed, send0, send1, sent_back)
    later = range(1, block_count)
    own_contexts = jnp.concatenate(
        [back_dot(grads[at][1], qkv_all[1]) + back_dot(grads[at][4], qkv_all[2]) for at in later], axis=0
    )
    grad_contexts = jnp.concatenate([own_contexts, came_back[BLOCK:].astype(f32)], axis=0).reshape(block_count, CTX, width)
    sums = adjoint_sums(grad_contexts, decay)
    local_starts = jnp.exp(-rate * (BEFORE + 1)) * ssm_all[2] * sums
    _, _, leaving_own = adjoint_behind(nothing, markers, local_starts, over_block)
    scan = CarriedIn(through, leaving_own, True)
    scan.step()
    started = scan.total
    q_grads = [part[0] for part in grads]
    kv_grads = [
        [grads[at][own - 1] for at in later] + [grads[last][own], grads[0][own - 1]]
        + [grads[at][own - 2] for at in range(block_count)]
        for own in (3, 6)
    ]
    keep0, came0, keep1, came1 = tie((keep0, came0, keep1, came1), sums)
    for mask in far[:1]:
        keep0, send0 = fold(keep0, came0)
        came0 = swap(send0, "blk", mask)
    keep1, send1 = fold(keep1, came1)
    came1 = swap(tie(send1, send0), "blk", far[-1])
    keep2, send2 = weight_grad(place, [[tie(mixed_low, started, send0, send1)], [normed_low]], [[grad_branch], q_grads])
    came2 = swap(send2, "blk", 1)
    scan.step(keep2)
    keep1, came1, came0 = tie((keep1, came1, came0), keep2)
    sum0 = sum_over_win(add_low(keep0, came0), 2)
    for mask in far[:-1][::-1]:
        keep1, send1 = fold(keep1, came1)
        came1 = swap(send1, "blk", mask)
    kv_left = tie(normed_low, scan.total, send1, send2, sum0)
    keep3, send3 = weight_grad(place, [[kv_left, came_normed, came_ctx, contexts_low]], kv_grads)
    came3 = swap(send3, "blk", 1)
    scan.step(keep3)
    whole2 = add_low(keep2, tie(came2, keep3, scan.total))
    keep2 = jnp.where(side == 1, whole2[:, rows:], whole2[:, :rows])
    send2 = jnp.where(side == 1, whole2[:, :rows], whole2[:, rows:])
    came2 = swap(send2, "win", 1)
    keep3, send3 = fold(keep3, tie(came3, send2))
    came3 = swap(send3, "blk", 2)
    while scan.mask < n:
        scan.step(send3)
    leaving = tie(scan.ahead[1], send2, send3)
    enters, starts, _ = adjoint_behind(leaving, markers, local_starts, over_block)
    grad_carried = markers[:, None, None] * starts
    at_context = beta * middles + jnp.exp(-rate * BEFORE) * begins
    grad_normed_ssm, grad_mix, grad_beta, grad_decay, passed = back_states(
        normed, grad_contexts, at_context, enters, rate, decay, beta, ssm_all[2]
    )
    came1, came2, came3, grad_normed_ssm = tie((came1, came2, came3, grad_normed_ssm))
    keep2, send2 = fold(keep2, came2)
    came2 = swap(send2, "blk", 2)
    keep3, send3 = fold(keep3, tie(came3, send2))
    came3 = swap(send3, "blk", far[-1])
    sum1 = sum_over_win(add_low(keep1, tie(came1, send3)), 2)
    mine_ff = jnp.stack([sum0, sum1])
    theirs_ff = swap(mine_ff, "win", 1)
    grad_tokens, grad_gain_one = input_back(
        tokens[0],
        tie(grad_normed_ssm, send2, send3, mine_ff),
        grad_middle,
        came_back,
        gain_all[:1],
        [q_grads] + [part[:block_count] for part in kv_grads],
        qkv_all,
    )
    keep2, send2 = fold(keep2, tie(came2, grad_tokens))
    came2 = swap(send2, "blk", far[-1])
    for mask in far[:-1][::-1]:
        keep3, send3 = fold(keep3, tie(came3, send2))
        came3 = swap(send3, "blk", mask)
    grad_gain_one = tie(grad_gain_one, send2, send3)
    grad_beta = grad_beta + jnp.sum(passed * middles, axis=0)
    grad_decay = grad_decay + jnp.sum(
        passed * (BEFORE * jnp.exp(-rate * (BEFORE - 1)) * begins + beta * slopes), axis=0
    )
    grad_rate = grad_beta * ssm_all[1] * jnp.exp(-2.0 * rate) / root - decay * grad_decay
    grad_ssm = jnp.stack([grad_rate * rate, grad_beta * root, grad_mix])
    ups, downs = both_sides(side, mine_ff, tie(theirs_ff, grad_tokens))
    chunk_at = upper_core.astype(jnp.int32)
    own_down = jnp.where(upper_core, downs[1], downs[0])
    other_down = jnp.where(upper_core, downs[0], downs[1])
    sent_ff = jnp.concatenate([ups[:, 1], other_down], axis=0)
    came_ff = swap(sent_ff, "blk", 1)
    up_halves = both_sides(chunk_at, ups[:, 0], came_ff[:2])
    down_halves = both_sides(chunk_at, own_down, came_ff[2:])
    columns = lambda v: v.reshape(v.shape[:-2] + (-1, rows, 128)).swapaxes(-3, -2).reshape(v.shape[:-2] + (rows, width))
    sum_up = columns(up_halves).reshape(2, 2, rows, n // 2, span).transpose(2, 3, 1, 0, 4).reshape(rows, FF).astype(f32)
    sum_down = columns(down_halves).reshape(-1, width).astype(f32)
    up_first, up_second, up_new = adamw_step(up_w, up_m, up_v, sum_up, 2.0 * D ** (-0.5), 0.1)
    down_first, down_second, down_new = adamw_step(
        down_w, down_m, down_v, sum_down, 2.0 * FF ** (-0.5), 0.1
    )
    result = middle + ff[0][0] + tie(ff[1][0], grad_tokens) + (backs[1].astype(f32) + backs[3].astype(f32))
    result = result.astype(low_type)
    sum_small = jnp.concatenate([grad_gain_one, grad_gain_two, grad_ssm.reshape(-1, width)], axis=0)
    mask = n // 2
    while mask > 2:
        sum_small = reduce_round(sum_small, mask)
        mask //= 2
    came2, came3 = tie((came2, came3), sum_small)
    for mask in far[:-1][::-1]:
        keep2, send2 = fold(keep2, came2)
        came2 = swap(send2, "blk", mask)
    mine3 = add_low(keep3, came3)
    sum3 = sum_over_win(mine3, 1)[0].astype(f32)
    sum_small = tie(sum_small, send2, mine3)
    for mask in (2, 1):
        sum_small = reduce_round(sum_small, mask)
    came2 = tie(came2, sum_small, up_new, down_new)
    mine2 = sum_over_win(add_low(keep2, came2), 2)[0]
    sum2 = both_sides(side, mine2, swap(mine2, "win", 1)).reshape(-1, width).astype(f32)
    sum_small = tie(sum_small, mine2)
    mask = 1
    while mask < lax.axis_size("win"):
        sum_small = sum_small + swap(sum_small, "win", mask)
        mask *= 2
    sum_gain, sum_ssm = sum_small[:2], sum_small[2:].reshape(ssm_w.shape)

    sum_out = sum2[:rows]
    sum_qkv = jnp.concatenate([sum2[rows:], sum3], axis=0).reshape(3, rows, width)
    qkv_first, qkv_second, qkv_new = adamw_step(
        qkv_w, qkv_m, qkv_v, sum_qkv, 2.0 * D ** (-0.5), 0.1
    )
    out_first, out_second, out_new = adamw_step(out_w, out_m, out_v, sum_out, 1.0, 0.1)
    gain_first, gain_second, gain_new = adamw_step(gain_w, gain_m, gain_v, sum_gain, 1.0, 0.0)
    ssm_first, ssm_second, ssm_new = adamw_step(ssm_w, ssm_m, ssm_v, sum_ssm, 4.0, 0.0)
    return (
        result[None],
        grad_tokens[None],
        grad_carried[None],
        qkv_first,
        qkv_second,
        qkv_new,
        out_first,
        out_second,
        out_new,
        up_first,
        up_second,
        up_new,
        down_first,
        down_second,
        down_new,
        gain_first,
        gain_second,
        gain_new,
        ssm_first,
        ssm_second[1:],
        ssm_second[0],
        ssm_new,
    )


def solution(mesh):
    in_specs = (
        P("win", "blk", None),
        P("win", "blk", None),
        P("win", "blk", None, None),
        P("win", "blk"),
        P(None, "blk", None),
        P(None, "blk", None),
        P(None, "blk", None),
        P("blk", None),
        P("blk", None),
        P("blk", None),
        P("blk", None),
        P("blk", None),
        P("blk", None),
        P("blk", None),
        P("blk", None),
        P("blk", None),
        P(None, "blk"),
        P(None, "blk"),
        P(None, "blk"),
        P(None, None, "blk"),
        P(None, None, "blk"),
        P(None, None, "blk"),
    )
    out_specs = (
        P("win", "blk", None),
        P("win", "blk", None),
        P("win", "blk", None, None),
        P(None, "blk", None),
        P(None, "blk", None),
        P(None, "blk", None),
        P("blk", None),
        P("blk", None),
        P("blk", None),
        P("blk", None),
        P("blk", None),
        P("blk", None),
        P("blk", None),
        P("blk", None),
        P("blk", None),
        P(None, "blk"),
        P(None, "blk"),
        P(None, "blk"),
        P(None, None, "blk"),
        P(None, None, "blk"),
        P(None, "blk"),
        P(None, None, "blk"),
    )
    return jax.shard_map(body, mesh=mesh, in_specs=in_specs, out_specs=out_specs, check_vma=False)
```
